128 devices in a mesh: rows: 16 (over y_hi, x, core), cols: 8 (over z, y_lo).
Axes of the slice: x: 4, y: 4 (y_hi: 2, y_lo: 2; y = y_hi * 2 + y_lo), z: 4, core: 2. Of those that a mesh axis runs over, the one named last changes fastest.
Arguments:
- inputs: bfloat16 [112, 224, 512], P('rows', 'cols'), may hold values from -16 to 16
- cotangent: bfloat16 [112, 224, 512], P('rows', 'cols'), may hold values from -4 to 4
- conv_gain: float32 [512], replicated, may hold values from 0.25 to 1.75
- expand_weight: bfloat16 [512, 2048], replicated, may hold values from -0.25 to 0.25
- depth_weight: float32 [9, 2048], replicated, may hold values from -2 to 2
- project_weight: bfloat16 [2048, 512], replicated, may hold values from -0.125 to 0.125
- block_gain: float32 [512], replicated, may hold values from 0.25 to 1.75
- block_qkv: bfloat16 [512, 1536], replicated, may hold values from -0.25 to 0.25
- block_out: bfloat16 [512, 512], replicated, may hold values from -0.25 to 0.25
- block_bias: float32 [16, 49, 49], replicated, may hold values from -4 to 320
- grid_gain: float32 [512], replicated, may hold values from 0.25 to 1.75
- grid_qkv: bfloat16 [512, 1536], replicated, may hold values from -0.25 to 0.25
- grid_out: bfloat16 [512, 512], replicated, may hold values from -0.25 to 0.25
- grid_bias: float32 [16, 49, 49], replicated, may hold values from -4 to 320
Outputs:
- output: bfloat16 [112, 224, 512], P('rows', 'cols')
- grad_inputs: bfloat16 [112, 224, 512], P('rows', 'cols')
The draws below stay inside these ranges and needn't reach their ends.
All inputs are finite; a program needn't handle non-finite values.
Results may differ from the reference program's by a relative error of at most 0.03.
Values may be sent and summed in bfloat16 or wider, within the bound.
A program may use at most 128 MiB of HBM per device.

```python
import math
import jax
import jax.numpy as jnp
from jax import lax

D = 512
FF = 2048
HEADS = 16
HEAD_DIM = 32
WIN = 7
HEIGHT = 112
BREADTH = 224


def scales(key, dims_shape, lowest, highest):
    spread = jax.random.uniform(key, dims_shape, jnp.float32, 0.0, math.log(highest / lowest))
    return lowest * jnp.exp(spread)


def draw_inputs(key, part):
    key = jax.random.fold_in(key, 3)
    subkeys = jax.random.split(key, 3)
    shape_full = (HEIGHT, BREADTH, D)
    basis = jnp.clip(jax.random.normal(subkeys[0], shape_full, jnp.float32), -2.0, 2.0)
    row_scale = scales(subkeys[1], (HEIGHT, BREADTH, 1), 0.2, 2.0)
    chan_scale = scales(subkeys[2], (1, 1, D), 0.3, 3.0)
    return (basis * row_scale * chan_scale).astype(jnp.bfloat16)


def draw_block_bias(key, part):
    key = jax.random.fold_in(key, 7)
    subkeys = jax.random.split(key, 1)
    table = jnp.clip(jax.random.normal(subkeys[0], (HEADS, WIN * WIN, WIN * WIN), jnp.float32), -4.0, 4.0)
    return table


def draw_grid_bias(key, part):
    key = jax.random.fold_in(key, 9)
    subkeys = jax.random.split(key, 1)
    table = jnp.clip(jax.random.normal(subkeys[0], (HEADS, WIN * WIN, WIN * WIN), jnp.float32), -4.0, 4.0)
    return table


def steps_of(rng, shape, pieces, least, top_value):
    factor_of = 1.0
    for position, shards_of in pieces:
        draws = jax.random.uniform(jax.random.fold_in(jax.random.fold_in(rng, 6), position), (shards_of,), jnp.float32, least / len(pieces), top_value / len(pieces))
        factor_of = factor_of * jnp.repeat(jnp.exp(draws), shape[position] // shards_of).reshape((-1,) + (1,) * (len(shape) - 1 - position))
    return factor_of


def scatter_about(stream_key, dims, scale, bound, pieces=(), kind=jnp.bfloat16):
    values = scale * jax.random.normal(stream_key, dims, jnp.float32)
    if pieces:
        values = values * steps_of(stream_key, dims, pieces, -0.22, 0.18)
    return jnp.clip(values, -bound, bound).astype(kind)


def setup_inputs(seed: int = 0) -> dict:
    key_of = jax.random.split(jax.random.key(seed), 15)
    inputs = draw_inputs(jax.random.fold_in(key_of[14], 71), 0)
    cotangent = scatter_about(key_of[1], (HEIGHT, BREADTH, D), 1.0, 4.0, ((0, 16), (1, 8)))
    conv_gain = jnp.clip(1.0 + 0.15 * jax.random.normal(key_of[2], (D,), jnp.float32), 0.25, 1.75)
    expand_weight = scatter_about(key_of[3], (D, FF), D ** -0.5, 0.25)
    depth_weight = scatter_about(key_of[4], (9, FF), 9 ** -0.5, 2.0, (), jnp.float32)
    project_weight = scatter_about(key_of[5], (FF, D), FF ** -0.5, 0.125)
    block_gain = jnp.clip(1.0 + 0.15 * jax.random.normal(key_of[6], (D,), jnp.float32), 0.25, 1.75)
    block_qkv = scatter_about(key_of[7], (D, 3 * D), D ** -0.5, 0.25)
    block_out = scatter_about(key_of[8], (D, D), D ** -0.5, 0.25)
    block_bias = draw_block_bias(jax.random.fold_in(key_of[14], 71), 0)
    grid_gain = jnp.clip(1.0 + 0.15 * jax.random.normal(key_of[10], (D,), jnp.float32), 0.25, 1.75)
    grid_qkv = scatter_about(key_of[11], (D, 3 * D), D ** -0.5, 0.25)
    grid_out = scatter_about(key_of[12], (D, D), D ** -0.5, 0.25)
    grid_bias = draw_grid_bias(jax.random.fold_in(key_of[14], 71), 0)
    return dict(inputs=inputs, cotangent=cotangent, conv_gain=conv_gain, expand_weight=expand_weight, depth_weight=depth_weight, project_weight=project_weight, block_gain=block_gain, block_qkv=block_qkv, block_out=block_out, block_bias=block_bias, grid_gain=grid_gain, grid_qkv=grid_qkv, grid_out=grid_out, grid_bias=grid_bias)


EPSILON = 1e-05

def layer_norm(values, norm_gain):
    floats = values.astype(jnp.float32)
    center = lax.optimization_barrier(jnp.mean(floats, axis=-1, keepdims=True))
    spread = lax.optimization_barrier(jnp.mean(jnp.square(floats - center), axis=-1, keepdims=True))
    return (floats - center) * lax.rsqrt(spread + EPSILON) * norm_gain

def attend(windows, norm_gain, qkv_weight, out_weight, bias_table):
    window_count, length, channels = windows.shape
    flattened = windows.reshape(window_count * length, channels)
    normed = layer_norm(flattened, norm_gain).astype(jnp.bfloat16)
    packed = jnp.dot(normed, qkv_weight, preferred_element_type=jnp.float32).astype(jnp.bfloat16)
    packed = packed.reshape(window_count, length, 3, HEADS, HEAD_DIM)
    queries = packed[:, :, 0].astype(jnp.float32)
    attn_keys = packed[:, :, 1].astype(jnp.float32)
    value_rows = packed[:, :, 2].astype(jnp.float32)
    scores = jnp.einsum('wqhd,wkhd->whqk', queries, attn_keys) * HEAD_DIM ** (-0.5) + bias_table
    weights = jax.nn.softmax(scores, axis=-1).astype(jnp.bfloat16)
    attended = jnp.einsum('whqk,wkhd->wqhd', weights.astype(jnp.float32), value_rows).astype(jnp.bfloat16)
    attended = attended.reshape(window_count * length, channels)
    summed = flattened.astype(jnp.float32) + jnp.dot(attended, out_weight, preferred_element_type=jnp.float32)
    return summed.astype(jnp.bfloat16).reshape(window_count, length, channels)

def depthwise(padded, depth_weight, height, breadth):
    summed = jnp.zeros((height, breadth, padded.shape[-1]), jnp.float32)
    for row_off in range(3):
        for col_off in range(3):
            summed = summed + padded[row_off:row_off + height, col_off:col_off + breadth] * depth_weight[3 * row_off + col_off]
    return summed

def forward(inputs, conv_gain, expand_weight, depth_weight, project_weight, block_gain, block_qkv, block_out, block_bias, grid_gain, grid_qkv, grid_out, grid_bias):
    height, breadth, channels = inputs.shape
    normed = layer_norm(inputs, conv_gain).astype(jnp.bfloat16)
    hidden = jnp.dot(normed.reshape(height * breadth, channels), expand_weight, preferred_element_type=jnp.float32)
    expanded = jax.nn.gelu(hidden, approximate=False).astype(jnp.bfloat16).reshape(height, breadth, -1)
    padded = jnp.pad(expanded.astype(jnp.float32), ((1, 1), (1, 1), (0, 0)))
    pre_act = depthwise(padded, depth_weight, height, breadth)
    branch = jax.nn.gelu(pre_act, approximate=False).astype(jnp.bfloat16)
    update = jnp.dot(branch.reshape(height * breadth, -1), project_weight, preferred_element_type=jnp.float32)
    mixed_map = (inputs.astype(jnp.float32) + update.reshape(height, breadth, channels)).astype(jnp.bfloat16)
    windows = mixed_map.reshape(height // WIN, WIN, breadth // WIN, WIN, channels).transpose(0, 2, 1, 3, 4)
    blocked = attend(windows.reshape(-1, WIN * WIN, channels), block_gain, block_qkv, block_out, block_bias)
    blocked = blocked.reshape(height // WIN, breadth // WIN, WIN, WIN, channels).transpose(0, 2, 1, 3, 4)
    blocked = blocked.reshape(height, breadth, channels)
    gridded = blocked.reshape(WIN, height // WIN, WIN, breadth // WIN, channels).transpose(1, 3, 0, 2, 4)
    result = attend(gridded.reshape(-1, WIN * WIN, channels), grid_gain, grid_qkv, grid_out, grid_bias)
    result = result.reshape(height // WIN, breadth // WIN, WIN, WIN, channels).transpose(2, 0, 3, 1, 4)
    return result.reshape(height, breadth, channels)

def reference(inputs, cotangent, conv_gain, expand_weight, depth_weight, project_weight, block_gain, block_qkv, block_out, block_bias, grid_gain, grid_qkv, grid_out, grid_bias):

    def apply_block(values):
        return forward(values, conv_gain, expand_weight, depth_weight, project_weight, block_gain, block_qkv, block_out, block_bias, grid_gain, grid_qkv, grid_out, grid_bias)
    result, pullback = jax.vjp(apply_block, inputs)
    gradient = pullback(cotangent)[0]
    return (result, gradient)
```

```python
import functools

import jax
import jax.numpy as jnp
import numpy as np
from jax import lax
from jax.experimental import pallas as pl
from jax.experimental.pallas import tpu as pltpu
from jax.sharding import PartitionSpec as P

ROWS, COLS = 16, 8
HEIGHT, BREADTH = 112, 224
WIN = 7
D = 512
FF = 2048
HEAD_DIM = 32
TR, TC = 7, 28
SW = 32
NWIN, WPAD = 4, 64
LEN = 49
CHUNK = 256
EPSILON = 1e-05
F32, BF16 = jnp.float32, jnp.bfloat16
MESH = pl.DeviceIdType.MESH


def win_row(row, col):
    return WPAD * (col // WIN) + WIN * row + col % WIN


def placements():
    halo = np.zeros((352, 448))
    for rho in range(11):
        for kappa in range(32):
            r, c = rho - 2, kappa - 2
            if 0 <= r < 7:
                if 0 <= c < 28:
                    at = 32 * r + c
                elif c < 0:
                    at = 352 + 2 * r + c + 2
                else:
                    at = 368 + 2 * r + c - 28
            elif r < 0:
                if 0 <= c < 28:
                    at = 224 + 32 * (r + 2) + c
                elif c < 0:
                    at = 384 + 2 * (r + 7) + c + 2
                else:
                    at = 400 + 2 * (r + 7) + c - 28
            else:
                if 0 <= c < 28:
                    at = 288 + 32 * (r - 7) + c
                elif c < 0:
                    at = 416 + 2 * (r - 7) + c + 2
                else:
                    at = 432 + 2 * (r - 7) + c - 28
            halo[32 * rho + kappa, at] = 1
    edge = np.zeros((32, 448))
    for r in range(7):
        for c in range(2):
            edge[2 * r + c, 32 * r + c] = 1
            edge[16 + 2 * r + c, 32 * r + 26 + c] = 1
    to_win = np.zeros((256, 448))
    from_win = np.zeros((208, 448))
    back_win = np.zeros((256, 448))
    for r in range(7):
        for c in range(28):
            to_win[win_row(r, c), 32 * r + c + 2] = 1
            from_win[28 * r + c, win_row(r, c)] = 1
            back_win[win_row(r, c), 28 * r + c] = 1
    edge2 = np.zeros((96, 448))
    for c in range(28):
        edge2[c, win_row(0, c)] = 1
        edge2[32 + c, win_row(6, c)] = 1
    for r in range(7):
        edge2[64 + r, win_row(r, 0)] = 1
        edge2[80 + r, win_row(r, 27)] = 1
    halo2 = np.zeros((288, 448))
    for rho in range(9):
        for kappa in range(1, 31):
            r, c = rho - 1, kappa - 2
            if 0 <= r < 7:
                if 0 <= c < 28:
                    at = win_row(r, c)
                elif c < 0:
                    at = 320 + r
                else:
                    at = 336 + r
            elif r < 0:
                at = 256 + c if 0 <= c < 28 else (352 + 6 if c < 0 else 368 + 6)
            else:
                at = 288 + c if 0 <= c < 28 else (384 if c < 0 else 400)
            halo2[32 * rho + kappa, at] = 1
    parts = dict(
        halo=halo, edge=edge, to_win=to_win, from_win=from_win, back_win=back_win,
        edge2=edge2, halo2=halo2,
    )
    starts, at = {}, 0
    for name, part in parts.items():
        starts[name] = (at, part.shape[0])
        at += part.shape[0]
    return np.concatenate(list(parts.values())), starts


PLACES, STARTS = placements()


def dot(a, b):
    return jnp.dot(a, b, preferred_element_type=F32)


def dot_nt(a, b):
    return lax.dot_general(a, b, (((1,), (1,)), ((), ())), preferred_element_type=F32)


def dot_tn(a, b):
    return lax.dot_general(a, b, (((0,), (0,)), ((), ())), preferred_element_type=F32)


def tail(u):
    d = 1.0 + (0.3275911 * 0.5**0.5) * jnp.abs(u)
    t = pl.reciprocal(d, approx=True)
    t = t * (2.0 - d * t)
    gauss = jnp.exp(-0.5 * (u * u))
    poly = 0.5 * 1.061405429
    for coefficient in (-1.453152027, 1.421413741, -0.284496736, 0.254829592):
        poly = poly * t + 0.5 * coefficient
    return poly * t * gauss, gauss


def gelu_of(u, half):
    return jnp.maximum(u, 0.0) - jnp.abs(u) * half


def slope_of(u, half, gauss):
    return jnp.where(u >= 0.0, 1.0 - half, half) + u * gauss * (0.5 / np.pi) ** 0.5


def standardize(x):
    center = jnp.mean(x, axis=-1, keepdims=True)
    moved = x - center
    spread = jnp.mean(moved * moved, axis=-1, keepdims=True)
    scale = lax.rsqrt(spread + EPSILON)
    return moved * scale, scale


def standardize_back(grad, xhat, scale):
    first = jnp.mean(grad, axis=-1, keepdims=True)
    second = jnp.mean(grad * xhat, axis=-1, keepdims=True)
    return scale * (grad - first - xhat * second)


def by_head(x):
    head = lax.broadcasted_iota(jnp.int32, x.shape, 1) // HEAD_DIM
    zero = jnp.zeros_like(x)
    return jnp.concatenate([jnp.where(head == h, x, zero) for h in range(4)], axis=0)


def own_head(x):
    head = lax.broadcasted_iota(jnp.int32, (WPAD, 128), 1) // HEAD_DIM
    out = x[0:WPAD]
    for h in range(1, 4):
        out = jnp.where(head == h, x[WPAD * h : WPAD * (h + 1)], out)
    return out


def kernel(
    x_ref, cot_ref, cgain_ref, dw_ref, bgain_ref, ggain_ref,
    places_hbm, we_hbm, wp_hbm, bqkv_hbm, bout_hbm, bbias_hbm, gqkv_hbm, gout_hbm, gbias_hbm,
    out_ref, grad_ref,
    places, we, wp, bqkv, bout, bbias, gqkv, gout, gbias, load_sem,
    stage, cat, edges, cat2, edges2, halo_sem, halo2_sem,
    cot_send, cot_recv, fwd_send, fwd_recv, res_send, res_recv, gra_send, gra_recv, grid_sem,
    mixbuf, xhat0, scale0, normed0, slope_u, slope_p, update,
    bias_b, bias_g, zwin, packed_b, xhat_b, scale_b, prob_b, att,
    zgrid, dgrid, packed_g, xhat_g, scale_g, prob_g, dout, da, dpk, gslot,
):
    i, j = lax.axis_index("rows"), lax.axis_index("cols")
    me = i * COLS + j

    def load(index, src, dst):
        return pltpu.make_async_copy(src, dst, load_sem.at[index])

    loads = [
        load(n, src, dst)
        for n, (src, dst) in enumerate(
            [
                (places_hbm, places), (we_hbm, we), (wp_hbm, wp), (bbias_hbm, bbias),
                (gbias_hbm, gbias), (bqkv_hbm, bqkv), (bout_hbm, bout),
                (gout_hbm, gout), (gqkv_hbm, gqkv),
            ]
        )
    ]
    for one in loads:
        one.start()
    l_places, l_we, l_wp, l_bb, l_gb, l_bqkv, l_bout, l_gout, l_gqkv = loads

    barrier = pltpu.get_barrier_semaphore()

    def greet(step, carry):
        other = lax.rem(me + step, ROWS * COLS)
        pl.semaphore_signal(
            barrier, inc=1, device_id=(lax.div(other, COLS), lax.rem(other, COLS)),
            device_id_type=MESH,
        )
        return carry

    lax.fori_loop(1, ROWS * COLS, greet, 0)

    def place(name, source):
        at, size = STARTS[name]
        return dot(places[at : at + size, 0 : source.shape[0]], source)

    stage[...] = jnp.zeros_like(stage)
    for r in range(TR):
        stage[SW * r : SW * r + TC, :] = x_ref[r].astype(F32)
    cat[0:224, :] = stage[0:224, :].astype(BF16)
    l_places.wait()
    edges[...] = place("edge", cat[0:224, :]).astype(BF16)

    mixbuf[...] = jnp.zeros_like(mixbuf)
    for r in range(TR):
        for k in range(4):
            mixbuf[pl.ds(112 * r + k, TC, stride=4), :] = cot_ref[
                r, :, 128 * k : 128 * (k + 1)
            ].astype(F32)
    cot_send[...] = mixbuf[0:784, :].reshape(LEN, 16, 128).astype(BF16)

    pl.semaphore_wait(barrier, ROWS * COLS - 1)

    north, south = lax.rem(i + ROWS - 1, ROWS), lax.rem(i + 1, ROWS)
    west, east = lax.rem(j + COLS - 1, COLS), lax.rem(j + 1, COLS)

    def swap(sems, parts):
        copies = [
            pltpu.make_async_remote_copy(
                src_ref=src, dst_ref=dst, send_sem=sems.at[0, n], recv_sem=sems.at[1, n],
                device_id=to, device_id_type=MESH,
            )
            for n, (src, dst, to) in enumerate(parts)
        ]
        for one in copies:
            one.start()
        return copies

    w_cols, e_cols = edges.at[pl.ds(0, 16)], edges.at[pl.ds(16, 16)]
    halo = swap(
        halo_sem,
        [
            (cat.at[pl.ds(0, 64)], cat.at[pl.ds(288, 64)], (north, j)),
            (cat.at[pl.ds(160, 64)], cat.at[pl.ds(224, 64)], (south, j)),
            (e_cols, cat.at[pl.ds(352, 16)], (i, east)),
            (w_cols, cat.at[pl.ds(368, 16)], (i, west)),
            (e_cols, cat.at[pl.ds(384, 16)], (south, east)),
            (w_cols, cat.at[pl.ds(400, 16)], (south, west)),
            (e_cols, cat.at[pl.ds(416, 16)], (north, east)),
            (w_cols, cat.at[pl.ds(432, 16)], (north, west)),
        ],
    )

    def send_chunks(send, recv, sems, forward):
        def body(c, carry):
            a, b = lax.div(c, WIN), lax.rem(c, WIN)
            if forward:
                row, col = WIN * i + a, WIN * j + b
                ti, tj = lax.rem(row, ROWS), lax.rem(col, COLS)
                slot = lax.div(row, ROWS) * WIN + lax.div(col, COLS)
            else:
                row, col = ROWS * a + i, COLS * b + j
                ti, tj = lax.div(row, WIN), lax.div(col, WIN)
                slot = lax.rem(row, WIN) * WIN + lax.rem(col, WIN)
            mine = jnp.logical_and(ti == i, tj == j)

            @pl.when(mine)
            def _():
                pltpu.make_async_copy(send.at[c], recv.at[slot], sems.at[1]).start()

            @pl.when(jnp.logical_not(mine))
            def _():
                pltpu.make_async_remote_copy(
                    src_ref=send.at[c], dst_ref=recv.at[slot], send_sem=sems.at[0],
                    recv_sem=sems.at[1], device_id=(ti, tj), device_id_type=MESH,
                ).start()

            return carry

        lax.fori_loop(0, LEN, body, 0)

    def wait_chunks(recv, sems):
        pltpu.make_async_copy(recv, recv, sems.at[1]).wait()

    def wait_sent(send, sems):
        some = lax.rem(10 * i, ROWS) < WIN

        @pl.when(some)
        def _():
            part = send.at[pl.ds(0, LEN - 1)]
            pltpu.make_async_copy(part, part, sems.at[0]).wait()

        @pl.when(jnp.logical_not(some))
        def _():
            pltpu.make_async_copy(send, send, sems.at[0]).wait()

    send_chunks(cot_send, cot_recv, grid_sem.at[0], True)

    def flip(bias, bias_t, h):
        square = jnp.concatenate(
            [bias[h], jnp.zeros((LEN, 128 - LEN), F32)], axis=1
        )
        square = jnp.concatenate([square, jnp.zeros((WPAD - LEN, 128), F32)], axis=0)
        turned = square.T[0:WPAD]
        key = lax.broadcasted_iota(jnp.int32, (WPAD, WPAD), 0)
        return jnp.where(key < LEN, turned, -1e30)

    def flip_all(bias, bias_t):
        for g in range(4):
            for h in range(2):
                pair = [flip(bias, bias_t, 4 * g + 2 * h + n) for n in range(2)]
                bias_t[g, :, 128 * h : 128 * (h + 1)] = jnp.concatenate(pair, axis=1)

    l_bb.wait()
    flip_all(bbias, bias_b)
    l_gb.wait()
    flip_all(gbias, bias_g)

    for one in halo:
        one.wait_recv()

    def inside(count, row_shift):
        slot = lax.broadcasted_iota(jnp.int32, (count, 1), 0)
        row = TR * i + lax.shift_right_logical(slot, 5) - row_shift
        col = TC * j + lax.bitwise_and(slot, 31) - 2
        return (row >= 0) & (row < HEIGHT) & (col >= 0) & (col < BREADTH)

    xh = jnp.where(inside(352, 2), place("halo", cat[...]), 0.0)
    xhat, scale = standardize(xh)
    xhat0[...] = xhat[64:288]
    scale0[...] = scale[64:288]
    stage[0:224, :] = xh[64:288]
    normed0[...] = (xhat * cgain_ref[...]).astype(BF16)
    update[...] = jnp.zeros_like(update)
    l_we.wait()
    l_wp.wait()

    def taps(at):
        return [dw_ref[n : n + 1, pl.ds(at, CHUNK)] for n in range(9)]

    def mbconv(step, carry):
        at = pl.multiple_of(step * CHUNK, CHUNK)
        u = dot(normed0[...], we[:, pl.ds(at, CHUNK)])
        half, gauss = tail(u)
        slope_u[:, pl.ds(at, CHUNK)] = slope_of(u, half, gauss)[64:288]
        e = gelu_of(u, half).astype(BF16).astype(F32)
        w = taps(at)
        y = [sum(e[SW * a : SW * a + 288] * w[3 * a + b] for a in range(3)) for b in range(3)]
        pre = pltpu.roll(y[0], 1, 0) + y[1] + pltpu.roll(y[2], 287, 0)
        half, gauss = tail(pre)
        slope_p[:, pl.ds(at, CHUNK)] = slope_of(pre, half, gauss)
        branch = gelu_of(pre[32:256], half[32:256]).astype(BF16)
        update[...] += dot(branch, wp[pl.ds(at, CHUNK), :])
        return carry

    lax.fori_loop(0, FF // CHUNK, mbconv, 0)
    mixed = (stage[0:224, :] + update[...]).astype(BF16)
    zwin[...] = place("to_win", mixed)

    root = HEAD_DIM**-0.5

    def project_in(z, gain_ref, qkv, packed, xhat_ref, scale_ref):
        xhat, scale = standardize(z)
        xhat_ref[...] = xhat
        scale_ref[...] = scale
        normed = (xhat * gain_ref[...]).astype(BF16)
        for n in range(3):
            at = n * 512
            packed[:, at : at + 512] = dot(normed, qkv[:, at : at + 512]).astype(BF16)

    def parts_of(packed, rows, g):
        return [packed[rows, 512 * n + 128 * g : 512 * n + 128 * (g + 1)] for n in range(3)]

    def attend(packed, bias_t, prob):
        def window(w, carry):
            rows = pl.ds(pl.multiple_of(w * WPAD, WPAD), WPAD)
            for g in range(4):
                q, k, v = parts_of(packed, rows, g)
                s = dot_nt(k, by_head(q)) * root + bias_t[g]
                e = jnp.exp(s - jnp.max(s, axis=0, keepdims=True))
                p = e * (1.0 / jnp.sum(e, axis=0, keepdims=True))
                prob[w, g] = p
                att[rows, 128 * g : 128 * (g + 1)] = own_head(dot_tn(p.astype(BF16), v)).astype(
                    BF16
                )
            return carry

        lax.fori_loop(0, NWIN, window, 0)

    def attend_back(packed, prob):
        def window(w, carry):
            rows = pl.ds(pl.multiple_of(w * WPAD, WPAD), WPAD)
            for g in range(4):
                q, k, v = parts_of(packed, rows, g)
                p = prob[w, g]
                dam = by_head(da[rows, 128 * g : 128 * (g + 1)])
                dp = dot_nt(v, dam).astype(BF16).astype(F32)
                ds = p * (dp - jnp.sum(p * dp, axis=0, keepdims=True))
                ds = ds.astype(BF16)
                dq = own_head(dot_tn(ds, k)) * root
                dk = dot(ds, by_head(q)) * root
                dv = dot(p.astype(BF16), dam)
                for n, one in enumerate((dq, dk, dv)):
                    dpk[rows, 512 * n + 128 * g : 512 * n + 128 * (g + 1)] = one.astype(BF16)
            return carry

        lax.fori_loop(0, NWIN, window, 0)

    def project_back(qkv, gain_ref, xhat_ref, scale_ref):
        dn = dot_nt(dpk[...], qkv[...]).astype(BF16).astype(F32)
        dx = standardize_back(dn * gain_ref[...], xhat_ref[...], scale_ref[...])
        return (dout[...].astype(F32) + dx.astype(BF16).astype(F32)).astype(BF16)

    l_bqkv.wait()
    project_in(zwin[...], bgain_ref, bqkv, packed_b, xhat_b, scale_b)
    attend(packed_b, bias_b, prob_b)
    l_bout.wait()
    blocked = (zwin[...] + dot(att[...], bout[...])).astype(BF16)

    spatial = place("from_win", blocked)
    for k in range(4):
        mixbuf[pl.ds(k, 208, stride=4), :] = spatial[:, 128 * k : 128 * (k + 1)]
    fwd_send[...] = mixbuf[0:784, :].reshape(LEN, 16, 128).astype(BF16)
    send_chunks(fwd_send, fwd_recv, grid_sem.at[1], True)

    def to_windows(recv, target):
        mixbuf[0:784, :] = recv[...].astype(F32).reshape(784, 128)
        for w in range(NWIN):
            for k in range(4):
                target[WPAD * w : WPAD * w + LEN, 128 * k : 128 * (k + 1)] = mixbuf[
                    pl.ds(4 * w + k, LEN, stride=16), :
                ]

    def from_windows(source, send):
        for w in range(NWIN):
            for k in range(4):
                mixbuf[pl.ds(4 * w + k, LEN, stride=16), :] = source[
                    WPAD * w : WPAD * w + LEN, 128 * k : 128 * (k + 1)
                ]
        send[...] = mixbuf[0:784, :].reshape(LEN, 16, 128).astype(BF16)

    dgrid[...] = jnp.zeros_like(dgrid)
    zgrid[...] = jnp.zeros_like(zgrid)
    wait_chunks(cot_recv, grid_sem.at[0])
    to_windows(cot_recv, dgrid)
    dout[...] = dgrid[...].astype(BF16)
    l_gout.wait()
    da[...] = dot_nt(dout[...], gout[...]).astype(BF16)
    l_gqkv.wait()

    wait_chunks(fwd_recv, grid_sem.at[1])
    to_windows(fwd_recv, zgrid)
    project_in(zgrid[...], ggain_ref, gqkv, packed_g, xhat_g, scale_g)
    attend(packed_g, bias_g, prob_g)
    attend_back(packed_g, prob_g)
    dgrid[...] = project_back(gqkv, ggain_ref, xhat_g, scale_g).astype(F32)
    from_windows(dgrid, gra_send)
    send_chunks(gra_send, gra_recv, grid_sem.at[3], False)
    zgrid[...] = (zgrid[...] + dot(att[...], gout[...])).astype(BF16).astype(F32)
    from_windows(zgrid, res_send)
    send_chunks(res_send, res_recv, grid_sem.at[2], False)

    wait_chunks(gra_recv, grid_sem.at[3])
    mixbuf[0:784, :] = gra_recv[...].astype(F32).reshape(784, 128)
    mixbuf[784:832, :] = jnp.zeros((48, 128), F32)
    spatial = jnp.concatenate([mixbuf[pl.ds(k, 208, stride=4), :] for k in range(4)], axis=1)
    dout[...] = place("back_win", spatial.astype(BF16)).astype(BF16)
    da[...] = dot_nt(dout[...], bout[...]).astype(BF16)
    attend_back(packed_b, prob_b)
    cat2[0:256, :] = project_back(bqkv, bgain_ref, xhat_b, scale_b)
    edges2[...] = place("edge2", cat2[0:256, :]).astype(BF16)
    w_col2, e_col2 = edges2.at[pl.ds(64, 16)], edges2.at[pl.ds(80, 16)]
    halo2 = swap(
        halo2_sem,
        [
            (edges2.at[pl.ds(0, 32)], cat2.at[pl.ds(288, 32)], (north, j)),
            (edges2.at[pl.ds(32, 32)], cat2.at[pl.ds(256, 32)], (south, j)),
            (e_col2, cat2.at[pl.ds(320, 16)], (i, east)),
            (w_col2, cat2.at[pl.ds(336, 16)], (i, west)),
            (e_col2, cat2.at[pl.ds(352, 16)], (south, east)),
            (w_col2, cat2.at[pl.ds(368, 16)], (south, west)),
            (e_col2, cat2.at[pl.ds(384, 16)], (north, east)),
            (w_col2, cat2.at[pl.ds(400, 16)], (north, west)),
        ],
    )

    wait_chunks(res_recv, grid_sem.at[2])
    mixbuf[0:784, :] = res_recv[...].astype(F32).reshape(784, 128)
    for r in range(TR):
        for k in range(4):
            out_ref[r, :, 128 * k : 128 * (k + 1)] = mixbuf[
                pl.ds(112 * r + k, TC, stride=4), :
            ].astype(BF16)

    for one in halo2:
        one.wait_recv()
    gm = jnp.where(inside(288, 1), place("halo2", cat2[...]), 0.0)
    stage[0:224, :] = gm[32:256]
    gslot[...] = gm.astype(BF16)
    update[...] = jnp.zeros_like(update)

    def mbconv_back(step, carry):
        at = pl.multiple_of(step * CHUNK, CHUNK)
        gp = dot_nt(gslot[...], wp[pl.ds(at, CHUNK), :]).astype(BF16).astype(F32)
        gp = gp * slope_p[:, pl.ds(at, CHUNK)]
        w = taps(at)
        y = [
            sum(gp[SW * (2 - a) : SW * (2 - a) + 224] * w[3 * a + b] for a in range(3))
            for b in range(3)
        ]
        ge = pltpu.roll(y[0], 223, 0) + y[1] + pltpu.roll(y[2], 1, 0)
        gh = ge.astype(BF16).astype(F32) * slope_u[:, pl.ds(at, CHUNK)]
        update[...] += dot_nt(gh.astype(BF16), we[:, pl.ds(at, CHUNK)])
        return carry

    lax.fori_loop(0, FF // CHUNK, mbconv_back, 0)
    dn = update[...].astype(BF16).astype(F32)
    dx = standardize_back(dn * cgain_ref[...], xhat0[...], scale0[...])
    stage[0:224, :] = stage[0:224, :] + dx.astype(BF16).astype(F32)
    for r in range(TR):
        grad_ref[r] = stage[SW * r + 2 : SW * r + 2 + TC, :].astype(BF16)

    for one in halo + halo2:
        one.wait_send()
    for n, send in enumerate((cot_send, fwd_send, res_send, gra_send)):
        wait_sent(send, grid_sem.at[n])


def local(
    inputs, cotangent, conv_gain, expand_weight, depth_weight, project_weight,
    block_gain, block_qkv, block_out, block_bias, grid_gain, grid_qkv, grid_out, grid_bias,
):
    vmem, hbm = pl.BlockSpec(memory_space=pltpu.VMEM), pl.BlockSpec(memory_space=pl.ANY)
    places = jnp.asarray(PLACES, BF16)
    chunks = pltpu.VMEM((LEN, 16, 128), BF16)
    tokens = jax.ShapeDtypeStruct((TR, TC, D), BF16)
    bias = pltpu.VMEM((16, LEN, LEN), F32)
    bias_t = pltpu.VMEM((4, WPAD, 256), F32)
    win_f32, win_bf16 = pltpu.VMEM((256, D), F32), pltpu.VMEM((256, D), BF16)
    packed = pltpu.VMEM((256, 3 * D), BF16)
    scale = pltpu.VMEM((256, 1), F32)
    prob = pltpu.VMEM((NWIN, 4, WPAD, 256), F32)
    scratch = [
        pltpu.VMEM(PLACES.shape, BF16), pltpu.VMEM((D, FF), BF16), pltpu.VMEM((FF, D), BF16),
        pltpu.VMEM((D, 3 * D), BF16), pltpu.VMEM((D, D), BF16), bias,
        pltpu.VMEM((D, 3 * D), BF16), pltpu.VMEM((D, D), BF16), bias,
        pltpu.SemaphoreType.DMA((9,)),
        pltpu.VMEM((224, D), F32), pltpu.VMEM((448, D), BF16), pltpu.VMEM((32, D), BF16),
        pltpu.VMEM((416, D), BF16), pltpu.VMEM((96, D), BF16),
        pltpu.SemaphoreType.DMA((2, 8)), pltpu.SemaphoreType.DMA((2, 8)),
        chunks, chunks, chunks, chunks, chunks, chunks, chunks, chunks,
        pltpu.SemaphoreType.DMA((4, 2)),
        pltpu.VMEM((832, 128), F32), pltpu.VMEM((224, D), F32), pltpu.VMEM((224, 1), F32),
        pltpu.VMEM((352, D), BF16), pltpu.VMEM((224, FF), F32), pltpu.VMEM((288, FF), F32),
        pltpu.VMEM((224, D), F32),
        bias_t, bias_t, win_f32, packed, win_f32, scale, prob, win_bf16,
        win_f32, win_f32, packed, win_f32, scale, prob, win_bf16, win_bf16, packed,
        pltpu.VMEM((288, D), BF16),
    ]
    return pl.pallas_call(
        kernel,
        out_shape=(tokens, tokens),
        in_specs=[vmem] * 6 + [hbm] * 9,
        out_specs=(vmem, vmem),
        scratch_shapes=scratch,
        compiler_params=pltpu.CompilerParams(
            collective_id=0, has_side_effects=True, vmem_limit_bytes=56 * 2**20
        ),
        name="mbconv_attention",
    )(
        inputs, cotangent, conv_gain.reshape(1, D), depth_weight, block_gain.reshape(1, D),
        grid_gain.reshape(1, D), places, expand_weight, project_weight, block_qkv, block_out,
        block_bias, grid_qkv, grid_out, grid_bias,
    )


def solution(mesh):
    tokens = P("rows", "cols", None)
    in_specs = (tokens, tokens) + (P(),) * 12
    return jax.shard_map(
        local, mesh=mesh, in_specs=in_specs, out_specs=(tokens, tokens), check_vma=False
    )
```

```python
import functools

import jax
import jax.numpy as jnp
import numpy as np
from jax import lax
from jax.experimental import pallas as pl
from jax.experimental.pallas import tpu as pltpu
from jax.sharding import PartitionSpec as P

ROWS, COLS = 16, 8
HEIGHT, BREADTH = 112, 224
WIN = 7
D = 512
FF = 2048
HEAD_DIM = 32
TR, TC = 7, 28
SW = 32
NWIN, WPAD = 4, 64
LEN = 49
CHUNK = 1024
EPSILON = 1e-05
F32, BF16 = jnp.float32, jnp.bfloat16
MESH = pl.DeviceIdType.MESH


def win_row(row, col):
    return WPAD * (col // WIN) + WIN * row + col % WIN


def placements():
    halo = np.zeros((352, 448))
    for rho in range(11):
        for kappa in range(32):
            r, c = rho - 2, kappa - 2
            if 0 <= r < 7:
                if 0 <= c < 28:
                    at = 32 * r + c
                elif c < 0:
                    at = 352 + 2 * r + c + 2
                else:
                    at = 368 + 2 * r + c - 28
            elif r < 0:
                if 0 <= c < 28:
                    at = 224 + 32 * (r + 2) + c
                elif c < 0:
                    at = 384 + 2 * (r + 7) + c + 2
                else:
                    at = 400 + 2 * (r + 7) + c - 28
            else:
                if 0 <= c < 28:
                    at = 288 + 32 * (r - 7) + c
                elif c < 0:
                    at = 416 + 2 * (r - 7) + c + 2
                else:
                    at = 432 + 2 * (r - 7) + c - 28
            halo[32 * rho + kappa, at] = 1
    edge = np.zeros((32, 448))
    for r in range(7):
        for c in range(2):
            edge[2 * r + c, 32 * r + c] = 1
            edge[16 + 2 * r + c, 32 * r + 26 + c] = 1
    to_win = np.zeros((256, 448))
    from_win = np.zeros((208, 448))
    back_win = np.zeros((256, 448))
    for r in range(7):
        for c in range(28):
            to_win[win_row(r, c), 32 * r + c + 2] = 1
            from_win[28 * r + c, win_row(r, c)] = 1
            back_win[win_row(r, c), 28 * r + c] = 1
    edge2 = np.zeros((96, 448))
    for c in range(28):
        edge2[c, win_row(0, c)] = 1
        edge2[32 + c, win_row(6, c)] = 1
    for r in range(7):
        edge2[64 + r, win_row(r, 0)] = 1
        edge2[80 + r, win_row(r, 27)] = 1
    halo2 = np.zeros((288, 448))
    for rho in range(9):
        for kappa in range(1, 31):
            r, c = rho - 1, kappa - 2
            if 0 <= r < 7:
                if 0 <= c < 28:
                    at = win_row(r, c)
                elif c < 0:
                    at = 320 + r
                else:
                    at = 336 + r
            elif r < 0:
                at = 256 + c if 0 <= c < 28 else (352 + 6 if c < 0 else 368 + 6)
            else:
                at = 288 + c if 0 <= c < 28 else (384 if c < 0 else 400)
            halo2[32 * rho + kappa, at] = 1
    parts = dict(
        halo=halo, edge=edge, to_win=to_win, from_win=from_win, back_win=back_win,
        edge2=edge2, halo2=halo2,
    )
    starts, at = {}, 0
    for name, part in parts.items():
        starts[name] = (at, part.shape[0])
        at += part.shape[0]
    return np.concatenate(list(parts.values())), starts


PLACES, STARTS = placements()


def dot(a, b):
    return jnp.dot(a, b, preferred_element_type=F32)


def dot_nt(a, b):
    return lax.dot_general(a, b, (((1,), (1,)), ((), ())), preferred_element_type=F32)


def dot_tn(a, b):
    return lax.dot_general(a, b, (((0,), (0,)), ((), ())), preferred_element_type=F32)


def gelu_of(u):
    share = 0.5 + 0.5 * lax.erf(u * 0.5**0.5)
    density = jnp.exp2((-0.5 / np.log(2.0)) * (u * u))
    return u * share, share + (u * (0.5 / np.pi) ** 0.5) * density


def standardize(x):
    center = jnp.mean(x, axis=-1, keepdims=True)
    moved = x - center
    spread = jnp.mean(moved * moved, axis=-1, keepdims=True)
    scale = lax.rsqrt(spread + EPSILON)
    return moved * scale, scale


def standardize_back(grad, xhat, scale):
    first = jnp.mean(grad, axis=-1, keepdims=True)
    second = jnp.mean(grad * xhat, axis=-1, keepdims=True)
    return scale * (grad - first - xhat * second)


def by_head(x):
    head = lax.broadcasted_iota(jnp.int32, x.shape, 1) // HEAD_DIM
    zero = jnp.zeros_like(x)
    return jnp.concatenate([jnp.where(head == h, x, zero) for h in range(4)], axis=0)


def own_head(x):
    head = lax.broadcasted_iota(jnp.int32, (WPAD, 128), 1) // HEAD_DIM
    out = x[0:WPAD]
    for h in range(1, 4):
        out = jnp.where(head == h, x[WPAD * h : WPAD * (h + 1)], out)
    return out


def kernel(
    x_ref, cot_ref, cgain_ref, dw_ref, bgain_ref, ggain_ref,
    places_hbm, we_hbm, wp_hbm, bqkv_hbm, bout_hbm, bbias_hbm, gqkv_hbm, gout_hbm, gbias_hbm,
    out_ref, grad_ref,
    places, we, wp, bqkv, bout, bbias, gqkv, gout, gbias, load_sem,
    stage, cat, edges, cat2, edges2, halo_sem, halo2_sem,
    cot_send, cot_recv, fwd_send, fwd_recv, res_send, res_recv, gra_send, gra_recv, grid_sem,
    mixbuf, xhat0, scale0, normed0, slope_u, slope_p, update,
    bias_b, bias_g, zwin, packed_b, xhat_b, scale_b, prob_b, att,
    zgrid, dgrid, packed_g, xhat_g, scale_g, prob_g, dout, da, dpk, gslot,
):
    i, j = lax.axis_index("rows"), lax.axis_index("cols")
    me = i * COLS + j

    def load(index, src, dst):
        return pltpu.make_async_copy(src, dst, load_sem.at[index])

    loads = [
        load(n, src, dst)
        for n, (src, dst) in enumerate(
            [
                (places_hbm, places), (we_hbm, we), (wp_hbm, wp), (bbias_hbm, bbias),
                (gbias_hbm, gbias), (bqkv_hbm, bqkv), (bout_hbm, bout),
                (gout_hbm, gout), (gqkv_hbm, gqkv),
            ]
        )
    ]
    for one in loads:
        one.start()
    l_places, l_we, l_wp, l_bb, l_gb, l_bqkv, l_bout, l_gout, l_gqkv = loads

    barrier = pltpu.get_barrier_semaphore()

    def greet(step, carry):
        other = lax.rem(me + step, ROWS * COLS)
        pl.semaphore_signal(
            barrier, inc=1, device_id=(lax.div(other, COLS), lax.rem(other, COLS)),
            device_id_type=MESH,
        )
        return carry

    lax.fori_loop(1, ROWS * COLS, greet, 0)

    def place(name, source):
        at, size = STARTS[name]
        return dot(places[at : at + size, 0 : source.shape[0]], source)

    stage[...] = jnp.zeros_like(stage)
    for r in range(TR):
        stage[SW * r : SW * r + TC, :] = x_ref[r].astype(F32)
    cat[0:224, :] = stage[0:224, :].astype(BF16)
    l_places.wait()
    edges[...] = place("edge", cat[0:224, :]).astype(BF16)

    mixbuf[...] = jnp.zeros_like(mixbuf)
    for r in range(TR):
        for k in range(4):
            mixbuf[pl.ds(112 * r + k, TC, stride=4), :] = cot_ref[
                r, :, 128 * k : 128 * (k + 1)
            ].astype(F32)
    cot_send[...] = mixbuf[0:784, :].reshape(LEN, 16, 128).astype(BF16)

    pl.semaphore_wait(barrier, ROWS * COLS - 1)

    north, south = lax.rem(i + ROWS - 1, ROWS), lax.rem(i + 1, ROWS)
    west, east = lax.rem(j + COLS - 1, COLS), lax.rem(j + 1, COLS)

    def swap(sems, parts):
        copies = [
            pltpu.make_async_remote_copy(
                src_ref=src, dst_ref=dst, send_sem=sems.at[0, n], recv_sem=sems.at[1, n],
                device_id=to, device_id_type=MESH,
            )
            for n, (src, dst, to) in enumerate(parts)
        ]
        for one in copies:
            one.start()
        return copies

    w_cols, e_cols = edges.at[pl.ds(0, 16)], edges.at[pl.ds(16, 16)]
    halo = swap(
        halo_sem,
        [
            (cat.at[pl.ds(0, 64)], cat.at[pl.ds(288, 64)], (north, j)),
            (cat.at[pl.ds(160, 64)], cat.at[pl.ds(224, 64)], (south, j)),
            (e_cols, cat.at[pl.ds(352, 16)], (i, east)),
            (w_cols, cat.at[pl.ds(368, 16)], (i, west)),
            (e_cols, cat.at[pl.ds(384, 16)], (south, east)),
            (w_cols, cat.at[pl.ds(400, 16)], (south, west)),
            (e_cols, cat.at[pl.ds(416, 16)], (north, east)),
            (w_cols, cat.at[pl.ds(432, 16)], (north, west)),
        ],
    )

    def send_chunks(send, recv, sems, forward):
        def body(c, carry):
            a, b = lax.div(c, WIN), lax.rem(c, WIN)
            if forward:
                row, col = WIN * i + a, WIN * j + b
                ti, tj = lax.rem(row, ROWS), lax.rem(col, COLS)
                slot = lax.div(row, ROWS) * WIN + lax.div(col, COLS)
            else:
                row, col = ROWS * a + i, COLS * b + j
                ti, tj = lax.div(row, WIN), lax.div(col, WIN)
                slot = lax.rem(row, WIN) * WIN + lax.rem(col, WIN)
            mine = jnp.logical_and(ti == i, tj == j)

            @pl.when(mine)
            def _():
                pltpu.make_async_copy(send.at[c], recv.at[slot], sems.at[1]).start()

            @pl.when(jnp.logical_not(mine))
            def _():
                pltpu.make_async_remote_copy(
                    src_ref=send.at[c], dst_ref=recv.at[slot], send_sem=sems.at[0],
                    recv_sem=sems.at[1], device_id=(ti, tj), device_id_type=MESH,
                ).start()

            return carry

        lax.fori_loop(0, LEN, body, 0)

    def wait_chunks(recv, sems):
        pltpu.make_async_copy(recv, recv, sems.at[1]).wait()

    def wait_sent(send, sems):
        some = lax.rem(10 * i, ROWS) < WIN

        @pl.when(some)
        def _():
            part = send.at[pl.ds(0, LEN - 1)]
            pltpu.make_async_copy(part, part, sems.at[0]).wait()

        @pl.when(jnp.logical_not(some))
        def _():
            pltpu.make_async_copy(send, send, sems.at[0]).wait()

    send_chunks(cot_send, cot_recv, grid_sem.at[0], True)

    def flip(bias, h):
        square = jnp.concatenate(
            [bias[pl.ds(h, LEN, stride=16), :], jnp.zeros((LEN, 128 - LEN), F32)], axis=1
        )
        square = jnp.concatenate([square, jnp.zeros((WPAD - LEN, 128), F32)], axis=0)
        turned = square.T[0:WPAD]
        key = lax.broadcasted_iota(jnp.int32, (WPAD, WPAD), 0)
        return jnp.where(key < LEN, turned, -1e30)

    def flip_all(bias, bias_t):
        for g in range(4):
            for h in range(2):
                pair = [flip(bias, 4 * g + 2 * h + n) for n in range(2)]
                bias_t[g, :, 128 * h : 128 * (h + 1)] = jnp.concatenate(pair, axis=1)

    l_bb.wait()
    flip_all(bbias, bias_b)
    l_gb.wait()
    flip_all(gbias, bias_g)

    for one in halo:
        one.wait_recv()

    def inside(count, row_shift):
        slot = lax.broadcasted_iota(jnp.int32, (count, 1), 0)
        row = TR * i + lax.shift_right_logical(slot, 5) - row_shift
        col = TC * j + lax.bitwise_and(slot, 31) - 2
        return (row >= 0) & (row < HEIGHT) & (col >= 0) & (col < BREADTH)

    xh = jnp.where(inside(352, 2), place("halo", cat[...]), 0.0)
    xhat, scale = standardize(xh)
    xhat0[...] = xhat[64:288]
    scale0[...] = scale[64:288]
    stage[0:224, :] = xh[64:288]
    normed0[...] = (xhat * cgain_ref[...]).astype(BF16)
    update[...] = jnp.zeros_like(update)
    l_we.wait()
    l_wp.wait()

    def taps(at):
        return [dw_ref[n : n + 1, pl.ds(at, CHUNK)] for n in range(9)]

    def mbconv(step, carry):
        at = pl.multiple_of(step * CHUNK, CHUNK)
        u = dot(normed0[...], we[:, pl.ds(at, CHUNK)])
        e, slope = gelu_of(u)
        slope_u[:, pl.ds(at, CHUNK)] = slope[64:288]
        e = e.astype(BF16).astype(F32)
        w = taps(at)
        y = [sum(e[SW * a : SW * a + 288] * w[3 * a + b] for a in range(3)) for b in range(3)]
        pre = pltpu.roll(y[0], 1, 0) + y[1] + pltpu.roll(y[2], 287, 0)
        branch, slope = gelu_of(pre)
        slope_p[:, pl.ds(at, CHUNK)] = slope
        update[...] += dot(branch[32:256].astype(BF16), wp[pl.ds(at, CHUNK), :])
        return carry

    lax.fori_loop(0, FF // CHUNK, mbconv, 0)
    mixed = (stage[0:224, :] + update[...]).astype(BF16)
    zwin[...] = place("to_win", mixed)

    root = HEAD_DIM**-0.5

    def project_in(z, gain_ref, qkv, packed, xhat_ref, scale_ref):
        xhat, scale = standardize(z)
        xhat_ref[...] = xhat
        scale_ref[...] = scale
        normed = (xhat * gain_ref[...]).astype(BF16)
        for n in range(3):
            at = n * 512
            packed[:, at : at + 512] = dot(normed, qkv[:, at : at + 512]).astype(BF16)

    def parts_of(packed, rows, g):
        return [packed[rows, 512 * n + 128 * g : 512 * n + 128 * (g + 1)] for n in range(3)]

    def attend(packed, bias_t, prob):
        def window(w, carry):
            rows = pl.ds(pl.multiple_of(w * WPAD, WPAD), WPAD)
            for g in range(4):
                q, k, v = parts_of(packed, rows, g)
                s = dot_nt(k, by_head(q)) * root + bias_t[g]
                e = jnp.exp(s - jnp.max(s, axis=0, keepdims=True))
                p = e * (1.0 / jnp.sum(e, axis=0, keepdims=True))
                prob[w, g] = p
                att[rows, 128 * g : 128 * (g + 1)] = own_head(dot_tn(p.astype(BF16), v)).astype(
                    BF16
                )
            return carry

        lax.fori_loop(0, NWIN, window, 0, unroll=True)

    def attend_back(packed, prob):
        def window(w, carry):
            rows = pl.ds(pl.multiple_of(w * WPAD, WPAD), WPAD)
            for g in range(4):
                q, k, v = parts_of(packed, rows, g)
                p = prob[w, g]
                dam = by_head(da[rows, 128 * g : 128 * (g + 1)])
                dp = dot_nt(v, dam).astype(BF16).astype(F32)
                ds = p * (dp - jnp.sum(p * dp, axis=0, keepdims=True))
                ds = ds.astype(BF16)
                dq = own_head(dot_tn(ds, k)) * root
                dk = dot(ds, by_head(q)) * root
                dv = dot(p.astype(BF16), dam)
                for n, one in enumerate((dq, dk, dv)):
                    dpk[rows, 512 * n + 128 * g : 512 * n + 128 * (g + 1)] = one.astype(BF16)
            return carry

        lax.fori_loop(0, NWIN, window, 0, unroll=True)

    def project_back(qkv, gain_ref, xhat_ref, scale_ref):
        dn = dot_nt(dpk[...], qkv[...]).astype(BF16).astype(F32)
        dx = standardize_back(dn * gain_ref[...], xhat_ref[...], scale_ref[...])
        return (dout[...].astype(F32) + dx.astype(BF16).astype(F32)).astype(BF16)

    l_bqkv.wait()
    project_in(zwin[...], bgain_ref, bqkv, packed_b, xhat_b, scale_b)
    attend(packed_b, bias_b, prob_b)
    l_bout.wait()
    blocked = (zwin[...] + dot(att[...], bout[...])).astype(BF16)

    spatial = place("from_win", blocked)
    for k in range(4):
        mixbuf[pl.ds(k, 208, stride=4), :] = spatial[:, 128 * k : 128 * (k + 1)]
    fwd_send[...] = mixbuf[0:784, :].reshape(LEN, 16, 128).astype(BF16)
    send_chunks(fwd_send, fwd_recv, grid_sem.at[1], True)

    def to_windows(recv, target):
        mixbuf[0:784, :] = recv[...].astype(F32).reshape(784, 128)
        for w in range(NWIN):
            for k in range(4):
                target[WPAD * w : WPAD * w + LEN, 128 * k : 128 * (k + 1)] = mixbuf[
                    pl.ds(4 * w + k, LEN, stride=16), :
                ]

    def from_windows(source, send):
        for w in range(NWIN):
            for k in range(4):
                mixbuf[pl.ds(4 * w + k, LEN, stride=16), :] = source[
                    WPAD * w : WPAD * w + LEN, 128 * k : 128 * (k + 1)
                ]
        send[...] = mixbuf[0:784, :].reshape(LEN, 16, 128).astype(BF16)

    dgrid[...] = jnp.zeros_like(dgrid)
    zgrid[...] = jnp.zeros_like(zgrid)
    wait_chunks(cot_recv, grid_sem.at[0])
    to_windows(cot_recv, dgrid)
    dout[...] = dgrid[...].astype(BF16)
    l_gout.wait()
    da[...] = dot_nt(dout[...], gout[...]).astype(BF16)
    l_gqkv.wait()

    wait_chunks(fwd_recv, grid_sem.at[1])
    to_windows(fwd_recv, zgrid)
    project_in(zgrid[...], ggain_ref, gqkv, packed_g, xhat_g, scale_g)
    attend(packed_g, bias_g, prob_g)
    attend_back(packed_g, prob_g)
    dgrid[...] = project_back(gqkv, ggain_ref, xhat_g, scale_g).astype(F32)
    from_windows(dgrid, gra_send)
    send_chunks(gra_send, gra_recv, grid_sem.at[3], False)
    zgrid[...] = (zgrid[...] + dot(att[...], gout[...])).astype(BF16).astype(F32)
    from_windows(zgrid, res_send)
    send_chunks(res_send, res_recv, grid_sem.at[2], False)

    wait_chunks(gra_recv, grid_sem.at[3])
    mixbuf[0:784, :] = gra_recv[...].astype(F32).reshape(784, 128)
    mixbuf[784:832, :] = jnp.zeros((48, 128), F32)
    spatial = jnp.concatenate([mixbuf[pl.ds(k, 208, stride=4), :] for k in range(4)], axis=1)
    dout[...] = place("back_win", spatial.astype(BF16)).astype(BF16)
    da[...] = dot_nt(dout[...], bout[...]).astype(BF16)
    attend_back(packed_b, prob_b)
    cat2[0:256, :] = project_back(bqkv, bgain_ref, xhat_b, scale_b)
    edges2[...] = place("edge2", cat2[0:256, :]).astype(BF16)
    w_col2, e_col2 = edges2.at[pl.ds(64, 16)], edges2.at[pl.ds(80, 16)]
    halo2 = swap(
        halo2_sem,
        [
            (edges2.at[pl.ds(0, 32)], cat2.at[pl.ds(288, 32)], (north, j)),
            (edges2.at[pl.ds(32, 32)], cat2.at[pl.ds(256, 32)], (south, j)),
            (e_col2, cat2.at[pl.ds(320, 16)], (i, east)),
            (w_col2, cat2.at[pl.ds(336, 16)], (i, west)),
            (e_col2, cat2.at[pl.ds(352, 16)], (south, east)),
            (w_col2, cat2.at[pl.ds(368, 16)], (south, west)),
            (e_col2, cat2.at[pl.ds(384, 16)], (north, east)),
            (w_col2, cat2.at[pl.ds(400, 16)], (north, west)),
        ],
    )

    wait_chunks(res_recv, grid_sem.at[2])
    mixbuf[0:784, :] = res_recv[...].astype(F32).reshape(784, 128)
    for r in range(TR):
        for k in range(4):
            out_ref[r, :, 128 * k : 128 * (k + 1)] = mixbuf[
                pl.ds(112 * r + k, TC, stride=4), :
            ].astype(BF16)

    for one in halo2:
        one.wait_recv()
    gm = jnp.where(inside(288, 1), place("halo2", cat2[...]), 0.0)
    stage[0:224, :] = gm[32:256]
    gslot[...] = gm.astype(BF16)
    update[...] = jnp.zeros_like(update)

    def mbconv_back(step, carry):
        at = pl.multiple_of(step * CHUNK, CHUNK)
        gp = dot_nt(gslot[...], wp[pl.ds(at, CHUNK), :]).astype(BF16).astype(F32)
        gp = gp * slope_p[:, pl.ds(at, CHUNK)]
        w = taps(at)
        y = [
            sum(gp[SW * (2 - a) : SW * (2 - a) + 224] * w[3 * a + b] for a in range(3))
            for b in range(3)
        ]
        ge = pltpu.roll(y[0], 223, 0) + y[1] + pltpu.roll(y[2], 1, 0)
        gh = ge.astype(BF16).astype(F32) * slope_u[:, pl.ds(at, CHUNK)]
        update[...] += dot_nt(gh.astype(BF16), we[:, pl.ds(at, CHUNK)])
        return carry

    lax.fori_loop(0, FF // CHUNK, mbconv_back, 0)
    dn = update[...].astype(BF16).astype(F32)
    dx = standardize_back(dn * cgain_ref[...], xhat0[...], scale0[...])
    stage[0:224, :] = stage[0:224, :] + dx.astype(BF16).astype(F32)
    for r in range(TR):
        grad_ref[r] = stage[SW * r + 2 : SW * r + 2 + TC, :].astype(BF16)

    for one in halo + halo2:
        one.wait_send()
    for n, send in enumerate((cot_send, fwd_send, res_send, gra_send)):
        wait_sent(send, grid_sem.at[n])


def local(
    inputs, cotangent, conv_gain, expand_weight, depth_weight, project_weight,
    block_gain, block_qkv, block_out, block_bias, grid_gain, grid_qkv, grid_out, grid_bias,
):
    def by_query(bias):
        return bias.transpose(1, 0, 2).reshape(16 * LEN, LEN)

    vmem, hbm = pl.BlockSpec(memory_space=pltpu.VMEM), pl.BlockSpec(memory_space=pl.ANY)
    places = jnp.asarray(PLACES, BF16)
    chunks = pltpu.VMEM((LEN, 16, 128), BF16)
    tokens = jax.ShapeDtypeStruct((TR, TC, D), BF16)
    bias = pltpu.VMEM((16 * LEN, LEN), F32)
    bias_t = pltpu.VMEM((4, WPAD, 256), F32)
    win_f32, win_bf16 = pltpu.VMEM((256, D), F32), pltpu.VMEM((256, D), BF16)
    packed = pltpu.VMEM((256, 3 * D), BF16)
    scale = pltpu.VMEM((256, 1), F32)
    prob = pltpu.VMEM((NWIN, 4, WPAD, 256), F32)
    scratch = [
        pltpu.VMEM(PLACES.shape, BF16), pltpu.VMEM((D, FF), BF16), pltpu.VMEM((FF, D), BF16),
        pltpu.VMEM((D, 3 * D), BF16), pltpu.VMEM((D, D), BF16), bias,
        pltpu.VMEM((D, 3 * D), BF16), pltpu.VMEM((D, D), BF16), bias,
        pltpu.SemaphoreType.DMA((9,)),
        pltpu.VMEM((224, D), F32), pltpu.VMEM((448, D), BF16), pltpu.VMEM((32, D), BF16),
        pltpu.VMEM((416, D), BF16), pltpu.VMEM((96, D), BF16),
        pltpu.SemaphoreType.DMA((2, 8)), pltpu.SemaphoreType.DMA((2, 8)),
        chunks, chunks, chunks, chunks, chunks, chunks, chunks, chunks,
        pltpu.SemaphoreType.DMA((4, 2)),
        pltpu.VMEM((832, 128), F32), pltpu.VMEM((224, D), F32), pltpu.VMEM((224, 1), F32),
        pltpu.VMEM((352, D), BF16), pltpu.VMEM((224, FF), F32), pltpu.VMEM((288, FF), F32),
        pltpu.VMEM((224, D), F32),
        bias_t, bias_t, win_f32, packed, win_f32, scale, prob, win_bf16,
        win_f32, win_f32, packed, win_f32, scale, prob, win_bf16, win_bf16, packed,
        pltpu.VMEM((288, D), BF16),
    ]
    return pl.pallas_call(
        kernel,
        out_shape=(tokens, tokens),
        in_specs=[vmem] * 6 + [hbm] * 9,
        out_specs=(vmem, vmem),
        scratch_shapes=scratch,
        compiler_params=pltpu.CompilerParams(
            collective_id=0, has_side_effects=True, vmem_limit_bytes=56 * 2**20
        ),
        name="mbconv_attention",
    )(
        inputs, cotangent, conv_gain.reshape(1, D), depth_weight, block_gain.reshape(1, D),
        grid_gain.reshape(1, D), places, expand_weight, project_weight, block_qkv, block_out,
        by_query(block_bias), grid_qkv, grid_out, by_query(grid_bias),
    )


def solution(mesh):
    tokens = P("rows", "cols", None)
    in_specs = (tokens, tokens) + (P(),) * 12
    return jax.shard_map(
        local, mesh=mesh, in_specs=in_specs, out_specs=(tokens, tokens), check_vma=False
    )
```

```python
import functools

import jax
import jax.numpy as jnp
import numpy as np
from jax import lax
from jax.experimental import pallas as pl
from jax.experimental.pallas import tpu as pltpu
from jax.sharding import PartitionSpec as P

ROWS, COLS = 16, 8
HEIGHT, BREADTH = 112, 224
WIN = 7
D = 512
FF = 2048
HEAD_DIM = 32
TR, TC = 7, 28
SW = 32
NWIN, WPAD = 4, 64
LEN = 49
CHUNK = 1024
TILES = CHUNK // 128
EPSILON = 1e-05
F32, BF16 = jnp.float32, jnp.bfloat16
MESH = pl.DeviceIdType.MESH


def win_row(row, col):
    return WPAD * (col // WIN) + WIN * row + col % WIN


def placements():
    edge = np.zeros((32, 256))
    slots = np.zeros((256, 256))
    to_win = np.zeros((256, 256))
    from_win = np.zeros((208, 256))
    back_win = np.zeros((256, 256))
    for r in range(TR):
        for c in range(2):
            edge[2 * r + c, SW * r + c + 2] = 1
            edge[16 + 2 * r + c, SW * r + c + 28] = 1
        for c in range(TC):
            to_win[win_row(r, c), SW * r + c + 2] = 1
            slots[SW * r + c + 2, win_row(r, c)] = 1
            from_win[TC * r + c, win_row(r, c)] = 1
            back_win[win_row(r, c), TC * r + c] = 1
        slots[224 + r, win_row(r, 0)] = 1
        slots[240 + r, win_row(r, 27)] = 1
    halo = np.zeros((192, 256))
    for line in range(2):
        for c in range(TC):
            for half in range(2):
                at = 64 * half + SW * line + c + 2
                halo[at, at] = 1
        for c in range(2):
            for half in range(2):
                for side in range(2):
                    at = 64 * half + SW * line + (30 * side + c)
                    row = line + (0 if half else 5)
                    halo[at, 128 + 16 * (2 + 2 * half + side) + 2 * row + c] = 1
    for r in range(TR):
        for c in range(2):
            for side in range(2):
                halo[128 + 16 * (2 * side + c) + r + 2, 128 + 16 * side + 2 * r + c] = 1
    halo2 = np.zeros((96, 256))
    for half in range(2):
        for c in range(TC):
            halo2[32 * half + c + 2, 32 * half + c + 2] = 1
        for side in range(2):
            row = 0 if half else 6
            halo2[32 * half + 1 + 29 * side, 64 + 16 * (2 + 2 * half + side) + row] = 1
    for r in range(TR):
        for side in range(2):
            halo2[64 + 16 * side + r, 64 + 16 * side + r] = 1
    parts = dict(
        edge=edge, halo=halo, to_win=to_win, from_win=from_win, back_win=back_win,
        slots=slots, halo2=halo2,
    )
    starts, at = {}, 0
    for name, part in parts.items():
        starts[name] = (at, part.shape[0])
        at += part.shape[0]
    return np.concatenate(list(parts.values())), starts


PLACES, STARTS = placements()


def dot(a, b):
    return jnp.dot(a, b, preferred_element_type=F32)


def dot_nt(a, b):
    return lax.dot_general(a, b, (((1,), (1,)), ((), ())), preferred_element_type=F32)


def dot_tn(a, b):
    return lax.dot_general(a, b, (((0,), (0,)), ((), ())), preferred_element_type=F32)


def gelu_of(u):
    share = 0.5 + 0.5 * lax.erf(u * 0.5**0.5)
    density = jnp.exp2((-0.5 / np.log(2.0)) * (u * u))
    return u * share, share + (u * (0.5 / np.pi) ** 0.5) * density


def standardize(x):
    center = jnp.mean(x, axis=-1, keepdims=True)
    moved = x - center
    spread = jnp.mean(moved * moved, axis=-1, keepdims=True)
    scale = lax.rsqrt(spread + EPSILON)
    return moved * scale, scale


def standardize_back(grad, xhat, scale):
    first = jnp.mean(grad, axis=-1, keepdims=True)
    second = jnp.mean(grad * xhat, axis=-1, keepdims=True)
    return scale * (grad - first - xhat * second)


def by_head(x):
    head = lax.broadcasted_iota(jnp.int32, x.shape, 1) // HEAD_DIM
    zero = jnp.zeros_like(x)
    return jnp.concatenate([jnp.where(head == h, x, zero) for h in range(4)], axis=0)


def own_head(x):
    head = lax.broadcasted_iota(jnp.int32, (WPAD, 128), 1) // HEAD_DIM
    out = x[0:WPAD]
    for h in range(1, 4):
        out = jnp.where(head == h, x[WPAD * h : WPAD * (h + 1)], out)
    return out


def kernel(
    x_ref, cot_ref, cgain_ref, dw_ref, bgain_ref, ggain_ref,
    places_hbm, we_hbm, wp_hbm, bqkv_hbm, bout_hbm, bbias_hbm, gqkv_hbm, gout_hbm, gbias_hbm,
    out_ref, grad_ref,
    places, we, wp, bqkv, bout, bbias, gqkv, gout, gbias, load_sem,
    stage, own, cat, edges, own2, cat2, halo_sem, halo2_sem,
    cot_send, cot_recv, fwd_send, fwd_recv, res_send, res_recv, gra_send, gra_recv, grid_sem,
    mixbuf, xhat0, scale0, normed0, normed1, slope_u, slope_p, pre_act, update,
    bias_b, bias_g, zwin, packed_b, xhat_b, scale_b, prob_b, att,
    zgrid, dgrid, packed_g, xhat_g, scale_g, prob_g, dout, da, dpk, halo_grad, grad_e,
):
    i, j = lax.axis_index("rows"), lax.axis_index("cols")
    me = i * COLS + j

    def load(index, src, dst):
        return pltpu.make_async_copy(src, dst, load_sem.at[index])

    loads = [
        load(n, src, dst)
        for n, (src, dst) in enumerate(
            [
                (places_hbm, places), (we_hbm, we), (wp_hbm, wp), (bbias_hbm, bbias),
                (gbias_hbm, gbias), (bqkv_hbm, bqkv), (bout_hbm, bout),
                (gout_hbm, gout), (gqkv_hbm, gqkv),
            ]
        )
    ]
    for one in loads:
        one.start()
    l_places, l_we, l_wp, l_bb, l_gb, l_bqkv, l_bout, l_gout, l_gqkv = loads

    barrier = pltpu.get_barrier_semaphore()

    def greet(step, carry):
        other = lax.rem(me + step, ROWS * COLS)
        pl.semaphore_signal(
            barrier, inc=1, device_id=(lax.div(other, COLS), lax.rem(other, COLS)),
            device_id_type=MESH,
        )
        return carry

    lax.fori_loop(1, ROWS * COLS, greet, 0)

    def place(name, source):
        at, size = STARTS[name]
        return dot(places[at : at + size, 0 : source.shape[0]], source)

    stage[...] = jnp.zeros_like(stage)
    for r in range(TR):
        stage[SW * r + 2 : SW * r + 2 + TC, :] = x_ref[r].astype(F32)
    own[...] = stage[...].astype(BF16)
    l_places.wait()
    edges[...] = place("edge", own[...]).astype(BF16)

    mixbuf[...] = jnp.zeros_like(mixbuf)
    for r in range(TR):
        for k in range(4):
            mixbuf[pl.ds(112 * r + k, TC, stride=4), :] = cot_ref[
                r, :, 128 * k : 128 * (k + 1)
            ].astype(F32)
    cot_send[...] = mixbuf[0:784, :].reshape(LEN, 16, 128).astype(BF16)

    def flip(bias, h):
        square = jnp.concatenate(
            [bias[pl.ds(h, LEN, stride=16), :], jnp.zeros((LEN, 128 - LEN), F32)], axis=1
        )
        square = jnp.concatenate([square, jnp.zeros((WPAD - LEN, 128), F32)], axis=0)
        turned = square.T[0:WPAD]
        key = lax.broadcasted_iota(jnp.int32, (WPAD, WPAD), 0)
        return jnp.where(key < LEN, turned, -1e30)

    def flip_all(bias, bias_t):
        for g in range(4):
            for h in range(2):
                pair = [flip(bias, 4 * g + 2 * h + n) for n in range(2)]
                bias_t[g, :, 128 * h : 128 * (h + 1)] = jnp.concatenate(pair, axis=1)

    l_bb.wait()
    flip_all(bbias, bias_b)
    l_gb.wait()
    flip_all(gbias, bias_g)

    xhat, scale = standardize(stage[...])
    xhat0[...] = xhat
    scale0[...] = scale
    normed0[...] = (xhat * cgain_ref[...]).astype(BF16)
    l_we.wait()

    def taps(at):
        return [dw_ref[n : n + 1, pl.ds(at, CHUNK)] for n in range(9)]

    def wide(ref, step, rows=slice(None)):
        return jnp.concatenate([ref[step * TILES + n, rows, :] for n in range(TILES)], axis=1)

    def put_wide(ref, step, rows, value):
        for n in range(TILES):
            ref[step * TILES + n, rows, :] = value[:, 128 * n : 128 * (n + 1)]

    def add_wide(ref, step, first, value):
        rows = slice(first, first + value.shape[0])
        put_wide(ref, step, rows, wide(ref, step, rows) + value)

    def lines(x, first, last):
        return x[SW * first : SW * last]

    def side_by_side(y):
        count = y[0].shape[0]
        return pltpu.roll(y[0], 1, 0) + y[1] + pltpu.roll(y[2], count - 1, 0)

    def expand_own(step, carry):
        at = pl.multiple_of(step * CHUNK, CHUNK)
        e, slope = gelu_of(dot(normed0[...], we[:, pl.ds(at, CHUNK)]))
        slope_u[:, pl.ds(at, CHUNK)] = slope
        e = e.astype(BF16).astype(F32)
        w = taps(at)
        y = []
        for b in range(3):
            t = [e * w[3 * a + b] for a in range(3)]
            y.append(
                jnp.concatenate(
                    [
                        lines(t[2], 0, 1),
                        lines(t[1], 0, 1) + lines(t[2], 1, 2),
                        lines(t[0], 0, 5) + lines(t[1], 1, 6) + lines(t[2], 2, 7),
                        lines(t[0], 5, 6) + lines(t[1], 6, 7),
                        lines(t[0], 6, 7),
                    ],
                    axis=0,
                )
            )
        put_wide(pre_act, step, slice(None), side_by_side(y))
        return carry

    lax.fori_loop(0, 1, expand_own, 0)
    pl.semaphore_wait(barrier, ROWS * COLS - 1)

    north, south = lax.rem(i + ROWS - 1, ROWS), lax.rem(i + 1, ROWS)
    west, east = lax.rem(j + COLS - 1, COLS), lax.rem(j + 1, COLS)

    def swap(sems, parts):
        copies = [
            pltpu.make_async_remote_copy(
                src_ref=src, dst_ref=dst, send_sem=sems.at[0, n], recv_sem=sems.at[1, n],
                device_id=to, device_id_type=MESH,
            )
            for n, (src, dst, to) in enumerate(parts)
        ]
        for one in copies:
            one.start()
        return copies

    w_cols, e_cols = edges.at[pl.ds(0, 16)], edges.at[pl.ds(16, 16)]
    halo = swap(
        halo_sem,
        [
            (own.at[pl.ds(0, 64)], cat.at[pl.ds(64, 64)], (north, j)),
            (own.at[pl.ds(160, 64)], cat.at[pl.ds(0, 64)], (south, j)),
            (e_cols, cat.at[pl.ds(128, 16)], (i, east)),
            (w_cols, cat.at[pl.ds(144, 16)], (i, west)),
            (e_cols, cat.at[pl.ds(160, 16)], (south, east)),
            (w_cols, cat.at[pl.ds(176, 16)], (south, west)),
            (e_cols, cat.at[pl.ds(192, 16)], (north, east)),
            (w_cols, cat.at[pl.ds(208, 16)], (north, west)),
        ],
    )

    def send_chunks(send, recv, sems, forward):
        def body(c, carry):
            a, b = lax.div(c, WIN), lax.rem(c, WIN)
            if forward:
                row, col = WIN * i + a, WIN * j + b
                ti, tj = lax.rem(row, ROWS), lax.rem(col, COLS)
                slot = lax.div(row, ROWS) * WIN + lax.div(col, COLS)
            else:
                row, col = ROWS * a + i, COLS * b + j
                ti, tj = lax.div(row, WIN), lax.div(col, WIN)
                slot = lax.rem(row, WIN) * WIN + lax.rem(col, WIN)
            mine = jnp.logical_and(ti == i, tj == j)

            @pl.when(mine)
            def _():
                pltpu.make_async_copy(send.at[c], recv.at[slot], sems.at[1]).start()

            @pl.when(jnp.logical_not(mine))
            def _():
                pltpu.make_async_remote_copy(
                    src_ref=send.at[c], dst_ref=recv.at[slot], send_sem=sems.at[0],
                    recv_sem=sems.at[1], device_id=(ti, tj), device_id_type=MESH,
                ).start()

            return carry

        lax.fori_loop(0, LEN, body, 0)

    def wait_chunks(recv, sems):
        pltpu.make_async_copy(recv, recv, sems.at[1]).wait()

    def wait_sent(send, sems):
        some = lax.rem(10 * i, ROWS) < WIN

        @pl.when(some)
        def _():
            part = send.at[pl.ds(0, LEN - 1)]
            pltpu.make_async_copy(part, part, sems.at[0]).wait()

        @pl.when(jnp.logical_not(some))
        def _():
            pltpu.make_async_copy(send, send, sems.at[0]).wait()

    send_chunks(cot_send, cot_recv, grid_sem.at[0], True)

    lax.fori_loop(1, FF // CHUNK, expand_own, 0)

    for one in halo:
        one.wait_recv()
    has_n, has_s, has_w, has_e = (
        jnp.where(there, 1.0, 0.0) for there in (i > 0, i < ROWS - 1, j > 0, j < COLS - 1)
    )

    def inside(count, strip, column):
        at = lax.broadcasted_iota(jnp.int32, (count, 1), 0)
        slot = lax.bitwise_and(at, SW - 1)
        keep = jnp.where(slot < 2, has_w, 1.0) * jnp.where(slot < 30, 1.0, has_e)
        strips = jnp.where(at < strip, has_n, has_s) * keep
        columns = jnp.where(at < 2 * strip + column, has_w, has_e)
        return jnp.where(at < 2 * strip, strips, columns)

    xh = place("halo", cat[...]) * inside(192, 64, 32)
    normed1[...] = (standardize(xh)[0] * cgain_ref[...]).astype(BF16)
    update[...] = jnp.zeros_like(update)
    l_wp.wait()

    def add_column(ref, slot, count, step, value):
        rows = pl.ds(slot, count, stride=SW)
        put_wide(ref, step, rows, wide(ref, step, rows) + value[0:count])

    def mbconv(step, carry):
        at = pl.multiple_of(step * CHUNK, CHUNK)
        here = pl.ds(at, CHUNK)
        e, _ = gelu_of(dot(normed1[...], we[:, here]))
        e = e.astype(BF16).astype(F32)
        w = taps(at)
        n0, n1, s0, s1 = (lines(e, n, n + 1) for n in range(4))
        w0, w1, e0, e1 = (e[128 + 16 * n : 144 + 16 * n] for n in range(4))
        around = [
            (0, [n0 * w[b] + n1 * w[3 + b] for b in range(3)]),
            (32, [n1 * w[b] for b in range(3)]),
            (224, [s0 * w[6 + b] for b in range(3)]),
            (256, [s0 * w[3 + b] + s1 * w[6 + b] for b in range(3)]),
        ]
        for first, y in around:
            add_wide(pre_act, step, first, side_by_side(y))

        def down(terms):
            return terms[0] + pltpu.roll(terms[1], 15, 0) + pltpu.roll(terms[2], 14, 0)

        sides = [
            (1, [w0 * w[3 * a] + w1 * w[3 * a + 1] for a in range(3)]),
            (2, [w1 * w[3 * a] for a in range(3)]),
            (29, [e0 * w[3 * a + 2] for a in range(3)]),
            (30, [e0 * w[3 * a + 1] + e1 * w[3 * a + 2] for a in range(3)]),
        ]
        for slot, terms in sides:
            add_column(pre_act, slot, 9, step, down(terms))
        branch, slope = gelu_of(wide(pre_act, step))
        put_wide(slope_p, step, slice(None), slope)
        update[...] += dot(branch[32:256].astype(BF16), wp[here, :])
        return carry

    lax.fori_loop(0, FF // CHUNK, mbconv, 0)
    mixed = (stage[...] + update[...]).astype(BF16)
    zwin[...] = place("to_win", mixed)

    root = HEAD_DIM**-0.5

    def project_in(z, gain_ref, qkv, packed, xhat_ref, scale_ref):
        xhat, scale = standardize(z)
        xhat_ref[...] = xhat
        scale_ref[...] = scale
        normed = (xhat * gain_ref[...]).astype(BF16)
        for n in range(3):
            at = n * 512
            packed[:, at : at + 512] = dot(normed, qkv[:, at : at + 512]).astype(BF16)

    def parts_of(packed, rows, g):
        return [packed[rows, 512 * n + 128 * g : 512 * n + 128 * (g + 1)] for n in range(3)]

    def attend(packed, bias_t, prob):
        def window(w, carry):
            rows = pl.ds(pl.multiple_of(w * WPAD, WPAD), WPAD)
            for g in range(4):
                q, k, v = parts_of(packed, rows, g)
                s = dot_nt(k, by_head(q)) * root + bias_t[g]
                e = jnp.exp(s - jnp.max(s, axis=0, keepdims=True))
                p = e * (1.0 / jnp.sum(e, axis=0, keepdims=True))
                prob[w, g] = p
                att[rows, 128 * g : 128 * (g + 1)] = own_head(dot_tn(p.astype(BF16), v)).astype(
                    BF16
                )
            return carry

        lax.fori_loop(0, NWIN, window, 0, unroll=True)

    def attend_back(packed, prob):
        def window(w, carry):
            rows = pl.ds(pl.multiple_of(w * WPAD, WPAD), WPAD)
            for g in range(4):
                q, k, v = parts_of(packed, rows, g)
                p = prob[w, g]
                dam = by_head(da[rows, 128 * g : 128 * (g + 1)])
                dp = dot_nt(v, dam).astype(BF16).astype(F32)
                ds = p * (dp - jnp.sum(p * dp, axis=0, keepdims=True))
                ds = ds.astype(BF16)
                dq = own_head(dot_tn(ds, k)) * root
                dk = dot(ds, by_head(q)) * root
                dv = dot(p.astype(BF16), dam)
                for n, one in enumerate((dq, dk, dv)):
                    dpk[rows, 512 * n + 128 * g : 512 * n + 128 * (g + 1)] = one.astype(BF16)
            return carry

        lax.fori_loop(0, NWIN, window, 0, unroll=True)

    def project_back(qkv, gain_ref, xhat_ref, scale_ref):
        dn = dot_nt(dpk[...], qkv[...]).astype(BF16).astype(F32)
        dx = standardize_back(dn * gain_ref[...], xhat_ref[...], scale_ref[...])
        return (dout[...].astype(F32) + dx.astype(BF16).astype(F32)).astype(BF16)

    l_bqkv.wait()
    project_in(zwin[...], bgain_ref, bqkv, packed_b, xhat_b, scale_b)
    attend(packed_b, bias_b, prob_b)
    l_bout.wait()
    blocked = (zwin[...] + dot(att[...], bout[...])).astype(BF16)

    spatial = place("from_win", blocked)
    for k in range(4):
        mixbuf[pl.ds(k, 208, stride=4), :] = spatial[:, 128 * k : 128 * (k + 1)]
    fwd_send[...] = mixbuf[0:784, :].reshape(LEN, 16, 128).astype(BF16)
    send_chunks(fwd_send, fwd_recv, grid_sem.at[1], True)

    def to_windows(recv, target):
        mixbuf[0:784, :] = recv[...].astype(F32).reshape(784, 128)
        for w in range(NWIN):
            for k in range(4):
                target[WPAD * w : WPAD * w + LEN, 128 * k : 128 * (k + 1)] = mixbuf[
                    pl.ds(4 * w + k, LEN, stride=16), :
                ]

    def from_windows(source, send):
        for w in range(NWIN):
            for k in range(4):
                mixbuf[pl.ds(4 * w + k, LEN, stride=16), :] = source[
                    WPAD * w : WPAD * w + LEN, 128 * k : 128 * (k + 1)
                ]
        send[...] = mixbuf[0:784, :].reshape(LEN, 16, 128).astype(BF16)

    dgrid[...] = jnp.zeros_like(dgrid)
    zgrid[...] = jnp.zeros_like(zgrid)
    wait_chunks(cot_recv, grid_sem.at[0])
    to_windows(cot_recv, dgrid)
    dout[...] = dgrid[...].astype(BF16)
    l_gout.wait()
    da[...] = dot_nt(dout[...], gout[...]).astype(BF16)
    l_gqkv.wait()

    wait_chunks(fwd_recv, grid_sem.at[1])
    to_windows(fwd_recv, zgrid)
    project_in(zgrid[...], ggain_ref, gqkv, packed_g, xhat_g, scale_g)
    attend(packed_g, bias_g, prob_g)
    attend_back(packed_g, prob_g)
    dgrid[...] = project_back(gqkv, ggain_ref, xhat_g, scale_g).astype(F32)
    from_windows(dgrid, gra_send)
    send_chunks(gra_send, gra_recv, grid_sem.at[3], False)
    zgrid[...] = (zgrid[...] + dot(att[...], gout[...])).astype(BF16).astype(F32)
    from_windows(zgrid, res_send)
    send_chunks(res_send, res_recv, grid_sem.at[2], False)

    wait_chunks(gra_recv, grid_sem.at[3])
    mixbuf[0:784, :] = gra_recv[...].astype(F32).reshape(784, 128)
    mixbuf[784:832, :] = jnp.zeros((48, 128), F32)
    spatial = jnp.concatenate([mixbuf[pl.ds(k, 208, stride=4), :] for k in range(4)], axis=1)
    dout[...] = place("back_win", spatial.astype(BF16)).astype(BF16)
    da[...] = dot_nt(dout[...], bout[...]).astype(BF16)
    attend_back(packed_b, prob_b)
    slotted = place("slots", project_back(bqkv, bgain_ref, xhat_b, scale_b))
    stage[...] = slotted[0:224]
    own2[...] = slotted.astype(BF16)
    w_col2, e_col2 = own2.at[pl.ds(224, 16)], own2.at[pl.ds(240, 16)]
    halo2 = swap(
        halo2_sem,
        [
            (own2.at[pl.ds(0, 32)], cat2.at[pl.ds(32, 32)], (north, j)),
            (own2.at[pl.ds(192, 32)], cat2.at[pl.ds(0, 32)], (south, j)),
            (e_col2, cat2.at[pl.ds(64, 16)], (i, east)),
            (w_col2, cat2.at[pl.ds(80, 16)], (i, west)),
            (e_col2, cat2.at[pl.ds(96, 16)], (south, east)),
            (w_col2, cat2.at[pl.ds(112, 16)], (south, west)),
            (e_col2, cat2.at[pl.ds(128, 16)], (north, east)),
            (w_col2, cat2.at[pl.ds(144, 16)], (north, west)),
        ],
    )

    def back_own(step, carry):
        here = pl.ds(pl.multiple_of(step * CHUNK, CHUNK), CHUNK)
        gp = dot_nt(own2[0:224, :], wp[here, :]).astype(BF16).astype(F32)
        gp = gp * wide(slope_p, step, slice(32, 256))
        w = taps(pl.multiple_of(step * CHUNK, CHUNK))
        y = []
        for b in range(3):
            t = [gp * w[3 * a + 2 - b] for a in range(3)]
            y.append(
                jnp.concatenate(
                    [
                        lines(t[0], 1, 2) + lines(t[1], 0, 1),
                        lines(t[0], 2, 7) + lines(t[1], 1, 6) + lines(t[2], 0, 5),
                        lines(t[1], 6, 7) + lines(t[2], 5, 6),
                    ],
                    axis=0,
                )
            )
        put_wide(grad_e, step, slice(None), side_by_side(y))
        return carry

    lax.fori_loop(0, FF // CHUNK, back_own, 0)
    update[...] = jnp.zeros_like(update)
    wait_chunks(res_recv, grid_sem.at[2])
    out_ref[...] = res_recv[...]

    for one in halo2:
        one.wait_recv()
    gm = place("halo2", cat2[...]) * inside(96, 32, 16)
    halo_grad[...] = gm.astype(BF16)

    def mbconv_back(step, carry):
        at = pl.multiple_of(step * CHUNK, CHUNK)
        here = pl.ds(at, CHUNK)
        gp = dot_nt(halo_grad[...], wp[here, :]).astype(BF16).astype(F32)
        w = taps(at)

        north_gp = gp[0:32] * wide(slope_p, step, slice(0, 32))
        south_gp = gp[32:64] * wide(slope_p, step, slice(256, 288))
        west_gp = gp[64:72] * wide(slope_p, step, pl.ds(SW + 1, 8, stride=SW))
        east_gp = gp[80:88] * wide(slope_p, step, pl.ds(SW + 30, 8, stride=SW))
        add_wide(grad_e, step, 0, side_by_side([north_gp * w[8 - b] for b in range(3)]))
        add_wide(grad_e, step, 192, side_by_side([south_gp * w[2 - b] for b in range(3)]))

        def down(x, b):
            return (
                pltpu.roll(x * w[b], 7, 0) + x * w[3 + b] + pltpu.roll(x * w[6 + b], 1, 0)
            )

        add_column(grad_e, 2, 7, step, down(west_gp, 2))
        add_column(grad_e, 29, 7, step, down(east_gp, 0))
        gh = wide(grad_e, step).astype(BF16).astype(F32) * slope_u[:, here]
        update[...] += dot_nt(gh.astype(BF16), we[:, here])
        return carry

    lax.fori_loop(0, FF // CHUNK, mbconv_back, 0)
    dn = update[...].astype(BF16).astype(F32)
    dx = standardize_back(dn * cgain_ref[...], xhat0[...], scale0[...])
    stage[...] = stage[...] + dx.astype(BF16).astype(F32)
    for r in range(TR):
        grad_ref[r] = stage[SW * r + 2 : SW * r + 2 + TC, :].astype(BF16)

    for one in halo + halo2:
        one.wait_send()
    for n, send in enumerate((cot_send, fwd_send, res_send, gra_send)):
        wait_sent(send, grid_sem.at[n])


def finish(chunks_ref, kept_ref, out_ref, grad_ref, mixbuf):
    mixbuf[...] = chunks_ref[...].astype(F32).reshape(784, 128)
    for r in range(TR):
        for k in range(4):
            out_ref[r, :, 128 * k : 128 * (k + 1)] = mixbuf[
                pl.ds(112 * r + k, TC, stride=4), :
            ].astype(BF16)
    grad_ref[...] = kept_ref[...]


def local(
    inputs, cotangent, conv_gain, expand_weight, depth_weight, project_weight,
    block_gain, block_qkv, block_out, block_bias, grid_gain, grid_qkv, grid_out, grid_bias,
):
    def by_query(bias):
        return bias.transpose(1, 0, 2).reshape(16 * LEN, LEN)

    vmem, hbm = pl.BlockSpec(memory_space=pltpu.VMEM), pl.BlockSpec(memory_space=pl.ANY)
    places = jnp.asarray(PLACES, BF16)
    chunks = pltpu.VMEM((LEN, 16, 128), BF16)
    tokens = jax.ShapeDtypeStruct((TR, TC, D), BF16)
    bias = pltpu.VMEM((16 * LEN, LEN), F32)
    bias_t = pltpu.VMEM((4, WPAD, 256), F32)
    win_f32, win_bf16 = pltpu.VMEM((256, D), F32), pltpu.VMEM((256, D), BF16)
    packed = pltpu.VMEM((256, 3 * D), BF16)
    scale = pltpu.VMEM((256, 1), F32)
    prob = pltpu.VMEM((NWIN, 4, WPAD, 256), F32)
    scratch = [
        pltpu.VMEM(PLACES.shape, BF16), pltpu.VMEM((D, FF), BF16), pltpu.VMEM((FF, D), BF16),
        pltpu.VMEM((D, 3 * D), BF16), pltpu.VMEM((D, D), BF16), bias,
        pltpu.VMEM((D, 3 * D), BF16), pltpu.VMEM((D, D), BF16), bias,
        pltpu.SemaphoreType.DMA((9,)),
        pltpu.VMEM((224, D), F32), pltpu.VMEM((224, D), BF16), pltpu.VMEM((224, D), BF16),
        pltpu.VMEM((32, D), BF16), pltpu.VMEM((256, D), BF16), pltpu.VMEM((160, D), BF16),
        pltpu.SemaphoreType.DMA((2, 8)), pltpu.SemaphoreType.DMA((2, 8)),
        chunks, chunks, chunks, chunks, chunks, chunks, chunks, chunks,
        pltpu.SemaphoreType.DMA((4, 2)),
        pltpu.VMEM((832, 128), F32), pltpu.VMEM((224, D), F32), pltpu.VMEM((224, 1), F32),
        pltpu.VMEM((224, D), BF16), pltpu.VMEM((192, D), BF16), pltpu.VMEM((224, FF), F32),
        pltpu.VMEM((FF // 128, 288, 128), F32), pltpu.VMEM((FF // 128, 288, 128), F32),
        pltpu.VMEM((224, D), F32),
        bias_t, bias_t, win_f32, packed, win_f32, scale, prob, win_bf16,
        win_f32, win_f32, packed, win_f32, scale, prob, win_bf16, win_bf16, packed,
        pltpu.VMEM((96, D), BF16), pltpu.VMEM((FF // 128, 224, 128), F32),
    ]
    result, grad = pl.pallas_call(
        kernel,
        out_shape=(jax.ShapeDtypeStruct((LEN, 16, 128), BF16), tokens),
        in_specs=[vmem] * 6 + [hbm] * 9,
        out_specs=(vmem, vmem),
        scratch_shapes=scratch,
        compiler_params=pltpu.CompilerParams(
            collective_id=0, has_side_effects=True, vmem_limit_bytes=56 * 2**20
        ),
        name="mbconv_attention",
    )(
        inputs, cotangent, conv_gain.reshape(1, D), depth_weight, block_gain.reshape(1, D),
        grid_gain.reshape(1, D), places, expand_weight, project_weight, block_qkv, block_out,
        by_query(block_bias), grid_qkv, grid_out, by_query(grid_bias),
    )
    return pl.pallas_call(
        finish,
        out_shape=(tokens, tokens),
        in_specs=[vmem] * 2,
        out_specs=(vmem, vmem),
        scratch_shapes=[pltpu.VMEM((784, 128), F32)],
        name="finish",
    )(result, grad)


def solution(mesh):
    tokens = P("rows", "cols", None)
    in_specs = (tokens, tokens) + (P(),) * 12
    return jax.shard_map(
        local, mesh=mesh, in_specs=in_specs, out_specs=(tokens, tokens), check_vma=False
    )
```

```python
import functools

import jax
import jax.numpy as jnp
import numpy as np
from jax import lax
from jax.experimental import pallas as pl
from jax.experimental.pallas import tpu as pltpu
from jax.sharding import PartitionSpec as P

ROWS, COLS = 16, 8
HEIGHT, BREADTH = 112, 224
WIN = 7
D = 512
FF = 2048
HEAD_DIM = 32
TR, TC = 7, 28
SW = 32
NWIN, WPAD = 4, 64
LEN = 49
CHUNK = 2048
TILES = CHUNK // 128
EPSILON = 1e-05
F32, BF16 = jnp.float32, jnp.bfloat16
MESH = pl.DeviceIdType.MESH


def win_row(row, col):
    return WPAD * (col // WIN) + WIN * row + col % WIN


def placements():
    edge = np.zeros((32, 256))
    slots = np.zeros((256, 256))
    to_win = np.zeros((256, 256))
    from_win = np.zeros((208, 256))
    back_win = np.zeros((256, 256))
    for r in range(TR):
        for c in range(2):
            edge[2 * r + c, SW * r + c + 2] = 1
            edge[16 + 2 * r + c, SW * r + c + 28] = 1
        for c in range(TC):
            to_win[win_row(r, c), SW * r + c + 2] = 1
            slots[SW * r + c + 2, win_row(r, c)] = 1
            from_win[TC * r + c, win_row(r, c)] = 1
            back_win[win_row(r, c), TC * r + c] = 1
        slots[224 + r, win_row(r, 0)] = 1
        slots[240 + r, win_row(r, 27)] = 1
    halo = np.zeros((192, 256))
    for line in range(2):
        for c in range(TC):
            for half in range(2):
                at = 64 * half + SW * line + c + 2
                halo[at, at] = 1
        for c in range(2):
            for half in range(2):
                for side in range(2):
                    at = 64 * half + SW * line + (30 * side + c)
                    row = line + (0 if half else 5)
                    halo[at, 128 + 16 * (2 + 2 * half + side) + 2 * row + c] = 1
    for r in range(TR):
        for c in range(2):
            for side in range(2):
                halo[128 + 16 * (2 * side + c) + r + 2, 128 + 16 * side + 2 * r + c] = 1
    halo2 = np.zeros((96, 256))
    for half in range(2):
        for c in range(TC):
            halo2[32 * half + c + 2, 32 * half + c + 2] = 1
        for side in range(2):
            row = 0 if half else 6
            halo2[32 * half + 1 + 29 * side, 64 + 16 * (2 + 2 * half + side) + row] = 1
    for r in range(TR):
        for side in range(2):
            halo2[64 + 16 * side + r, 64 + 16 * side + r] = 1
    parts = dict(
        edge=edge, halo=halo, to_win=to_win, from_win=from_win, back_win=back_win,
        slots=slots, halo2=halo2,
    )
    starts, at = {}, 0
    for name, part in parts.items():
        starts[name] = (at, part.shape[0])
        at += part.shape[0]
    return np.concatenate(list(parts.values())), starts


PLACES, STARTS = placements()


def dot(a, b):
    return jnp.dot(a, b, preferred_element_type=F32)


def dot_nt(a, b):
    return lax.dot_general(a, b, (((1,), (1,)), ((), ())), preferred_element_type=F32)


def dot_tn(a, b):
    return lax.dot_general(a, b, (((0,), (0,)), ((), ())), preferred_element_type=F32)


def gelu_of(u):
    share = 0.5 + 0.5 * lax.erf(u * 0.5**0.5)
    density = jnp.exp2((-0.5 / np.log(2.0)) * (u * u))
    return u * share, share + (u * (0.5 / np.pi) ** 0.5) * density


def standardize(x):
    center = jnp.mean(x, axis=-1, keepdims=True)
    moved = x - center
    spread = jnp.mean(moved * moved, axis=-1, keepdims=True)
    scale = lax.rsqrt(spread + EPSILON)
    return moved * scale, scale


def standardize_back(grad, xhat, scale):
    first = jnp.mean(grad, axis=-1, keepdims=True)
    second = jnp.mean(grad * xhat, axis=-1, keepdims=True)
    return scale * (grad - first - xhat * second)


def by_head(x):
    head = lax.broadcasted_iota(jnp.int32, x.shape, 1) // HEAD_DIM
    zero = jnp.zeros_like(x)
    return jnp.concatenate([jnp.where(head == h, x, zero) for h in range(4)], axis=0)


def own_head(x):
    head = lax.broadcasted_iota(jnp.int32, (WPAD, 128), 1) // HEAD_DIM
    out = x[0:WPAD]
    for h in range(1, 4):
        out = jnp.where(head == h, x[WPAD * h : WPAD * (h + 1)], out)
    return out


def kernel(
    x_ref, cot_ref, cgain_ref, dw_ref, bgain_ref, ggain_ref,
    places_hbm, we_hbm, wp_hbm, bqkv_hbm, bout_hbm, bbias_hbm, gqkv_hbm, gout_hbm, gbias_hbm,
    out_ref, grad_ref,
    places, we, wp, bqkv, bout, bbias, gqkv, gout, gbias, load_sem,
    stage, own, cat, edges, own2, cat2, halo_sem, halo2_sem,
    cot_send, cot_recv, fwd_send, fwd_recv, res_send, res_recv, gra_send, gra_recv, grid_sem,
    mixbuf, xhat0, scale0, normed0, normed1, slope_u, slope_p, pre_act, update,
    bias_b, bias_g, zwin, packed_b, xhat_b, scale_b, prob_b, att,
    zgrid, dgrid, packed_g, xhat_g, scale_g, prob_g, dout, da, dpk, dscore, halo_grad, grad_e,
):
    i, j = lax.axis_index("rows"), lax.axis_index("cols")
    me = i * COLS + j

    def load(index, src, dst):
        return pltpu.make_async_copy(src, dst, load_sem.at[index])

    loads = [
        load(n, src, dst)
        for n, (src, dst) in enumerate(
            [
                (places_hbm, places), (we_hbm, we), (wp_hbm, wp), (bbias_hbm, bbias),
                (gbias_hbm, gbias), (bqkv_hbm, bqkv), (bout_hbm, bout),
                (gout_hbm, gout), (gqkv_hbm, gqkv),
            ]
        )
    ]
    for one in loads:
        one.start()
    l_places, l_we, l_wp, l_bb, l_gb, l_bqkv, l_bout, l_gout, l_gqkv = loads

    barrier = pltpu.get_barrier_semaphore()

    def greet(step, carry):
        other = lax.rem(me + step, ROWS * COLS)
        pl.semaphore_signal(
            barrier, inc=1, device_id=(lax.div(other, COLS), lax.rem(other, COLS)),
            device_id_type=MESH,
        )
        return carry

    lax.fori_loop(1, ROWS * COLS, greet, 0)

    def place(name, source):
        at, size = STARTS[name]
        return dot(places[at : at + size, 0 : source.shape[0]], source)

    stage[...] = jnp.zeros_like(stage)
    for r in range(TR):
        stage[SW * r + 2 : SW * r + 2 + TC, :] = x_ref[r].astype(F32)
    own[...] = stage[...].astype(BF16)
    l_places.wait()
    edges[...] = place("edge", own[...]).astype(BF16)

    mixbuf[...] = jnp.zeros_like(mixbuf)
    for r in range(TR):
        for k in range(4):
            mixbuf[pl.ds(112 * r + k, TC, stride=4), :] = cot_ref[
                r, :, 128 * k : 128 * (k + 1)
            ].astype(F32)
    cot_send[...] = mixbuf[0:784, :].reshape(LEN, 16, 128).astype(BF16)

    def flip(bias, h):
        square = jnp.concatenate(
            [bias[pl.ds(h, LEN, stride=16), :], jnp.zeros((LEN, 128 - LEN), F32)], axis=1
        )
        square = jnp.concatenate([square, jnp.zeros((WPAD - LEN, 128), F32)], axis=0)
        turned = square.T[0:WPAD]
        key = lax.broadcasted_iota(jnp.int32, (WPAD, WPAD), 0)
        return jnp.where(key < LEN, turned, -1e30)

    def flip_all(bias, bias_t):
        for g in range(4):
            for h in range(2):
                pair = [flip(bias, 4 * g + 2 * h + n) for n in range(2)]
                bias_t[g, :, 128 * h : 128 * (h + 1)] = jnp.concatenate(pair, axis=1)

    l_bb.wait()
    flip_all(bbias, bias_b)
    l_gb.wait()
    flip_all(gbias, bias_g)

    xhat, scale = standardize(stage[...])
    xhat0[...] = xhat
    scale0[...] = scale
    normed0[...] = (xhat * cgain_ref[...]).astype(BF16)
    l_we.wait()

    def taps(at):
        return [dw_ref[n : n + 1, pl.ds(at, CHUNK)] for n in range(9)]

    def wide(ref, step, rows=slice(None)):
        return jnp.concatenate([ref[step * TILES + n, rows, :] for n in range(TILES)], axis=1)

    def put_wide(ref, step, rows, value):
        for n in range(TILES):
            ref[step * TILES + n, rows, :] = value[:, 128 * n : 128 * (n + 1)]

    def add_wide(ref, step, first, value):
        rows = slice(first, first + value.shape[0])
        put_wide(ref, step, rows, wide(ref, step, rows) + value)

    def lines(x, first, last):
        return x[SW * first : SW * last]

    def side_by_side(y):
        count = y[0].shape[0]
        return pltpu.roll(y[0], 1, 0) + y[1] + pltpu.roll(y[2], count - 1, 0)

    def expand_own(step, carry):
        at = pl.multiple_of(step * CHUNK, CHUNK)
        e, slope = gelu_of(dot(normed0[...], we[:, pl.ds(at, CHUNK)]))
        slope_u[:, pl.ds(at, CHUNK)] = slope
        e = e.astype(BF16).astype(F32)
        w = taps(at)
        y = []
        for b in range(3):
            t = [e * w[3 * a + b] for a in range(3)]
            y.append(
                jnp.concatenate(
                    [
                        lines(t[2], 0, 1),
                        lines(t[1], 0, 1) + lines(t[2], 1, 2),
                        lines(t[0], 0, 5) + lines(t[1], 1, 6) + lines(t[2], 2, 7),
                        lines(t[0], 5, 6) + lines(t[1], 6, 7),
                        lines(t[0], 6, 7),
                    ],
                    axis=0,
                )
            )
        put_wide(pre_act, step, slice(None), side_by_side(y))
        return carry

    lax.fori_loop(0, 1, expand_own, 0)
    pl.semaphore_wait(barrier, ROWS * COLS - 1)

    north, south = lax.rem(i + ROWS - 1, ROWS), lax.rem(i + 1, ROWS)
    west, east = lax.rem(j + COLS - 1, COLS), lax.rem(j + 1, COLS)

    def swap(sems, parts):
        copies = [
            pltpu.make_async_remote_copy(
                src_ref=src, dst_ref=dst, send_sem=sems.at[0, n], recv_sem=sems.at[1, n],
                device_id=to, device_id_type=MESH,
            )
            for n, (src, dst, to) in enumerate(parts)
        ]
        for one in copies:
            one.start()
        return copies

    w_cols, e_cols = edges.at[pl.ds(0, 16)], edges.at[pl.ds(16, 16)]
    halo = swap(
        halo_sem,
        [
            (own.at[pl.ds(0, 64)], cat.at[pl.ds(64, 64)], (north, j)),
            (own.at[pl.ds(160, 64)], cat.at[pl.ds(0, 64)], (south, j)),
            (e_cols, cat.at[pl.ds(128, 16)], (i, east)),
            (w_cols, cat.at[pl.ds(144, 16)], (i, west)),
            (e_cols, cat.at[pl.ds(160, 16)], (south, east)),
            (w_cols, cat.at[pl.ds(176, 16)], (south, west)),
            (e_cols, cat.at[pl.ds(192, 16)], (north, east)),
            (w_cols, cat.at[pl.ds(208, 16)], (north, west)),
        ],
    )

    def send_chunks(send, recv, sems, forward):
        def body(c, carry):
            a, b = lax.div(c, WIN), lax.rem(c, WIN)
            if forward:
                row, col = WIN * i + a, WIN * j + b
                ti, tj = lax.rem(row, ROWS), lax.rem(col, COLS)
                slot = lax.div(row, ROWS) * WIN + lax.div(col, COLS)
            else:
                row, col = ROWS * a + i, COLS * b + j
                ti, tj = lax.div(row, WIN), lax.div(col, WIN)
                slot = lax.rem(row, WIN) * WIN + lax.rem(col, WIN)
            mine = jnp.logical_and(ti == i, tj == j)

            @pl.when(mine)
            def _():
                pltpu.make_async_copy(send.at[c], recv.at[slot], sems.at[1]).start()

            @pl.when(jnp.logical_not(mine))
            def _():
                pltpu.make_async_remote_copy(
                    src_ref=send.at[c], dst_ref=recv.at[slot], send_sem=sems.at[0],
                    recv_sem=sems.at[1], device_id=(ti, tj), device_id_type=MESH,
                ).start()

            return carry

        lax.fori_loop(0, LEN, body, 0)

    def wait_chunks(recv, sems):
        pltpu.make_async_copy(recv, recv, sems.at[1]).wait()

    def wait_sent(send, sems):
        some = lax.rem(10 * i, ROWS) < WIN

        @pl.when(some)
        def _():
            part = send.at[pl.ds(0, LEN - 1)]
            pltpu.make_async_copy(part, part, sems.at[0]).wait()

        @pl.when(jnp.logical_not(some))
        def _():
            pltpu.make_async_copy(send, send, sems.at[0]).wait()

    send_chunks(cot_send, cot_recv, grid_sem.at[0], True)

    lax.fori_loop(1, FF // CHUNK, expand_own, 0)

    for one in halo:
        one.wait_recv()
    has_n, has_s, has_w, has_e = (
        jnp.where(there, 1.0, 0.0) for there in (i > 0, i < ROWS - 1, j > 0, j < COLS - 1)
    )

    def inside(count, strip, column):
        at = lax.broadcasted_iota(jnp.int32, (count, 1), 0)
        slot = lax.bitwise_and(at, SW - 1)
        keep = jnp.where(slot < 2, has_w, 1.0) * jnp.where(slot < 30, 1.0, has_e)
        strips = jnp.where(at < strip, has_n, has_s) * keep
        columns = jnp.where(at < 2 * strip + column, has_w, has_e)
        return jnp.where(at < 2 * strip, strips, columns)

    xh = place("halo", cat[...]) * inside(192, 64, 32)
    normed1[...] = (standardize(xh)[0] * cgain_ref[...]).astype(BF16)
    update[...] = jnp.zeros_like(update)
    l_wp.wait()

    def add_column(ref, slot, count, step, value):
        rows = pl.ds(slot, count, stride=SW)
        put_wide(ref, step, rows, wide(ref, step, rows) + value[0:count])

    def mbconv(step, carry):
        at = pl.multiple_of(step * CHUNK, CHUNK)
        here = pl.ds(at, CHUNK)
        e, _ = gelu_of(dot(normed1[...], we[:, here]))
        e = e.astype(BF16).astype(F32)
        w = taps(at)
        n0, n1, s0, s1 = (lines(e, n, n + 1) for n in range(4))
        w0, w1, e0, e1 = (e[128 + 16 * n : 144 + 16 * n] for n in range(4))
        around = [
            (0, [n0 * w[b] + n1 * w[3 + b] for b in range(3)]),
            (32, [n1 * w[b] for b in range(3)]),
            (224, [s0 * w[6 + b] for b in range(3)]),
            (256, [s0 * w[3 + b] + s1 * w[6 + b] for b in range(3)]),
        ]
        for first, y in around:
            add_wide(pre_act, step, first, side_by_side(y))

        def down(terms):
            return terms[0] + pltpu.roll(terms[1], 15, 0) + pltpu.roll(terms[2], 14, 0)

        sides = [
            (1, [w0 * w[3 * a] + w1 * w[3 * a + 1] for a in range(3)]),
            (2, [w1 * w[3 * a] for a in range(3)]),
            (29, [e0 * w[3 * a + 2] for a in range(3)]),
            (30, [e0 * w[3 * a + 1] + e1 * w[3 * a + 2] for a in range(3)]),
        ]
        for slot, terms in sides:
            add_column(pre_act, slot, 9, step, down(terms))
        branch, slope = gelu_of(wide(pre_act, step))
        put_wide(slope_p, step, slice(None), slope)
        update[...] += dot(branch[32:256].astype(BF16), wp[here, :])
        return carry

    lax.fori_loop(0, FF // CHUNK, mbconv, 0)
    mixed = (stage[...] + update[...]).astype(BF16)
    zwin[...] = place("to_win", mixed)

    root = HEAD_DIM**-0.5

    def project_in(z, gain_ref, qkv, packed, xhat_ref, scale_ref):
        xhat, scale = standardize(z)
        xhat_ref[...] = xhat
        scale_ref[...] = scale
        normed = (xhat * gain_ref[...]).astype(BF16)
        for n in range(3):
            at = n * 512
            packed[:, at : at + 512] = dot(normed, qkv[:, at : at + 512]).astype(BF16)

    def parts_of(packed, rows, g):
        return [packed[rows, 512 * n + 128 * g : 512 * n + 128 * (g + 1)] for n in range(3)]

    def attend(packed, bias_t, prob):
        def window(w, carry):
            rows = pl.ds(pl.multiple_of(w * WPAD, WPAD), WPAD)
            for g in range(4):
                q, k, v = parts_of(packed, rows, g)
                s = dot_nt(k, by_head(q)) * root + bias_t[g]
                e = jnp.exp(s - jnp.max(s, axis=0, keepdims=True))
                prob[w, g] = e * (1.0 / jnp.sum(e, axis=0, keepdims=True))
            return carry

        lax.fori_loop(0, NWIN, window, 0, unroll=True)

        def gather(w, carry):
            rows = pl.ds(pl.multiple_of(w * WPAD, WPAD), WPAD)
            for g in range(4):
                v = parts_of(packed, rows, g)[2]
                one = own_head(dot_tn(prob[w, g].astype(BF16), v))
                att[rows, 128 * g : 128 * (g + 1)] = one.astype(BF16)
            return carry

        lax.fori_loop(0, NWIN, gather, 0, unroll=True)

    def attend_back(packed, prob):
        def window(w, carry):
            rows = pl.ds(pl.multiple_of(w * WPAD, WPAD), WPAD)
            for g in range(4):
                q, k, v = parts_of(packed, rows, g)
                p = prob[w, g]
                dam = by_head(da[rows, 128 * g : 128 * (g + 1)])
                dp = dot_nt(v, dam).astype(BF16).astype(F32)
                ds = p * (dp - jnp.sum(p * dp, axis=0, keepdims=True))
                ds = ds.astype(BF16)
                dscore[w, g] = ds
                dk = dot(ds, by_head(q)) * root
                dv = dot(p.astype(BF16), dam)
                for n, one in ((1, dk), (2, dv)):
                    dpk[rows, 512 * n + 128 * g : 512 * n + 128 * (g + 1)] = one.astype(BF16)
            return carry

        lax.fori_loop(0, NWIN, window, 0, unroll=True)

        def queries(w, carry):
            rows = pl.ds(pl.multiple_of(w * WPAD, WPAD), WPAD)
            for g in range(4):
                k = parts_of(packed, rows, g)[1]
                dq = own_head(dot_tn(dscore[w, g], k)) * root
                dpk[rows, 128 * g : 128 * (g + 1)] = dq.astype(BF16)
            return carry

        lax.fori_loop(0, NWIN, queries, 0, unroll=True)

    def project_back(qkv, gain_ref, xhat_ref, scale_ref):
        dn = dot_nt(dpk[...], qkv[...]).astype(BF16).astype(F32)
        dx = standardize_back(dn * gain_ref[...], xhat_ref[...], scale_ref[...])
        return (dout[...].astype(F32) + dx.astype(BF16).astype(F32)).astype(BF16)

    l_bqkv.wait()
    project_in(zwin[...], bgain_ref, bqkv, packed_b, xhat_b, scale_b)
    attend(packed_b, bias_b, prob_b)
    l_bout.wait()
    blocked = (zwin[...] + dot(att[...], bout[...])).astype(BF16)

    spatial = place("from_win", blocked)
    for k in range(4):
        mixbuf[pl.ds(k, 208, stride=4), :] = spatial[:, 128 * k : 128 * (k + 1)]
    fwd_send[...] = mixbuf[0:784, :].reshape(LEN, 16, 128).astype(BF16)
    send_chunks(fwd_send, fwd_recv, grid_sem.at[1], True)

    def to_windows(recv, target):
        mixbuf[0:784, :] = recv[...].astype(F32).reshape(784, 128)
        for w in range(NWIN):
            for k in range(4):
                target[WPAD * w : WPAD * w + LEN, 128 * k : 128 * (k + 1)] = mixbuf[
                    pl.ds(4 * w + k, LEN, stride=16), :
                ]

    def from_windows(source, send):
        for w in range(NWIN):
            for k in range(4):
                mixbuf[pl.ds(4 * w + k, LEN, stride=16), :] = source[
                    WPAD * w : WPAD * w + LEN, 128 * k : 128 * (k + 1)
                ]
        send[...] = mixbuf[0:784, :].reshape(LEN, 16, 128).astype(BF16)

    dgrid[...] = jnp.zeros_like(dgrid)
    zgrid[...] = jnp.zeros_like(zgrid)
    wait_chunks(cot_recv, grid_sem.at[0])
    to_windows(cot_recv, dgrid)
    dout[...] = dgrid[...].astype(BF16)
    l_gout.wait()
    da[...] = dot_nt(dout[...], gout[...]).astype(BF16)
    l_gqkv.wait()

    wait_chunks(fwd_recv, grid_sem.at[1])
    to_windows(fwd_recv, zgrid)
    project_in(zgrid[...], ggain_ref, gqkv, packed_g, xhat_g, scale_g)
    attend(packed_g, bias_g, prob_g)
    attend_back(packed_g, prob_g)
    dgrid[...] = project_back(gqkv, ggain_ref, xhat_g, scale_g).astype(F32)
    from_windows(dgrid, gra_send)
    send_chunks(gra_send, gra_recv, grid_sem.at[3], False)
    zgrid[...] = (zgrid[...] + dot(att[...], gout[...])).astype(BF16).astype(F32)
    from_windows(zgrid, res_send)
    send_chunks(res_send, res_recv, grid_sem.at[2], False)

    wait_chunks(gra_recv, grid_sem.at[3])
    mixbuf[0:784, :] = gra_recv[...].astype(F32).reshape(784, 128)
    mixbuf[784:832, :] = jnp.zeros((48, 128), F32)
    spatial = jnp.concatenate([mixbuf[pl.ds(k, 208, stride=4), :] for k in range(4)], axis=1)
    dout[...] = place("back_win", spatial.astype(BF16)).astype(BF16)
    da[...] = dot_nt(dout[...], bout[...]).astype(BF16)
    attend_back(packed_b, prob_b)
    slotted = place("slots", project_back(bqkv, bgain_ref, xhat_b, scale_b))
    stage[...] = slotted[0:224]
    own2[...] = slotted.astype(BF16)
    w_col2, e_col2 = own2.at[pl.ds(224, 16)], own2.at[pl.ds(240, 16)]
    halo2 = swap(
        halo2_sem,
        [
            (own2.at[pl.ds(0, 32)], cat2.at[pl.ds(32, 32)], (north, j)),
            (own2.at[pl.ds(192, 32)], cat2.at[pl.ds(0, 32)], (south, j)),
            (e_col2, cat2.at[pl.ds(64, 16)], (i, east)),
            (w_col2, cat2.at[pl.ds(80, 16)], (i, west)),
            (e_col2, cat2.at[pl.ds(96, 16)], (south, east)),
            (w_col2, cat2.at[pl.ds(112, 16)], (south, west)),
            (e_col2, cat2.at[pl.ds(128, 16)], (north, east)),
            (w_col2, cat2.at[pl.ds(144, 16)], (north, west)),
        ],
    )

    def back_own(step, carry):
        here = pl.ds(pl.multiple_of(step * CHUNK, CHUNK), CHUNK)
        gp = dot_nt(own2[0:224, :], wp[here, :]).astype(BF16).astype(F32)
        gp = gp * wide(slope_p, step, slice(32, 256))
        w = taps(pl.multiple_of(step * CHUNK, CHUNK))
        y = []
        for b in range(3):
            t = [gp * w[3 * a + 2 - b] for a in range(3)]
            y.append(
                jnp.concatenate(
                    [
                        lines(t[0], 1, 2) + lines(t[1], 0, 1),
                        lines(t[0], 2, 7) + lines(t[1], 1, 6) + lines(t[2], 0, 5),
                        lines(t[1], 6, 7) + lines(t[2], 5, 6),
                    ],
                    axis=0,
                )
            )
        put_wide(grad_e, step, slice(None), side_by_side(y))
        return carry

    lax.fori_loop(0, FF // CHUNK, back_own, 0)
    update[...] = jnp.zeros_like(update)
    wait_chunks(res_recv, grid_sem.at[2])
    out_ref[...] = res_recv[...]

    for one in halo2:
        one.wait_recv()
    gm = place("halo2", cat2[...]) * inside(96, 32, 16)
    halo_grad[...] = gm.astype(BF16)

    def mbconv_back(step, carry):
        at = pl.multiple_of(step * CHUNK, CHUNK)
        here = pl.ds(at, CHUNK)
        gp = dot_nt(halo_grad[...], wp[here, :]).astype(BF16).astype(F32)
        w = taps(at)

        north_gp = gp[0:32] * wide(slope_p, step, slice(0, 32))
        south_gp = gp[32:64] * wide(slope_p, step, slice(256, 288))
        west_gp = gp[64:72] * wide(slope_p, step, pl.ds(SW + 1, 8, stride=SW))
        east_gp = gp[80:88] * wide(slope_p, step, pl.ds(SW + 30, 8, stride=SW))
        add_wide(grad_e, step, 0, side_by_side([north_gp * w[8 - b] for b in range(3)]))
        add_wide(grad_e, step, 192, side_by_side([south_gp * w[2 - b] for b in range(3)]))

        def down(x, b):
            return (
                pltpu.roll(x * w[b], 7, 0) + x * w[3 + b] + pltpu.roll(x * w[6 + b], 1, 0)
            )

        add_column(grad_e, 2, 7, step, down(west_gp, 2))
        add_column(grad_e, 29, 7, step, down(east_gp, 0))
        gh = wide(grad_e, step).astype(BF16).astype(F32) * slope_u[:, here]
        update[...] += dot_nt(gh.astype(BF16), we[:, here])
        return carry

    lax.fori_loop(0, FF // CHUNK, mbconv_back, 0)
    dn = update[...].astype(BF16).astype(F32)
    dx = standardize_back(dn * cgain_ref[...], xhat0[...], scale0[...])
    stage[...] = stage[...] + dx.astype(BF16).astype(F32)
    for r in range(TR):
        grad_ref[r] = stage[SW * r + 2 : SW * r + 2 + TC, :].astype(BF16)

    for one in halo + halo2:
        one.wait_send()
    for n, send in enumerate((cot_send, fwd_send, res_send, gra_send)):
        wait_sent(send, grid_sem.at[n])


def finish(chunks_ref, kept_ref, out_ref, grad_ref, mixbuf):
    mixbuf[...] = chunks_ref[...].astype(F32).reshape(784, 128)
    for r in range(TR):
        for k in range(4):
            out_ref[r, :, 128 * k : 128 * (k + 1)] = mixbuf[
                pl.ds(112 * r + k, TC, stride=4), :
            ].astype(BF16)
    grad_ref[...] = kept_ref[...]


def local(
    inputs, cotangent, conv_gain, expand_weight, depth_weight, project_weight,
    block_gain, block_qkv, block_out, block_bias, grid_gain, grid_qkv, grid_out, grid_bias,
):
    def by_query(bias):
        return bias.transpose(1, 0, 2).reshape(16 * LEN, LEN)

    vmem, hbm = pl.BlockSpec(memory_space=pltpu.VMEM), pl.BlockSpec(memory_space=pl.ANY)
    places = jnp.asarray(PLACES, BF16)
    chunks = pltpu.VMEM((LEN, 16, 128), BF16)
    tokens = jax.ShapeDtypeStruct((TR, TC, D), BF16)
    bias = pltpu.VMEM((16 * LEN, LEN), F32)
    bias_t = pltpu.VMEM((4, WPAD, 256), F32)
    win_f32, win_bf16 = pltpu.VMEM((256, D), F32), pltpu.VMEM((256, D), BF16)
    packed = pltpu.VMEM((256, 3 * D), BF16)
    scale = pltpu.VMEM((256, 1), F32)
    prob = pltpu.VMEM((NWIN, 4, WPAD, 256), F32)
    scratch = [
        pltpu.VMEM(PLACES.shape, BF16), pltpu.VMEM((D, FF), BF16), pltpu.VMEM((FF, D), BF16),
        pltpu.VMEM((D, 3 * D), BF16), pltpu.VMEM((D, D), BF16), bias,
        pltpu.VMEM((D, 3 * D), BF16), pltpu.VMEM((D, D), BF16), bias,
        pltpu.SemaphoreType.DMA((9,)),
        pltpu.VMEM((224, D), F32), pltpu.VMEM((224, D), BF16), pltpu.VMEM((224, D), BF16),
        pltpu.VMEM((32, D), BF16), pltpu.VMEM((256, D), BF16), pltpu.VMEM((160, D), BF16),
        pltpu.SemaphoreType.DMA((2, 8)), pltpu.SemaphoreType.DMA((2, 8)),
        chunks, chunks, chunks, chunks, chunks, chunks, chunks, chunks,
        pltpu.SemaphoreType.DMA((4, 2)),
        pltpu.VMEM((832, 128), F32), pltpu.VMEM((224, D), F32), pltpu.VMEM((224, 1), F32),
        pltpu.VMEM((224, D), BF16), pltpu.VMEM((192, D), BF16), pltpu.VMEM((224, FF), F32),
        pltpu.VMEM((FF // 128, 288, 128), F32), pltpu.VMEM((FF // 128, 288, 128), F32),
        pltpu.VMEM((224, D), F32),
        bias_t, bias_t, win_f32, packed, win_f32, scale, prob, win_bf16,
        win_f32, win_f32, packed, win_f32, scale, prob, win_bf16, win_bf16, packed,
        pltpu.VMEM((NWIN, 4, WPAD, 256), BF16), pltpu.VMEM((96, D), BF16),
        pltpu.VMEM((FF // 128, 224, 128), F32),
    ]
    result, grad = pl.pallas_call(
        kernel,
        out_shape=(jax.ShapeDtypeStruct((LEN, 16, 128), BF16), tokens),
        in_specs=[vmem] * 6 + [hbm] * 9,
        out_specs=(vmem, vmem),
        scratch_shapes=scratch,
        compiler_params=pltpu.CompilerParams(
            collective_id=0, has_side_effects=True, vmem_limit_bytes=56 * 2**20
        ),
        name="mbconv_attention",
    )(
        inputs, cotangent, conv_gain.reshape(1, D), depth_weight, block_gain.reshape(1, D),
        grid_gain.reshape(1, D), places, expand_weight, project_weight, block_qkv, block_out,
        by_query(block_bias), grid_qkv, grid_out, by_query(grid_bias),
    )
    return pl.pallas_call(
        finish,
        out_shape=(tokens, tokens),
        in_specs=[vmem] * 2,
        out_specs=(vmem, vmem),
        scratch_shapes=[pltpu.VMEM((784, 128), F32)],
        name="finish",
    )(result, grad)


def solution(mesh):
    tokens = P("rows", "cols", None)
    in_specs = (tokens, tokens) + (P(),) * 12
    return jax.shard_map(
        local, mesh=mesh, in_specs=in_specs, out_specs=(tokens, tokens), check_vma=False
    )
```

```python
import functools

import jax
import jax.numpy as jnp
import numpy as np
from jax import lax
from jax.experimental import pallas as pl
from jax.experimental.pallas import tpu as pltpu
from jax.sharding import PartitionSpec as P

ROWS, COLS = 16, 8
HEIGHT, BREADTH = 112, 224
WIN = 7
D = 512
FF = 2048
HEAD_DIM = 32
TR, TC = 7, 28
SW = 32
NWIN, WPAD = 4, 64
LEN = 49
EPSILON = 1e-05
F32, BF16 = jnp.float32, jnp.bfloat16
MESH = pl.DeviceIdType.MESH


def win_row(row, col):
    return WPAD * (col // WIN) + WIN * row + col % WIN


def placements():
    edge = np.zeros((32, 256))
    slots = np.zeros((256, 256))
    to_win = np.zeros((256, 256))
    from_win = np.zeros((208, 256))
    back_win = np.zeros((256, 256))
    for r in range(TR):
        for c in range(2):
            edge[2 * r + c, SW * r + c + 2] = 1
            edge[16 + 2 * r + c, SW * r + c + 28] = 1
        for c in range(TC):
            to_win[win_row(r, c), SW * r + c + 2] = 1
            slots[SW * r + c + 2, win_row(r, c)] = 1
            from_win[TC * r + c, win_row(r, c)] = 1
            back_win[win_row(r, c), TC * r + c] = 1
        slots[224 + r, win_row(r, 0)] = 1
        slots[240 + r, win_row(r, 27)] = 1
    halo = np.zeros((160, 256))
    for line in range(2):
        for c in range(TC):
            for half in range(2):
                at = 64 * half + SW * line + c + 2
                halo[at, at] = 1
        for c in range(2):
            for half in range(2):
                for side in range(2):
                    at = 64 * half + SW * line + (30 * side + c)
                    row = line + (0 if half else 5)
                    halo[at, 128 + 16 * (2 + 2 * half + side) + 2 * row + c] = 1
    for r in range(TR):
        for c in range(2):
            for side in range(2):
                halo[128 + 8 * (2 * side + c) + r, 128 + 16 * side + 2 * r + c] = 1
    halo2 = np.zeros((80, 256))
    for half in range(2):
        for c in range(TC):
            halo2[32 * half + c + 2, 32 * half + c + 2] = 1
        for side in range(2):
            row = 0 if half else 6
            halo2[32 * half + 1 + 29 * side, 64 + 16 * (2 + 2 * half + side) + row] = 1
    for r in range(TR):
        for side in range(2):
            halo2[64 + 8 * side + r, 64 + 16 * side + r] = 1
    parts = dict(
        edge=edge, halo=halo, to_win=to_win, from_win=from_win, back_win=back_win,
        slots=slots, halo2=halo2,
    )
    starts, at = {}, 0
    for name, part in parts.items():
        starts[name] = (at, part.shape[0])
        at += part.shape[0]
    return np.concatenate(list(parts.values())), starts


PLACES, STARTS = placements()


def dot(a, b):
    return jnp.dot(a, b, preferred_element_type=F32)


def dot_nt(a, b):
    return lax.dot_general(a, b, (((1,), (1,)), ((), ())), preferred_element_type=F32)


def dot_tn(a, b):
    return lax.dot_general(a, b, (((0,), (0,)), ((), ())), preferred_element_type=F32)


def gelu_of(u):
    share = 0.5 + 0.5 * lax.erf(u * 0.5**0.5)
    density = jnp.exp2((-0.5 / np.log(2.0)) * (u * u))
    return u * share, share + (u * (0.5 / np.pi) ** 0.5) * density


def standardize(x):
    center = jnp.mean(x, axis=-1, keepdims=True)
    moved = x - center
    spread = jnp.mean(moved * moved, axis=-1, keepdims=True)
    scale = lax.rsqrt(spread + EPSILON)
    return moved * scale, scale


def standardize_back(grad, xhat, scale):
    first = jnp.mean(grad, axis=-1, keepdims=True)
    second = jnp.mean(grad * xhat, axis=-1, keepdims=True)
    return scale * (grad - first - xhat * second)


def by_head(x):
    head = lax.broadcasted_iota(jnp.int32, x.shape, 1) // HEAD_DIM
    zero = jnp.zeros_like(x)
    return jnp.concatenate([jnp.where(head == h, x, zero) for h in range(4)], axis=0)


def own_head(x):
    head = lax.broadcasted_iota(jnp.int32, (WPAD, 128), 1) // HEAD_DIM
    out = x[0:WPAD]
    for h in range(1, 4):
        out = jnp.where(head == h, x[WPAD * h : WPAD * (h + 1)], out)
    return out


def kernel(
    x_ref, cot_ref, cgain_ref, dw_ref, bgain_ref, ggain_ref,
    places_hbm, we_hbm, wp_hbm, bqkv_hbm, bout_hbm, bbias_hbm, gqkv_hbm, gout_hbm, gbias_hbm,
    out_ref, grad_ref,
    places, we, wp, bqkv, bout, bbias, gqkv, gout, gbias, load_sem, reach,
    stage, own, cat, edges, own2, cat2, halo_sem, halo2_sem,
    cot_send, cot_recv, fwd_send, fwd_recv, res_send, res_recv, gra_send, gra_recv, grid_sem,
    mixbuf, xhat0, scale0, normed0, normed1, slope_u, slope_p, pre_act, update,
    bias_b, bias_g, zwin, packed_b, xhat_b, scale_b, prob_b, att,
    zgrid, dgrid, packed_g, xhat_g, scale_g, prob_g, dout, da, dpk, dscore, halo_grad, grad_e,
):
    i, j = lax.axis_index("rows"), lax.axis_index("cols")
    me = i * COLS + j

    def load(index, src, dst):
        return pltpu.make_async_copy(src, dst, load_sem.at[index])

    loads = [
        load(n, src, dst)
        for n, (src, dst) in enumerate(
            [
                (places_hbm, places), (we_hbm, we), (wp_hbm, wp), (bbias_hbm, bbias),
                (gbias_hbm, gbias), (bqkv_hbm, bqkv), (bout_hbm, bout),
                (gout_hbm, gout), (gqkv_hbm, gqkv),
            ]
        )
    ]
    for one in loads:
        one.start()
    l_places, l_we, l_wp, l_bb, l_gb, l_bqkv, l_bout, l_gout, l_gqkv = loads

    def around(step, rows=(-1, 0, 1), cols=(-1, 0, 1)):
        for a in rows:
            for b in cols:
                if a or b:
                    yield lax.rem(i + ROWS + step * a, ROWS), lax.rem(j + COLS + step * b, COLS)

    def greet(sem, devices):
        for device in devices:
            pl.semaphore_signal(sem, inc=1, device_id=device, device_id_type=MESH)

    barrier = pltpu.get_barrier_semaphore()
    greet(barrier, around(1))

    def place(name, source):
        at, size = STARTS[name]
        return dot(places[at : at + size, 0 : source.shape[0]], source)

    stage[...] = jnp.zeros_like(stage)
    for r in range(TR):
        stage[SW * r + 2 : SW * r + 2 + TC, :] = x_ref[r].astype(F32)
    own[...] = stage[...].astype(BF16)
    l_places.wait()
    edges[...] = place("edge", own[...]).astype(BF16)

    mixbuf[...] = jnp.zeros_like(mixbuf)
    for r in range(TR):
        for k in range(4):
            mixbuf[pl.ds(112 * r + k, TC, stride=4), :] = cot_ref[
                r, :, 128 * k : 128 * (k + 1)
            ].astype(F32)
    cot_send[...] = mixbuf[0:784, :].reshape(LEN, 16, 128).astype(BF16)

    pl.semaphore_wait(barrier, 8)

    north, south = lax.rem(i + ROWS - 1, ROWS), lax.rem(i + 1, ROWS)
    west, east = lax.rem(j + COLS - 1, COLS), lax.rem(j + 1, COLS)

    def swap(sems, parts):
        copies = [
            pltpu.make_async_remote_copy(
                src_ref=src, dst_ref=dst, send_sem=sems.at[0, n], recv_sem=sems.at[1, n],
                device_id=to, device_id_type=MESH,
            )
            for n, (src, dst, to) in enumerate(parts)
        ]
        for one in copies:
            one.start()
        return copies

    w_cols, e_cols = edges.at[pl.ds(0, 16)], edges.at[pl.ds(16, 16)]
    halo = swap(
        halo_sem,
        [
            (own.at[pl.ds(0, 64)], cat.at[pl.ds(64, 64)], (north, j)),
            (own.at[pl.ds(160, 64)], cat.at[pl.ds(0, 64)], (south, j)),
            (e_cols, cat.at[pl.ds(128, 16)], (i, east)),
            (w_cols, cat.at[pl.ds(144, 16)], (i, west)),
            (e_cols, cat.at[pl.ds(160, 16)], (south, east)),
            (w_cols, cat.at[pl.ds(176, 16)], (south, west)),
            (e_cols, cat.at[pl.ds(192, 16)], (north, east)),
            (w_cols, cat.at[pl.ds(208, 16)], (north, west)),
        ],
    )

    def send_chunks(send, recv, sems, forward):
        def body(c, carry):
            a, b = lax.div(c, WIN), lax.rem(c, WIN)
            if forward:
                row, col = WIN * i + a, WIN * j + b
                ti, tj = lax.rem(row, ROWS), lax.rem(col, COLS)
                slot = lax.div(row, ROWS) * WIN + lax.div(col, COLS)
            else:
                row, col = ROWS * a + i, COLS * b + j
                ti, tj = lax.div(row, WIN), lax.div(col, WIN)
                slot = lax.rem(row, WIN) * WIN + lax.rem(col, WIN)
            mine = jnp.logical_and(ti == i, tj == j)

            @pl.when(mine)
            def _():
                pltpu.make_async_copy(send.at[c], recv.at[slot], sems.at[1]).start()

            @pl.when(jnp.logical_not(mine))
            def _():
                pltpu.make_async_remote_copy(
                    src_ref=send.at[c], dst_ref=recv.at[slot], send_sem=sems.at[0],
                    recv_sem=sems.at[1], device_id=(ti, tj), device_id_type=MESH,
                ).start()

            return carry

        lax.fori_loop(0, LEN, body, 0)

    def wait_chunks(recv, sems):
        pltpu.make_async_copy(recv, recv, sems.at[1]).wait()

    def wait_sent(send, sems):
        some = lax.rem(10 * i, ROWS) < WIN

        @pl.when(some)
        def _():
            part = send.at[pl.ds(0, LEN - 1)]
            pltpu.make_async_copy(part, part, sems.at[0]).wait()

        @pl.when(jnp.logical_not(some))
        def _():
            pltpu.make_async_copy(send, send, sems.at[0]).wait()

    greet(reach.at[0], around(1))

    xhat, scale = standardize(stage[...])
    xhat0[...] = xhat
    scale0[...] = scale
    normed0[...] = (xhat * cgain_ref[...]).astype(BF16)
    l_we.wait()

    w = [dw_ref[n : n + 1, :] for n in range(9)]

    def wide(ref, rows=slice(None)):
        return jnp.concatenate([ref[n, rows, :] for n in range(ref.shape[0])], axis=1)

    def put_wide(ref, rows, value):
        for n in range(ref.shape[0]):
            ref[n, rows, :] = value[:, 128 * n : 128 * (n + 1)]

    def add_wide(ref, rows, value):
        put_wide(ref, rows, wide(ref, rows) + value)

    def column(first, count):
        return pl.ds(first, count, stride=SW)

    def lines(x, first, last):
        return x[SW * first : SW * last]

    def side_by_side(y):
        count = y[0].shape[0]
        return pltpu.roll(y[0], 1, 0) + y[1] + pltpu.roll(y[2], count - 1, 0)

    def expand_own():
        e, slope = gelu_of(dot(normed0[...], we[...]))
        put_wide(slope_u, slice(0, 224), slope)
        e = e.astype(BF16).astype(F32)
        y = []
        for b in range(3):
            t = [e * w[3 * a + b] for a in range(3)]
            y.append(
                jnp.concatenate(
                    [
                        lines(t[2], 0, 1),
                        lines(t[1], 0, 1) + lines(t[2], 1, 2),
                        lines(t[0], 0, 5) + lines(t[1], 1, 6) + lines(t[2], 2, 7),
                        lines(t[0], 5, 6) + lines(t[1], 6, 7),
                        lines(t[0], 6, 7),
                    ],
                    axis=0,
                )
            )
        put_wide(pre_act, slice(None), side_by_side(y))

    expand_own()
    pl.semaphore_wait(reach.at[0], 8)
    greet(reach.at[1], around(2))

    def flip(bias, h):
        square = jnp.concatenate(
            [bias[pl.ds(h, LEN, stride=16), :], jnp.zeros((LEN, 128 - LEN), F32)], axis=1
        )
        square = jnp.concatenate([square, jnp.zeros((WPAD - LEN, 128), F32)], axis=0)
        turned = square.T[0:WPAD]
        key = lax.broadcasted_iota(jnp.int32, (WPAD, WPAD), 0)
        return jnp.where(key < LEN, turned, -1e30)

    def flip_all(bias, bias_t):
        for g in range(4):
            for h in range(2):
                pair = [flip(bias, 4 * g + 2 * h + n) for n in range(2)]
                bias_t[g, :, 128 * h : 128 * (h + 1)] = jnp.concatenate(pair, axis=1)

    l_bb.wait()
    flip_all(bbias, bias_b)
    l_gb.wait()
    flip_all(gbias, bias_g)

    branch, slope = gelu_of(wide(pre_act, slice(32, 256)))
    put_wide(slope_p, slice(32, 256), slope)
    l_wp.wait()
    put_wide(update, slice(None), dot(branch.astype(BF16), wp[...]))

    pl.semaphore_wait(reach.at[1], 8)
    greet(reach.at[2], around(4, cols=(0,)))

    for one in halo:
        one.wait_recv()
    has_n, has_s, has_w, has_e = (
        jnp.where(there, 1.0, 0.0) for there in (i > 0, i < ROWS - 1, j > 0, j < COLS - 1)
    )

    def inside(count, strip, column):
        at = lax.broadcasted_iota(jnp.int32, (count, 1), 0)
        slot = lax.bitwise_and(at, SW - 1)
        keep = jnp.where(slot < 2, has_w, 1.0) * jnp.where(slot < 30, 1.0, has_e)
        strips = jnp.where(at < strip, has_n, has_s) * keep
        columns = jnp.where(at < 2 * strip + column, has_w, has_e)
        return jnp.where(at < 2 * strip, strips, columns)

    xh = place("halo", cat[...]) * inside(160, 64, 16)
    normed1[...] = (standardize(xh)[0] * cgain_ref[...]).astype(BF16)
    e, _ = gelu_of(dot(normed1[...], we[...]))
    e = e.astype(BF16).astype(F32)
    n0, n1, s0, s1 = (lines(e, n, n + 1) for n in range(4))
    w0, w1, e0, e1 = (
        pltpu.roll(
            jnp.concatenate([e[128 + 8 * n : 136 + 8 * n], jnp.zeros((8, FF), F32)], axis=0), 2, 0
        )
        for n in range(4)
    )
    around = [
        (0, [n0 * w[b] + n1 * w[3 + b] for b in range(3)]),
        (32, [n1 * w[b] for b in range(3)]),
        (224, [s0 * w[6 + b] for b in range(3)]),
        (256, [s0 * w[3 + b] + s1 * w[6 + b] for b in range(3)]),
    ]
    for first, y in around:
        add_wide(pre_act, slice(first, first + SW), side_by_side(y))
    sides = [
        (1, [w0 * w[3 * a] + w1 * w[3 * a + 1] for a in range(3)]),
        (2, [w1 * w[3 * a] for a in range(3)]),
        (29, [e0 * w[3 * a + 2] for a in range(3)]),
        (30, [e0 * w[3 * a + 1] + e1 * w[3 * a + 2] for a in range(3)]),
    ]
    for slot, y in sides:
        y = y[0] + pltpu.roll(y[1], 15, 0) + pltpu.roll(y[2], 14, 0)
        add_wide(pre_act, column(slot, 9), y[0:9])

    kept = []
    for rows in [slice(0, 32), slice(32, 64), slice(224, 256), slice(256, 288)] + [
        column(SW + slot, 8) for slot in (1, 2, 29, 30)
    ]:
        branch, slope = gelu_of(wide(pre_act, rows))
        put_wide(slope_p, rows, slope)
        kept.append(branch)
    rim = jnp.concatenate([kept[1], kept[2], kept[5], kept[6]], axis=0).astype(BF16)

    def put_rim(ref, value):
        put_wide(ref, slice(0, 32), value[0:32])
        put_wide(ref, slice(192, 224), value[32:64])
        put_wide(ref, column(2, TR), value[64 : 64 + TR])
        put_wide(ref, column(29, TR), value[72 : 72 + TR])

    put_rim(update, dot(rim, wp[...]))
    mixed = (stage[...] + wide(update)).astype(BF16)
    zwin[...] = place("to_win", mixed)

    root = HEAD_DIM**-0.5

    def project_in(z, gain_ref, qkv, packed, xhat_ref, scale_ref):
        xhat, scale = standardize(z)
        xhat_ref[...] = xhat
        scale_ref[...] = scale
        normed = (xhat * gain_ref[...]).astype(BF16)
        for n in range(3):
            at = n * 512
            packed[:, at : at + 512] = dot(normed, qkv[:, at : at + 512]).astype(BF16)

    def parts_of(packed, rows, g):
        return [packed[rows, 512 * n + 128 * g : 512 * n + 128 * (g + 1)] for n in range(3)]

    def attend(packed, bias_t, prob):
        def window(w, carry):
            rows = pl.ds(pl.multiple_of(w * WPAD, WPAD), WPAD)
            for g in range(4):
                q, k, v = parts_of(packed, rows, g)
                s = dot_nt(k, by_head(q)) * root + bias_t[g]
                e = jnp.exp(s - jnp.max(s, axis=0, keepdims=True))
                prob[w, g] = e * (1.0 / jnp.sum(e, axis=0, keepdims=True))
            return carry

        lax.fori_loop(0, NWIN, window, 0, unroll=True)

        def gather(w, carry):
            rows = pl.ds(pl.multiple_of(w * WPAD, WPAD), WPAD)
            for g in range(4):
                v = parts_of(packed, rows, g)[2]
                one = own_head(dot_tn(prob[w, g].astype(BF16), v))
                att[rows, 128 * g : 128 * (g + 1)] = one.astype(BF16)
            return carry

        lax.fori_loop(0, NWIN, gather, 0, unroll=True)

    def attend_back(packed, prob):
        def window(w, carry):
            rows = pl.ds(pl.multiple_of(w * WPAD, WPAD), WPAD)
            for g in range(4):
                q, k, v = parts_of(packed, rows, g)
                p = prob[w, g]
                dam = by_head(da[rows, 128 * g : 128 * (g + 1)])
                dp = dot_nt(v, dam).astype(BF16).astype(F32)
                ds = p * (dp - jnp.sum(p * dp, axis=0, keepdims=True))
                ds = ds.astype(BF16)
                dscore[w, g] = ds
                dk = dot(ds, by_head(q)) * root
                dv = dot(p.astype(BF16), dam)
                for n, one in ((1, dk), (2, dv)):
                    dpk[rows, 512 * n + 128 * g : 512 * n + 128 * (g + 1)] = one.astype(BF16)
            return carry

        lax.fori_loop(0, NWIN, window, 0, unroll=True)

        def queries(w, carry):
            rows = pl.ds(pl.multiple_of(w * WPAD, WPAD), WPAD)
            for g in range(4):
                k = parts_of(packed, rows, g)[1]
                dq = own_head(dot_tn(dscore[w, g], k)) * root
                dpk[rows, 128 * g : 128 * (g + 1)] = dq.astype(BF16)
            return carry

        lax.fori_loop(0, NWIN, queries, 0, unroll=True)

    def project_back(qkv, gain_ref, xhat_ref, scale_ref):
        dn = dot_nt(dpk[...], qkv[...]).astype(BF16).astype(F32)
        dx = standardize_back(dn * gain_ref[...], xhat_ref[...], scale_ref[...])
        return (dout[...].astype(F32) + dx.astype(BF16).astype(F32)).astype(BF16)

    l_bqkv.wait()
    project_in(zwin[...], bgain_ref, bqkv, packed_b, xhat_b, scale_b)
    attend(packed_b, bias_b, prob_b)
    l_bout.wait()
    blocked = (zwin[...] + dot(att[...], bout[...])).astype(BF16)

    spatial = place("from_win", blocked)
    for k in range(4):
        mixbuf[pl.ds(k, 208, stride=4), :] = spatial[:, 128 * k : 128 * (k + 1)]
    fwd_send[...] = mixbuf[0:784, :].reshape(LEN, 16, 128).astype(BF16)
    pl.semaphore_wait(reach.at[2], 2)
    send_chunks(fwd_send, fwd_recv, grid_sem.at[1], True)
    send_chunks(cot_send, cot_recv, grid_sem.at[0], True)

    def to_windows(recv, target):
        mixbuf[0:784, :] = recv[...].astype(F32).reshape(784, 128)
        for w in range(NWIN):
            for k in range(4):
                target[WPAD * w : WPAD * w + LEN, 128 * k : 128 * (k + 1)] = mixbuf[
                    pl.ds(4 * w + k, LEN, stride=16), :
                ]

    def from_windows(source, send):
        for w in range(NWIN):
            for k in range(4):
                mixbuf[pl.ds(4 * w + k, LEN, stride=16), :] = source[
                    WPAD * w : WPAD * w + LEN, 128 * k : 128 * (k + 1)
                ]
        send[...] = mixbuf[0:784, :].reshape(LEN, 16, 128).astype(BF16)

    dgrid[...] = jnp.zeros_like(dgrid)
    zgrid[...] = jnp.zeros_like(zgrid)
    l_gqkv.wait()

    wait_chunks(fwd_recv, grid_sem.at[1])
    to_windows(fwd_recv, zgrid)
    project_in(zgrid[...], ggain_ref, gqkv, packed_g, xhat_g, scale_g)
    attend(packed_g, bias_g, prob_g)
    wait_chunks(cot_recv, grid_sem.at[0])
    to_windows(cot_recv, dgrid)
    dout[...] = dgrid[...].astype(BF16)
    l_gout.wait()
    da[...] = dot_nt(dout[...], gout[...]).astype(BF16)
    attend_back(packed_g, prob_g)
    dgrid[...] = project_back(gqkv, ggain_ref, xhat_g, scale_g).astype(F32)
    from_windows(dgrid, gra_send)
    send_chunks(gra_send, gra_recv, grid_sem.at[3], False)
    zgrid[...] = (zgrid[...] + dot(att[...], gout[...])).astype(BF16).astype(F32)
    from_windows(zgrid, res_send)
    send_chunks(res_send, res_recv, grid_sem.at[2], False)

    wait_chunks(gra_recv, grid_sem.at[3])
    mixbuf[0:784, :] = gra_recv[...].astype(F32).reshape(784, 128)
    mixbuf[784:832, :] = jnp.zeros((48, 128), F32)
    spatial = jnp.concatenate([mixbuf[pl.ds(k, 208, stride=4), :] for k in range(4)], axis=1)
    dout[...] = place("back_win", spatial.astype(BF16)).astype(BF16)
    da[...] = dot_nt(dout[...], bout[...]).astype(BF16)
    attend_back(packed_b, prob_b)
    slotted = place("slots", project_back(bqkv, bgain_ref, xhat_b, scale_b))
    stage[...] = slotted[0:224]
    own2[...] = slotted.astype(BF16)
    w_col2, e_col2 = own2.at[pl.ds(224, 16)], own2.at[pl.ds(240, 16)]
    halo2 = swap(
        halo2_sem,
        [
            (own2.at[pl.ds(0, 32)], cat2.at[pl.ds(32, 32)], (north, j)),
            (own2.at[pl.ds(192, 32)], cat2.at[pl.ds(0, 32)], (south, j)),
            (e_col2, cat2.at[pl.ds(64, 16)], (i, east)),
            (w_col2, cat2.at[pl.ds(80, 16)], (i, west)),
            (e_col2, cat2.at[pl.ds(96, 16)], (south, east)),
            (w_col2, cat2.at[pl.ds(112, 16)], (south, west)),
            (e_col2, cat2.at[pl.ds(128, 16)], (north, east)),
            (w_col2, cat2.at[pl.ds(144, 16)], (north, west)),
        ],
    )

    def back_own():
        gp = dot_nt(own2[0:224, :], wp[...]).astype(BF16).astype(F32)
        gp = gp * wide(slope_p, slice(32, 256))
        y = []
        for b in range(3):
            t = [gp * w[3 * a + 2 - b] for a in range(3)]
            y.append(
                jnp.concatenate(
                    [
                        lines(t[0], 1, 2) + lines(t[1], 0, 1),
                        lines(t[0], 2, 7) + lines(t[1], 1, 6) + lines(t[2], 0, 5),
                        lines(t[1], 6, 7) + lines(t[2], 5, 6),
                    ],
                    axis=0,
                )
            )
        put_wide(grad_e, slice(0, 224), side_by_side(y))

    def back_hidden(rows):
        return wide(grad_e, rows).astype(BF16).astype(F32) * wide(slope_u, rows)

    back_own()
    put_wide(update, slice(None), dot_nt(back_hidden(slice(0, 224)).astype(BF16), we[...]))
    wait_chunks(res_recv, grid_sem.at[2])
    out_ref[...] = res_recv[...]

    for one in halo2:
        one.wait_recv()
    gm = place("halo2", cat2[...]) * inside(80, 32, 8)
    halo_grad[...] = gm.astype(BF16)

    gp = dot_nt(halo_grad[...], wp[...]).astype(BF16).astype(F32)
    north_gp = gp[0:32] * wide(slope_p, slice(0, 32))
    south_gp = gp[32:64] * wide(slope_p, slice(256, 288))
    west_gp = gp[64:72] * wide(slope_p, column(SW + 1, 8))
    east_gp = gp[72:80] * wide(slope_p, column(SW + 30, 8))
    add_wide(grad_e, slice(0, 32), side_by_side([north_gp * w[8 - b] for b in range(3)]))
    add_wide(grad_e, slice(192, 224), side_by_side([south_gp * w[2 - b] for b in range(3)]))
    for slot, x, b in ((2, west_gp, 2), (29, east_gp, 0)):
        y = pltpu.roll(x * w[b], 7, 0) + x * w[3 + b] + pltpu.roll(x * w[6 + b], 1, 0)
        add_wide(grad_e, column(slot, TR), y[0:TR])
    rim = jnp.concatenate(
        [
            back_hidden(rows)
            for rows in (slice(0, 32), slice(192, 224), column(2, 8), column(29, 8))
        ],
        axis=0,
    ).astype(BF16)
    put_rim(update, dot_nt(rim, we[...]))
    dn = wide(update).astype(BF16).astype(F32)
    dx = standardize_back(dn * cgain_ref[...], xhat0[...], scale0[...])
    stage[...] = stage[...] + dx.astype(BF16).astype(F32)
    for r in range(TR):
        grad_ref[r] = stage[SW * r + 2 : SW * r + 2 + TC, :].astype(BF16)

    for one in halo + halo2:
        one.wait_send()
    for n, send in enumerate((cot_send, fwd_send, res_send, gra_send)):
        wait_sent(send, grid_sem.at[n])


def finish(chunks_ref, kept_ref, out_ref, grad_ref, mixbuf):
    mixbuf[...] = chunks_ref[...].astype(F32).reshape(784, 128)
    for r in range(TR):
        for k in range(4):
            out_ref[r, :, 128 * k : 128 * (k + 1)] = mixbuf[
                pl.ds(112 * r + k, TC, stride=4), :
            ].astype(BF16)
    grad_ref[...] = kept_ref[...]


def local(
    inputs, cotangent, conv_gain, expand_weight, depth_weight, project_weight,
    block_gain, block_qkv, block_out, block_bias, grid_gain, grid_qkv, grid_out, grid_bias,
):
    def by_query(bias):
        return bias.transpose(1, 0, 2).reshape(16 * LEN, LEN)

    vmem, hbm = pl.BlockSpec(memory_space=pltpu.VMEM), pl.BlockSpec(memory_space=pl.ANY)
    places = jnp.asarray(PLACES, BF16)
    chunks = pltpu.VMEM((LEN, 16, 128), BF16)
    tokens = jax.ShapeDtypeStruct((TR, TC, D), BF16)
    bias = pltpu.VMEM((16 * LEN, LEN), F32)
    bias_t = pltpu.VMEM((4, WPAD, 256), F32)
    win_f32, win_bf16 = pltpu.VMEM((256, D), F32), pltpu.VMEM((256, D), BF16)
    packed = pltpu.VMEM((256, 3 * D), BF16)
    scale = pltpu.VMEM((256, 1), F32)
    prob = pltpu.VMEM((NWIN, 4, WPAD, 256), F32)
    scratch = [
        pltpu.VMEM(PLACES.shape, BF16), pltpu.VMEM((D, FF), BF16), pltpu.VMEM((FF, D), BF16),
        pltpu.VMEM((D, 3 * D), BF16), pltpu.VMEM((D, D), BF16), bias,
        pltpu.VMEM((D, 3 * D), BF16), pltpu.VMEM((D, D), BF16), bias,
        pltpu.SemaphoreType.DMA((9,)), pltpu.SemaphoreType.REGULAR((3,)),
        pltpu.VMEM((224, D), F32), pltpu.VMEM((224, D), BF16), pltpu.VMEM((224, D), BF16),
        pltpu.VMEM((32, D), BF16), pltpu.VMEM((256, D), BF16), pltpu.VMEM((160, D), BF16),
        pltpu.SemaphoreType.DMA((2, 8)), pltpu.SemaphoreType.DMA((2, 8)),
        chunks, chunks, chunks, chunks, chunks, chunks, chunks, chunks,
        pltpu.SemaphoreType.DMA((4, 2)),
        pltpu.VMEM((832, 128), F32), pltpu.VMEM((224, D), F32), pltpu.VMEM((224, 1), F32),
        pltpu.VMEM((224, D), BF16), pltpu.VMEM((160, D), BF16),
        pltpu.VMEM((FF // 128, 256, 128), F32), pltpu.VMEM((FF // 128, 288, 128), F32),
        pltpu.VMEM((FF // 128, 288, 128), F32), pltpu.VMEM((D // 128, 224, 128), F32),
        bias_t, bias_t, win_f32, packed, win_f32, scale, prob, win_bf16,
        win_f32, win_f32, packed, win_f32, scale, prob, win_bf16, win_bf16, packed,
        pltpu.VMEM((NWIN, 4, WPAD, 256), BF16), pltpu.VMEM((80, D), BF16),
        pltpu.VMEM((FF // 128, 256, 128), F32),
    ]
    result, grad = pl.pallas_call(
        kernel,
        out_shape=(jax.ShapeDtypeStruct((LEN, 16, 128), BF16), tokens),
        in_specs=[vmem] * 6 + [hbm] * 9,
        out_specs=(vmem, vmem),
        scratch_shapes=scratch,
        compiler_params=pltpu.CompilerParams(
            collective_id=0, has_side_effects=True, vmem_limit_bytes=56 * 2**20
        ),
        name="mbconv_attention",
    )(
        inputs, cotangent, conv_gain.reshape(1, D), depth_weight, block_gain.reshape(1, D),
        grid_gain.reshape(1, D), places, expand_weight, project_weight, block_qkv, block_out,
        by_query(block_bias), grid_qkv, grid_out, by_query(grid_bias),
    )
    return pl.pallas_call(
        finish,
        out_shape=(tokens, tokens),
        in_specs=[vmem] * 2,
        out_specs=(vmem, vmem),
        scratch_shapes=[pltpu.VMEM((784, 128), F32)],
        name="finish",
    )(result, grad)


def solution(mesh):
    tokens = P("rows", "cols", None)
    in_specs = (tokens, tokens) + (P(),) * 12
    return jax.shard_map(
        local, mesh=mesh, in_specs=in_specs, out_specs=(tokens, tokens), check_vma=False
    )
```

```python
import functools

import jax
import jax.numpy as jnp
import numpy as np
from jax import lax
from jax.experimental import pallas as pl
from jax.experimental.pallas import tpu as pltpu
from jax.sharding import PartitionSpec as P

ROWS, COLS = 16, 8
HEIGHT, BREADTH = 112, 224
WIN = 7
D = 512
FF = 2048
HEAD_DIM = 32
TR, TC = 7, 28
SW = 32
NWIN, WPAD = 4, 64
LEN = 49
EPSILON = 1e-05
F32, BF16 = jnp.float32, jnp.bfloat16
MESH = pl.DeviceIdType.MESH


def win_row(row, col):
    return WPAD * (col // WIN) + WIN * row + col % WIN


def placements():
    edge = np.zeros((32, 256))
    slots = np.zeros((256, 256))
    to_win = np.zeros((256, 256))
    from_win = np.zeros((208, 256))
    back_win = np.zeros((256, 256))
    for r in range(TR):
        for c in range(2):
            edge[2 * r + c, SW * r + c + 2] = 1
            edge[16 + 2 * r + c, SW * r + c + 28] = 1
        for c in range(TC):
            to_win[win_row(r, c), SW * r + c + 2] = 1
            slots[SW * r + c + 2, win_row(r, c)] = 1
            from_win[TC * r + c, win_row(r, c)] = 1
            back_win[win_row(r, c), TC * r + c] = 1
        slots[224 + r, win_row(r, 0)] = 1
        slots[240 + r, win_row(r, 27)] = 1
    halo = np.zeros((160, 256))
    for line in range(2):
        for c in range(TC):
            for half in range(2):
                at = 64 * half + SW * line + c + 2
                halo[at, at] = 1
        for c in range(2):
            for half in range(2):
                for side in range(2):
                    at = 64 * half + SW * line + (30 * side + c)
                    row = line + (0 if half else 5)
                    halo[at, 128 + 16 * (2 + 2 * half + side) + 2 * row + c] = 1
    for r in range(TR):
        for c in range(2):
            for side in range(2):
                halo[128 + 8 * (2 * side + c) + r, 128 + 16 * side + 2 * r + c] = 1
    halo2 = np.zeros((96, 256))
    for half in range(2):
        for c in range(TC):
            halo2[32 * half + c + 2, 32 * half + c + 2] = 1
        for side in range(2):
            row = 0 if half else 6
            halo2[32 * half + 1 + 29 * side, 64 + 16 * (2 + 2 * half + side) + row] = 1
    for r in range(TR):
        for side in range(2):
            halo2[64 + 16 * side + r + 1, 64 + 16 * side + r] = 1
    parts = dict(
        edge=edge, halo=halo, to_win=to_win, from_win=from_win, back_win=back_win,
        slots=slots, halo2=halo2,
    )
    starts, at = {}, 0
    for name, part in parts.items():
        starts[name] = (at, part.shape[0])
        at += part.shape[0]
    return np.concatenate(list(parts.values())), starts


PLACES, STARTS = placements()


def dot(a, b):
    return jnp.dot(a, b, preferred_element_type=F32)


def dot_nt(a, b):
    return lax.dot_general(a, b, (((1,), (1,)), ((), ())), preferred_element_type=F32)


def dot_tn(a, b):
    return lax.dot_general(a, b, (((0,), (0,)), ((), ())), preferred_element_type=F32)


def gelu_of(u):
    share = 0.5 + 0.5 * lax.erf(u * 0.5**0.5)
    density = jnp.exp2((-0.5 / np.log(2.0)) * (u * u))
    return u * share, share + (u * (0.5 / np.pi) ** 0.5) * density


def standardize(x):
    center = jnp.mean(x, axis=-1, keepdims=True)
    moved = x - center
    spread = jnp.mean(moved * moved, axis=-1, keepdims=True)
    scale = lax.rsqrt(spread + EPSILON)
    return moved * scale, scale


def standardize_back(grad, xhat, scale):
    first = jnp.mean(grad, axis=-1, keepdims=True)
    second = jnp.mean(grad * xhat, axis=-1, keepdims=True)
    return scale * (grad - first - xhat * second)


def by_head(x):
    head = lax.broadcasted_iota(jnp.int32, x.shape, 1) // HEAD_DIM
    zero = jnp.zeros_like(x)
    return jnp.concatenate([jnp.where(head == h, x, zero) for h in range(4)], axis=0)


def own_head(x):
    head = lax.broadcasted_iota(jnp.int32, (WPAD, 128), 1) // HEAD_DIM
    out = x[0:WPAD]
    for h in range(1, 4):
        out = jnp.where(head == h, x[WPAD * h : WPAD * (h + 1)], out)
    return out


def kernel(
    x_ref, cot_ref, cgain_ref, dw_ref, bgain_ref, ggain_ref,
    places_hbm, we_hbm, wp_hbm, bqkv_hbm, bout_hbm, bbias_hbm, gqkv_hbm, gout_hbm, gbias_hbm,
    out_ref, grad_ref,
    places, we, wp, bqkv, bout, bbias, gqkv, gout, gbias, load_sem, reach,
    stage, own, cat, edges, own2, cat2, halo_sem, halo2_sem,
    cot_send, cot_recv, fwd_send, fwd_recv, res_send, res_recv, gra_send, gra_recv, grid_sem,
    mixbuf, xhat0, scale0, normed0, normed1, slope_u, slope_p, pre_act, update,
    bias_b, bias_g, zwin, packed_b, xhat_b, scale_b, prob_b, att,
    zgrid, dgrid, packed_g, xhat_g, scale_g, prob_g, dout, da, dpk, dscore, halo_grad, grad_e,
    cols_pre, cols_slope, cols_u, cols_e, halo_e,
):
    i, j = lax.axis_index("rows"), lax.axis_index("cols")
    me = i * COLS + j

    def load(index, src, dst):
        return pltpu.make_async_copy(src, dst, load_sem.at[index])

    loads = [
        load(n, src, dst)
        for n, (src, dst) in enumerate(
            [
                (places_hbm, places), (we_hbm, we), (wp_hbm, wp), (bbias_hbm, bbias),
                (gbias_hbm, gbias), (bqkv_hbm, bqkv), (bout_hbm, bout),
                (gout_hbm, gout), (gqkv_hbm, gqkv),
            ]
        )
    ]
    for one in loads:
        one.start()
    l_places, l_we, l_wp, l_bb, l_gb, l_bqkv, l_bout, l_gout, l_gqkv = loads

    def around(step, rows=(-1, 0, 1), cols=(-1, 0, 1)):
        for a in rows:
            for b in cols:
                if a or b:
                    yield lax.rem(i + ROWS + step * a, ROWS), lax.rem(j + COLS + step * b, COLS)

    def greet(sem, devices):
        for device in devices:
            pl.semaphore_signal(sem, inc=1, device_id=device, device_id_type=MESH)

    barrier = pltpu.get_barrier_semaphore()
    greet(barrier, around(1))

    def place(name, source):
        at, size = STARTS[name]
        return dot(places[at : at + size, 0 : source.shape[0]], source)

    stage[...] = jnp.zeros_like(stage)
    for r in range(TR):
        stage[SW * r + 2 : SW * r + 2 + TC, :] = x_ref[r].astype(F32)
    own[...] = stage[...].astype(BF16)
    l_places.wait()
    edges[...] = place("edge", own[...]).astype(BF16)

    mixbuf[...] = jnp.zeros_like(mixbuf)
    for r in range(TR):
        for k in range(4):
            mixbuf[pl.ds(112 * r + k, TC, stride=4), :] = cot_ref[
                r, :, 128 * k : 128 * (k + 1)
            ].astype(F32)
    cot_send[...] = mixbuf[0:784, :].reshape(LEN, 16, 128).astype(BF16)

    pl.semaphore_wait(barrier, 8)

    north, south = lax.rem(i + ROWS - 1, ROWS), lax.rem(i + 1, ROWS)
    west, east = lax.rem(j + COLS - 1, COLS), lax.rem(j + 1, COLS)

    def swap(sems, parts):
        copies = [
            pltpu.make_async_remote_copy(
                src_ref=src, dst_ref=dst, send_sem=sems.at[0, n], recv_sem=sems.at[1, n],
                device_id=to, device_id_type=MESH,
            )
            for n, (src, dst, to) in enumerate(parts)
        ]
        for one in copies:
            one.start()
        return copies

    w_cols, e_cols = edges.at[pl.ds(0, 16)], edges.at[pl.ds(16, 16)]
    halo = swap(
        halo_sem,
        [
            (own.at[pl.ds(0, 64)], cat.at[pl.ds(64, 64)], (north, j)),
            (own.at[pl.ds(160, 64)], cat.at[pl.ds(0, 64)], (south, j)),
            (e_cols, cat.at[pl.ds(128, 16)], (i, east)),
            (w_cols, cat.at[pl.ds(144, 16)], (i, west)),
            (e_cols, cat.at[pl.ds(160, 16)], (south, east)),
            (w_cols, cat.at[pl.ds(176, 16)], (south, west)),
            (e_cols, cat.at[pl.ds(192, 16)], (north, east)),
            (w_cols, cat.at[pl.ds(208, 16)], (north, west)),
        ],
    )

    def send_chunks(send, recv, sems, forward):
        def body(c, carry):
            a, b = lax.div(c, WIN), lax.rem(c, WIN)
            if forward:
                row, col = WIN * i + a, WIN * j + b
                ti, tj = lax.rem(row, ROWS), lax.rem(col, COLS)
                slot = lax.div(row, ROWS) * WIN + lax.div(col, COLS)
            else:
                row, col = ROWS * a + i, COLS * b + j
                ti, tj = lax.div(row, WIN), lax.div(col, WIN)
                slot = lax.rem(row, WIN) * WIN + lax.rem(col, WIN)
            mine = jnp.logical_and(ti == i, tj == j)

            @pl.when(mine)
            def _():
                pltpu.make_async_copy(send.at[c], recv.at[slot], sems.at[1]).start()

            @pl.when(jnp.logical_not(mine))
            def _():
                pltpu.make_async_remote_copy(
                    src_ref=send.at[c], dst_ref=recv.at[slot], send_sem=sems.at[0],
                    recv_sem=sems.at[1], device_id=(ti, tj), device_id_type=MESH,
                ).start()

            return carry

        lax.fori_loop(0, LEN, body, 0)

    def wait_chunks(recv, sems):
        pltpu.make_async_copy(recv, recv, sems.at[1]).wait()

    def wait_sent(send, sems):
        some = lax.rem(10 * i, ROWS) < WIN

        @pl.when(some)
        def _():
            part = send.at[pl.ds(0, LEN - 1)]
            pltpu.make_async_copy(part, part, sems.at[0]).wait()

        @pl.when(jnp.logical_not(some))
        def _():
            pltpu.make_async_copy(send, send, sems.at[0]).wait()

    greet(reach.at[0], around(1))

    xhat, scale = standardize(stage[...])
    xhat0[...] = xhat
    scale0[...] = scale
    normed0[...] = (xhat * cgain_ref[...]).astype(BF16)
    l_we.wait()

    w = [dw_ref[n : n + 1, :] for n in range(9)]

    def wide(ref, rows=slice(None)):
        return jnp.concatenate([ref[n, rows, :] for n in range(ref.shape[0])], axis=1)

    def put_wide(ref, rows, value):
        for n in range(ref.shape[0]):
            ref[n, rows, :] = value[:, 128 * n : 128 * (n + 1)]

    def column(first, count):
        return pl.ds(first, count, stride=SW)

    def beside(strip, ends):
        at = lax.broadcasted_iota(jnp.int32, (8, 1), 0)
        first, last = strip[0:8], strip[24:32]
        for slot, row in ends:
            if slot < 8:
                first += jnp.where(at == slot, 1.0, 0.0) * row
            else:
                last += jnp.where(at == slot - 24, 1.0, 0.0) * row
        return jnp.concatenate([first, strip[8:24], last], axis=0)

    def lines(x, first, last):
        return x[SW * first : SW * last]

    def side_by_side(y):
        count = y[0].shape[0]
        return pltpu.roll(y[0], 1, 0) + y[1] + pltpu.roll(y[2], count - 1, 0)

    def expand_own():
        e, slope = gelu_of(dot(normed0[...], we[...]))
        put_wide(slope_u, slice(0, 224), slope)
        e = e.astype(BF16).astype(F32)
        y = []
        for b in range(3):
            t = [e * w[3 * a + b] for a in range(3)]
            y.append(
                jnp.concatenate(
                    [
                        lines(t[2], 0, 1),
                        lines(t[1], 0, 1) + lines(t[2], 1, 2),
                        lines(t[0], 0, 5) + lines(t[1], 1, 6) + lines(t[2], 2, 7),
                        lines(t[0], 5, 6) + lines(t[1], 6, 7),
                        lines(t[0], 6, 7),
                    ],
                    axis=0,
                )
            )
        put_wide(pre_act, slice(None), side_by_side(y))

    expand_own()
    pl.semaphore_wait(reach.at[0], 8)
    greet(reach.at[1], around(2))

    def flip(bias, h):
        square = jnp.concatenate(
            [bias[pl.ds(h, LEN, stride=16), :], jnp.zeros((LEN, 128 - LEN), F32)], axis=1
        )
        square = jnp.concatenate([square, jnp.zeros((WPAD - LEN, 128), F32)], axis=0)
        turned = square.T[0:WPAD]
        key = lax.broadcasted_iota(jnp.int32, (WPAD, WPAD), 0)
        return jnp.where(key < LEN, turned, -1e30)

    def flip_all(bias, bias_t):
        for g in range(4):
            for h in range(2):
                pair = [flip(bias, 4 * g + 2 * h + n) for n in range(2)]
                bias_t[g, :, 128 * h : 128 * (h + 1)] = jnp.concatenate(pair, axis=1)

    l_bb.wait()
    flip_all(bbias, bias_b)
    l_gb.wait()
    flip_all(gbias, bias_g)

    branch, slope = gelu_of(wide(pre_act, slice(32, 256)))
    put_wide(slope_p, slice(32, 256), slope)
    l_wp.wait()
    put_wide(update, slice(None), dot(branch.astype(BF16), wp[...]))

    pl.semaphore_wait(reach.at[1], 8)
    greet(reach.at[2], around(4, cols=(0,)))

    cols_pre[...] = jnp.zeros_like(cols_pre)
    for n, slot in enumerate((1, 2, 29, 30)):
        cols_pre[n, 0:9, :] = wide(pre_act, column(slot, 9))

    for one in halo:
        one.wait_recv()
    has_n, has_s, has_w, has_e = (
        jnp.where(there, 1.0, 0.0) for there in (i > 0, i < ROWS - 1, j > 0, j < COLS - 1)
    )

    def inside(count, strip, column):
        at = lax.broadcasted_iota(jnp.int32, (count, 1), 0)
        slot = lax.bitwise_and(at, SW - 1)
        keep = jnp.where(slot < 2, has_w, 1.0) * jnp.where(slot < 30, 1.0, has_e)
        strips = jnp.where(at < strip, has_n, has_s) * keep
        columns = jnp.where(at < 2 * strip + column, has_w, has_e)
        return jnp.where(at < 2 * strip, strips, columns)

    xh = place("halo", cat[...]) * inside(160, 64, 16)
    normed1[...] = (standardize(xh)[0] * cgain_ref[...]).astype(BF16)
    e, _ = gelu_of(dot(normed1[...], we[...]))
    e = e.astype(BF16).astype(F32)
    halo_e[...] = e

    def side(n):
        x = halo_e[128 + 8 * n : 136 + 8 * n, :]
        return pltpu.roll(jnp.concatenate([x, jnp.zeros((8, FF), F32)], axis=0), 2, 0)

    def downwards(terms):
        return terms[0] + pltpu.roll(terms[1], 15, 0) + pltpu.roll(terms[2], 14, 0)

    def strip(line, y, ends):
        ends = [(slot, x[line : line + 1]) for slot, x in ends]
        rows = slice(SW * line, SW * (line + 1))
        return wide(pre_act, rows) + beside(side_by_side(y), ends)

    left = downwards([side(1) * w[3 * a] for a in range(3)])
    right = downwards([side(2) * w[3 * a + 2] for a in range(3)])
    ends = [(2, left), (29, right)]
    rim = [
        strip(1, [lines(e, 1, 2) * w[b] for b in range(3)], ends),
        strip(7, [lines(e, 2, 3) * w[6 + b] for b in range(3)], ends),
        cols_pre[1] + left,
        cols_pre[2] + right,
    ]
    rim = jnp.concatenate([gelu_of(x)[0] for x in rim], axis=0).astype(BF16)

    def halo_slopes():
        n0, n1, s0, s1 = (halo_e[SW * n : SW * (n + 1), :] for n in range(4))
        w0, w1, e0, e1 = (side(n) for n in range(4))
        sides = [
            downwards([w0 * w[3 * a] + w1 * w[3 * a + 1] for a in range(3)]),
            downwards([w1 * w[3 * a] for a in range(3)]),
            downwards([e0 * w[3 * a + 2] for a in range(3)]),
            downwards([e0 * w[3 * a + 1] + e1 * w[3 * a + 2] for a in range(3)]),
        ]
        ends = list(zip((1, 2, 29, 30), sides))
        for line, y in (
            (0, [n0 * w[b] + n1 * w[3 + b] for b in range(3)]),
            (1, [n1 * w[b] for b in range(3)]),
            (7, [s0 * w[6 + b] for b in range(3)]),
            (8, [s0 * w[3 + b] + s1 * w[6 + b] for b in range(3)]),
        ):
            slope = gelu_of(strip(line, y, ends))[1]
            put_wide(slope_p, slice(SW * line, SW * (line + 1)), slope)
        for n, x in enumerate(sides):
            cols_slope[n] = gelu_of(cols_pre[n] + x)[1]
        for n, slot in enumerate((1, 2, 29, 30)):
            put_wide(slope_p, column(2 * SW + slot, 5), cols_slope[n, 2:7, :])
        for n, slot in ((0, 1), (3, 30)):
            cols_slope[n, 1:8, :] = wide(slope_p, column(SW + slot, TR))

    def put_rim(ref, value, first):
        put_wide(ref, column(2, TR), value[64 + first : 64 + first + TR])
        put_wide(ref, column(29, TR), value[80 + first : 80 + first + TR])
        put_wide(ref, slice(0, 32), value[0:32])
        put_wide(ref, slice(192, 224), value[32:64])

    put_rim(update, dot(rim, wp[...]), 1)
    mixed = (stage[...] + wide(update)).astype(BF16)
    zwin[...] = place("to_win", mixed)

    root = HEAD_DIM**-0.5

    def project_in(z, gain_ref, qkv, packed, xhat_ref, scale_ref):
        xhat, scale = standardize(z)
        xhat_ref[...] = xhat
        scale_ref[...] = scale
        normed = (xhat * gain_ref[...]).astype(BF16)
        for n in range(3):
            at = n * 512
            packed[:, at : at + 512] = dot(normed, qkv[:, at : at + 512]).astype(BF16)

    def parts_of(packed, rows, g):
        return [packed[rows, 512 * n + 128 * g : 512 * n + 128 * (g + 1)] for n in range(3)]

    def attend(packed, bias_t, prob):
        def window(w, carry):
            rows = pl.ds(pl.multiple_of(w * WPAD, WPAD), WPAD)
            for g in range(4):
                q, k, v = parts_of(packed, rows, g)
                s = dot_nt(k, by_head(q)) * root + bias_t[g]
                e = jnp.exp(s - jnp.max(s, axis=0, keepdims=True))
                prob[w, g] = e * (1.0 / jnp.sum(e, axis=0, keepdims=True))
            return carry

        lax.fori_loop(0, NWIN, window, 0, unroll=True)

        def gather(w, carry):
            rows = pl.ds(pl.multiple_of(w * WPAD, WPAD), WPAD)
            for g in range(4):
                v = parts_of(packed, rows, g)[2]
                one = own_head(dot_tn(prob[w, g].astype(BF16), v))
                att[rows, 128 * g : 128 * (g + 1)] = one.astype(BF16)
            return carry

        lax.fori_loop(0, NWIN, gather, 0, unroll=True)

    def attend_back(packed, prob):
        def window(w, carry):
            rows = pl.ds(pl.multiple_of(w * WPAD, WPAD), WPAD)
            for g in range(4):
                q, k, v = parts_of(packed, rows, g)
                p = prob[w, g]
                dam = by_head(da[rows, 128 * g : 128 * (g + 1)])
                dp = dot_nt(v, dam).astype(BF16).astype(F32)
                ds = p * (dp - jnp.sum(p * dp, axis=0, keepdims=True))
                ds = ds.astype(BF16)
                dscore[w, g] = ds
                dk = dot(ds, by_head(q)) * root
                dv = dot(p.astype(BF16), dam)
                for n, one in ((1, dk), (2, dv)):
                    dpk[rows, 512 * n + 128 * g : 512 * n + 128 * (g + 1)] = one.astype(BF16)
            return carry

        lax.fori_loop(0, NWIN, window, 0, unroll=True)

        def queries(w, carry):
            rows = pl.ds(pl.multiple_of(w * WPAD, WPAD), WPAD)
            for g in range(4):
                k = parts_of(packed, rows, g)[1]
                dq = own_head(dot_tn(dscore[w, g], k)) * root
                dpk[rows, 128 * g : 128 * (g + 1)] = dq.astype(BF16)
            return carry

        lax.fori_loop(0, NWIN, queries, 0, unroll=True)

    def project_back(qkv, gain_ref, xhat_ref, scale_ref):
        dn = dot_nt(dpk[...], qkv[...]).astype(BF16).astype(F32)
        dx = standardize_back(dn * gain_ref[...], xhat_ref[...], scale_ref[...])
        return (dout[...].astype(F32) + dx.astype(BF16).astype(F32)).astype(BF16)

    l_bqkv.wait()
    project_in(zwin[...], bgain_ref, bqkv, packed_b, xhat_b, scale_b)
    attend(packed_b, bias_b, prob_b)
    l_bout.wait()
    blocked = (zwin[...] + dot(att[...], bout[...])).astype(BF16)

    spatial = place("from_win", blocked)
    for k in range(4):
        mixbuf[pl.ds(k, 208, stride=4), :] = spatial[:, 128 * k : 128 * (k + 1)]
    fwd_send[...] = mixbuf[0:784, :].reshape(LEN, 16, 128).astype(BF16)
    pl.semaphore_wait(reach.at[2], 2)
    send_chunks(fwd_send, fwd_recv, grid_sem.at[1], True)
    send_chunks(cot_send, cot_recv, grid_sem.at[0], True)

    halo_slopes()
    cols_u[...] = jnp.zeros_like(cols_u)
    cols_e[...] = jnp.zeros_like(cols_e)
    for n, slot in enumerate((2, 29)):
        cols_u[n, 0:TR, :] = wide(slope_u, column(slot, TR))

    def to_windows(recv, target):
        mixbuf[0:784, :] = recv[...].astype(F32).reshape(784, 128)
        for w in range(NWIN):
            for k in range(4):
                target[WPAD * w : WPAD * w + LEN, 128 * k : 128 * (k + 1)] = mixbuf[
                    pl.ds(4 * w + k, LEN, stride=16), :
                ]

    def from_windows(source, send):
        for w in range(NWIN):
            for k in range(4):
                mixbuf[pl.ds(4 * w + k, LEN, stride=16), :] = source[
                    WPAD * w : WPAD * w + LEN, 128 * k : 128 * (k + 1)
                ]
        send[...] = mixbuf[0:784, :].reshape(LEN, 16, 128).astype(BF16)

    dgrid[...] = jnp.zeros_like(dgrid)
    zgrid[...] = jnp.zeros_like(zgrid)
    l_gqkv.wait()

    wait_chunks(fwd_recv, grid_sem.at[1])
    to_windows(fwd_recv, zgrid)
    project_in(zgrid[...], ggain_ref, gqkv, packed_g, xhat_g, scale_g)
    attend(packed_g, bias_g, prob_g)
    wait_chunks(cot_recv, grid_sem.at[0])
    to_windows(cot_recv, dgrid)
    dout[...] = dgrid[...].astype(BF16)
    l_gout.wait()
    da[...] = dot_nt(dout[...], gout[...]).astype(BF16)
    attend_back(packed_g, prob_g)
    dgrid[...] = project_back(gqkv, ggain_ref, xhat_g, scale_g).astype(F32)
    from_windows(dgrid, gra_send)
    send_chunks(gra_send, gra_recv, grid_sem.at[3], False)
    zgrid[...] = (zgrid[...] + dot(att[...], gout[...])).astype(BF16).astype(F32)
    from_windows(zgrid, res_send)
    send_chunks(res_send, res_recv, grid_sem.at[2], False)

    wait_chunks(gra_recv, grid_sem.at[3])
    mixbuf[0:784, :] = gra_recv[...].astype(F32).reshape(784, 128)
    mixbuf[784:832, :] = jnp.zeros((48, 128), F32)
    spatial = jnp.concatenate([mixbuf[pl.ds(k, 208, stride=4), :] for k in range(4)], axis=1)
    dout[...] = place("back_win", spatial.astype(BF16)).astype(BF16)
    da[...] = dot_nt(dout[...], bout[...]).astype(BF16)
    attend_back(packed_b, prob_b)
    slotted = place("slots", project_back(bqkv, bgain_ref, xhat_b, scale_b))
    stage[...] = slotted[0:224]
    own2[...] = slotted.astype(BF16)
    w_col2, e_col2 = own2.at[pl.ds(224, 16)], own2.at[pl.ds(240, 16)]
    halo2 = swap(
        halo2_sem,
        [
            (own2.at[pl.ds(0, 32)], cat2.at[pl.ds(32, 32)], (north, j)),
            (own2.at[pl.ds(192, 32)], cat2.at[pl.ds(0, 32)], (south, j)),
            (e_col2, cat2.at[pl.ds(64, 16)], (i, east)),
            (w_col2, cat2.at[pl.ds(80, 16)], (i, west)),
            (e_col2, cat2.at[pl.ds(96, 16)], (south, east)),
            (w_col2, cat2.at[pl.ds(112, 16)], (south, west)),
            (e_col2, cat2.at[pl.ds(128, 16)], (north, east)),
            (w_col2, cat2.at[pl.ds(144, 16)], (north, west)),
        ],
    )

    def back_own():
        gp = dot_nt(own2[0:224, :], wp[...]).astype(BF16).astype(F32)
        gp = gp * wide(slope_p, slice(32, 256))
        y = []
        for b in range(3):
            t = [gp * w[3 * a + 2 - b] for a in range(3)]
            y.append(
                jnp.concatenate(
                    [
                        lines(t[0], 1, 2) + lines(t[1], 0, 1),
                        lines(t[0], 2, 7) + lines(t[1], 1, 6) + lines(t[2], 0, 5),
                        lines(t[1], 6, 7) + lines(t[2], 5, 6),
                    ],
                    axis=0,
                )
            )
        put_wide(grad_e, slice(0, 224), side_by_side(y))

    def back_hidden(rows):
        return wide(grad_e, rows).astype(BF16).astype(F32) * wide(slope_u, rows)

    back_own()
    for n, slot in enumerate((2, 29)):
        cols_e[n, 0:TR, :] = wide(grad_e, column(slot, TR))
    put_wide(update, slice(None), dot_nt(back_hidden(slice(0, 224)).astype(BF16), we[...]))
    wait_chunks(res_recv, grid_sem.at[2])
    out_ref[...] = res_recv[...]

    for one in halo2:
        one.wait_recv()
    gm = place("halo2", cat2[...]) * inside(96, 32, 16)
    halo_grad[...] = gm.astype(BF16)

    gp = dot_nt(halo_grad[...], wp[...]).astype(BF16).astype(F32)
    north_gp = gp[0:32] * wide(slope_p, slice(0, 32))
    south_gp = gp[32:64] * wide(slope_p, slice(256, 288))
    sides = []
    for x, b in ((gp[64:80] * cols_slope[0], 2), (gp[80:96] * cols_slope[3], 0)):
        sides.append(
            pltpu.roll(x * w[b], 14, 0) + pltpu.roll(x * w[3 + b], 15, 0) + x * w[6 + b]
        )

    def hidden(grad, slope):
        return grad.astype(BF16).astype(F32) * slope

    rim = []
    for line, y in (
        (0, [north_gp * w[8 - b] for b in range(3)]),
        (6, [south_gp * w[2 - b] for b in range(3)]),
    ):
        rows = slice(SW * line, SW * (line + 1))
        ends = [(slot, x[line : line + 1]) for slot, x in zip((2, 29), sides)]
        rim.append(
            hidden(wide(grad_e, rows) + beside(side_by_side(y), ends), wide(slope_u, rows))
        )
    for n, x in enumerate(sides):
        rim.append(hidden(cols_e[n] + x, cols_u[n]))
    rim = jnp.concatenate(rim, axis=0).astype(BF16)
    put_rim(update, dot_nt(rim, we[...]), 0)
    dn = wide(update).astype(BF16).astype(F32)
    dx = standardize_back(dn * cgain_ref[...], xhat0[...], scale0[...])
    stage[...] = stage[...] + dx.astype(BF16).astype(F32)
    for r in range(TR):
        grad_ref[r] = stage[SW * r + 2 : SW * r + 2 + TC, :].astype(BF16)

    for one in halo + halo2:
        one.wait_send()
    for n, send in enumerate((cot_send, fwd_send, res_send, gra_send)):
        wait_sent(send, grid_sem.at[n])


def finish(chunks_ref, kept_ref, out_ref, grad_ref, mixbuf):
    mixbuf[...] = chunks_ref[...].astype(F32).reshape(784, 128)
    for r in range(TR):
        for k in range(4):
            out_ref[r, :, 128 * k : 128 * (k + 1)] = mixbuf[
                pl.ds(112 * r + k, TC, stride=4), :
            ].astype(BF16)
    grad_ref[...] = kept_ref[...]


def local(
    inputs, cotangent, conv_gain, expand_weight, depth_weight, project_weight,
    block_gain, block_qkv, block_out, block_bias, grid_gain, grid_qkv, grid_out, grid_bias,
):
    def by_query(bias):
        return bias.transpose(1, 0, 2).reshape(16 * LEN, LEN)

    vmem, hbm = pl.BlockSpec(memory_space=pltpu.VMEM), pl.BlockSpec(memory_space=pl.ANY)
    places = jnp.asarray(PLACES, BF16)
    chunks = pltpu.VMEM((LEN, 16, 128), BF16)
    tokens = jax.ShapeDtypeStruct((TR, TC, D), BF16)
    bias = pltpu.VMEM((16 * LEN, LEN), F32)
    bias_t = pltpu.VMEM((4, WPAD, 256), F32)
    win_f32, win_bf16 = pltpu.VMEM((256, D), F32), pltpu.VMEM((256, D), BF16)
    packed = pltpu.VMEM((256, 3 * D), BF16)
    scale = pltpu.VMEM((256, 1), F32)
    prob = pltpu.VMEM((NWIN, 4, WPAD, 256), F32)
    scratch = [
        pltpu.VMEM(PLACES.shape, BF16), pltpu.VMEM((D, FF), BF16), pltpu.VMEM((FF, D), BF16),
        pltpu.VMEM((D, 3 * D), BF16), pltpu.VMEM((D, D), BF16), bias,
        pltpu.VMEM((D, 3 * D), BF16), pltpu.VMEM((D, D), BF16), bias,
        pltpu.SemaphoreType.DMA((9,)), pltpu.SemaphoreType.REGULAR((3,)),
        pltpu.VMEM((224, D), F32), pltpu.VMEM((224, D), BF16), pltpu.VMEM((224, D), BF16),
        pltpu.VMEM((32, D), BF16), pltpu.VMEM((256, D), BF16), pltpu.VMEM((160, D), BF16),
        pltpu.SemaphoreType.DMA((2, 8)), pltpu.SemaphoreType.DMA((2, 8)),
        chunks, chunks, chunks, chunks, chunks, chunks, chunks, chunks,
        pltpu.SemaphoreType.DMA((4, 2)),
        pltpu.VMEM((832, 128), F32), pltpu.VMEM((224, D), F32), pltpu.VMEM((224, 1), F32),
        pltpu.VMEM((224, D), BF16), pltpu.VMEM((160, D), BF16),
        pltpu.VMEM((FF // 128, 256, 128), F32), pltpu.VMEM((FF // 128, 288, 128), F32),
        pltpu.VMEM((FF // 128, 288, 128), F32), pltpu.VMEM((D // 128, 224, 128), F32),
        bias_t, bias_t, win_f32, packed, win_f32, scale, prob, win_bf16,
        win_f32, win_f32, packed, win_f32, scale, prob, win_bf16, win_bf16, packed,
        pltpu.VMEM((NWIN, 4, WPAD, 256), BF16), pltpu.VMEM((96, D), BF16),
        pltpu.VMEM((FF // 128, 256, 128), F32),
        pltpu.VMEM((4, 16, FF), F32), pltpu.VMEM((4, 16, FF), F32),
        pltpu.VMEM((2, 16, FF), F32), pltpu.VMEM((2, 16, FF), F32), pltpu.VMEM((160, FF), F32),
    ]
    result, grad = pl.pallas_call(
        kernel,
        out_shape=(jax.ShapeDtypeStruct((LEN, 16, 128), BF16), tokens),
        in_specs=[vmem] * 6 + [hbm] * 9,
        out_specs=(vmem, vmem),
        scratch_shapes=scratch,
        compiler_params=pltpu.CompilerParams(
            collective_id=0, has_side_effects=True, vmem_limit_bytes=56 * 2**20
        ),
        name="mbconv_attention",
    )(
        inputs, cotangent, conv_gain.reshape(1, D), depth_weight, block_gain.reshape(1, D),
        grid_gain.reshape(1, D), places, expand_weight, project_weight, block_qkv, block_out,
        by_query(block_bias), grid_qkv, grid_out, by_query(grid_bias),
    )
    return pl.pallas_call(
        finish,
        out_shape=(tokens, tokens),
        in_specs=[vmem] * 2,
        out_specs=(vmem, vmem),
        scratch_shapes=[pltpu.VMEM((784, 128), F32)],
        name="finish",
    )(result, grad)


def solution(mesh):
    tokens = P("rows", "cols", None)
    in_specs = (tokens, tokens) + (P(),) * 12
    return jax.shard_map(
        local, mesh=mesh, in_specs=in_specs, out_specs=(tokens, tokens), check_vma=False
    )
```

```python
import functools

import jax
import jax.numpy as jnp
import numpy as np
from jax import lax
from jax.experimental import pallas as pl
from jax.experimental.pallas import tpu as pltpu
from jax.sharding import PartitionSpec as P

ROWS, COLS = 16, 8
HEIGHT, BREADTH = 112, 224
WIN = 7
D = 512
FF = 2048
HEAD_DIM = 32
TR, TC = 7, 28
SW = 32
NWIN, WPAD = 4, 64
LEN = 49
EPSILON = 1e-05
F32, BF16 = jnp.float32, jnp.bfloat16
MESH = pl.DeviceIdType.MESH


def win_row(row, col):
    return WPAD * (col // WIN) + WIN * row + col % WIN


def placements():
    slots = np.zeros((256, 256))
    to_win = np.zeros((256, 256))
    from_win = np.zeros((208, 256))
    back_win = np.zeros((256, 256))
    for r in range(TR):
        for c in range(TC):
            to_win[win_row(r, c), SW * r + c + 2] = 1
            slots[SW * r + c + 2, win_row(r, c)] = 1
            from_win[TC * r + c, win_row(r, c)] = 1
            back_win[win_row(r, c), TC * r + c] = 1
        slots[224 + r, win_row(r, 0)] = 1
        slots[240 + r, win_row(r, 27)] = 1
    halo = np.zeros((160, 256))
    for line in range(2):
        for c in range(TC):
            for half in range(2):
                at = 64 * half + SW * line + c + 2
                halo[at, at] = 1
        for c in range(2):
            for half in range(2):
                for side in range(2):
                    at = 64 * half + SW * line + (30 * side + c)
                    row = line + (0 if half else 5)
                    halo[at, 128 + 16 * (2 + 2 * half + side) + 2 * row + c] = 1
    for r in range(TR):
        for c in range(2):
            for side in range(2):
                halo[128 + 8 * (2 * side + c) + r, 128 + 16 * side + 2 * r + c] = 1
    halo2 = np.zeros((96, 256))
    for half in range(2):
        for c in range(TC):
            halo2[32 * half + c + 2, 32 * half + c + 2] = 1
        for side in range(2):
            row = 0 if half else 6
            halo2[32 * half + 1 + 29 * side, 64 + 16 * (2 + 2 * half + side) + row] = 1
    for r in range(TR):
        for side in range(2):
            halo2[64 + 16 * side + r + 1, 64 + 16 * side + r] = 1
    parts = dict(
        halo=halo, to_win=to_win, from_win=from_win, back_win=back_win,
        slots=slots, halo2=halo2,
    )
    starts, at = {}, 0
    for name, part in parts.items():
        starts[name] = (at, part.shape[0])
        at += part.shape[0]
    return np.concatenate(list(parts.values())), starts


PLACES, STARTS = placements()


def dot(a, b):
    return jnp.dot(a, b, preferred_element_type=F32)


def dot_nt(a, b):
    return lax.dot_general(a, b, (((1,), (1,)), ((), ())), preferred_element_type=F32)


def dot_tn(a, b):
    return lax.dot_general(a, b, (((0,), (0,)), ((), ())), preferred_element_type=F32)


def gelu_of(u):
    share = 0.5 + 0.5 * lax.erf(u * 0.5**0.5)
    density = jnp.exp2((-0.5 / np.log(2.0)) * (u * u))
    return u * share, share + (u * (0.5 / np.pi) ** 0.5) * density


def standardize(x):
    center = jnp.mean(x, axis=-1, keepdims=True)
    moved = x - center
    spread = jnp.mean(moved * moved, axis=-1, keepdims=True)
    scale = lax.rsqrt(spread + EPSILON)
    return moved * scale, scale


def standardize_back(grad, xhat, scale):
    first = jnp.mean(grad, axis=-1, keepdims=True)
    second = jnp.mean(grad * xhat, axis=-1, keepdims=True)
    return scale * (grad - first - xhat * second)


def by_head(x):
    head = lax.broadcasted_iota(jnp.int32, x.shape, 1) // HEAD_DIM
    zero = jnp.zeros_like(x)
    return jnp.concatenate([jnp.where(head == h, x, zero) for h in range(4)], axis=0)


def own_head(x):
    head = lax.broadcasted_iota(jnp.int32, (WPAD, 128), 1) // HEAD_DIM
    out = x[0:WPAD]
    for h in range(1, 4):
        out = jnp.where(head == h, x[WPAD * h : WPAD * (h + 1)], out)
    return out


def kernel(
    x_hbm, cot_hbm, cgain_hbm, dw_hbm, bgain_hbm, ggain_hbm,
    places_hbm, we_hbm, wp_hbm, bqkv_hbm, bout_hbm, bbias_hbm, gqkv_hbm, gout_hbm, gbias_hbm,
    out_ref, grad_ref,
    places, we, wp, bqkv, bout, bbias, gqkv, gout, gbias, load_sem, reach,
    x_ref, cot_ref, cgain_ref, dw_ref, bgain_ref, ggain_ref, rims,
    stage, own, cat, edges, own2, cat2, halo_sem, halo2_sem,
    cot_send, cot_recv, fwd_send, fwd_recv, res_send, res_recv, gra_send, gra_recv, grid_sem,
    mixbuf, xhat0, scale0, normed0, normed1, slope_u, slope_p, pre_act, update,
    bias_b, bias_g, zwin, packed_b, xhat_b, scale_b, prob_b, att,
    zgrid, dgrid, packed_g, xhat_g, scale_g, prob_g, dout, da, dpk, dscore, halo_grad, grad_e,
    cols_pre, cols_slope, cols_u, cols_e, halo_e,
):
    i, j = lax.axis_index("rows"), lax.axis_index("cols")
    me = i * COLS + j

    def around(step, rows=(-1, 0, 1), cols=(-1, 0, 1)):
        for a in rows:
            for b in cols:
                if a or b:
                    yield lax.rem(i + ROWS + step * a, ROWS), lax.rem(j + COLS + step * b, COLS)

    def greet(sem, devices):
        for device in devices:
            pl.semaphore_signal(sem, inc=1, device_id=device, device_id_type=MESH)

    barrier = pltpu.get_barrier_semaphore()
    greet(barrier, around(1))

    def load(index, src, dst):
        return pltpu.make_async_copy(src, dst, load_sem.at[index])

    loads = [
        load(n, src, dst)
        for n, (src, dst) in enumerate(
            [
                (x_hbm, x_ref), (places_hbm, places), (cgain_hbm, cgain_ref), (dw_hbm, dw_ref),
                (we_hbm, we), (cot_hbm, cot_ref), (wp_hbm, wp), (bgain_hbm, bgain_ref),
                (ggain_hbm, ggain_ref), (bbias_hbm, bbias),
                (gbias_hbm, gbias), (bqkv_hbm, bqkv), (bout_hbm, bout),
                (gout_hbm, gout), (gqkv_hbm, gqkv),
            ]
        )
    ]
    for one in loads:
        one.start()
    l_x, l_places, l_cgain, l_dw, l_we, l_cot, l_wp, l_bgain, l_ggain, l_bb = loads[:10]
    l_gb, l_bqkv, l_bout, l_gout, l_gqkv = loads[10:]

    def place(name, source):
        at, size = STARTS[name]
        return dot(places[at : at + size, 0 : source.shape[0]], source)

    stage[...] = jnp.zeros_like(stage)
    rims[...] = jnp.zeros_like(rims)
    l_x.wait()
    for r in range(TR):
        stage[SW * r + 2 : SW * r + 2 + TC, :] = x_ref[r].astype(F32)
    for r in range(TR):
        rims[2 * r : 2 * r + 2, :] = stage[SW * r + 2 : SW * r + 4, :]
        rims[16 + 2 * r : 18 + 2 * r, :] = stage[SW * r + 28 : SW * r + 30, :]
    own[...] = stage[...].astype(BF16)
    edges[...] = rims[...].astype(BF16)

    pl.semaphore_wait(barrier, 8)

    north, south = lax.rem(i + ROWS - 1, ROWS), lax.rem(i + 1, ROWS)
    west, east = lax.rem(j + COLS - 1, COLS), lax.rem(j + 1, COLS)

    def swap(sems, parts):
        copies = [
            pltpu.make_async_remote_copy(
                src_ref=src, dst_ref=dst, send_sem=sems.at[0, n], recv_sem=sems.at[1, n],
                device_id=to, device_id_type=MESH,
            )
            for n, (src, dst, to) in enumerate(parts)
        ]
        for one in copies:
            one.start()
        return copies

    w_cols, e_cols = edges.at[pl.ds(0, 16)], edges.at[pl.ds(16, 16)]
    halo = swap(
        halo_sem,
        [
            (own.at[pl.ds(0, 64)], cat.at[pl.ds(64, 64)], (north, j)),
            (own.at[pl.ds(160, 64)], cat.at[pl.ds(0, 64)], (south, j)),
            (e_cols, cat.at[pl.ds(128, 16)], (i, east)),
            (w_cols, cat.at[pl.ds(144, 16)], (i, west)),
            (e_cols, cat.at[pl.ds(160, 16)], (south, east)),
            (w_cols, cat.at[pl.ds(176, 16)], (south, west)),
            (e_cols, cat.at[pl.ds(192, 16)], (north, east)),
            (w_cols, cat.at[pl.ds(208, 16)], (north, west)),
        ],
    )

    def send_chunks(send, recv, sems, forward):
        def body(c, carry):
            a, b = lax.div(c, WIN), lax.rem(c, WIN)
            if forward:
                row, col = WIN * i + a, WIN * j + b
                ti, tj = lax.rem(row, ROWS), lax.rem(col, COLS)
                slot = lax.div(row, ROWS) * WIN + lax.div(col, COLS)
            else:
                row, col = ROWS * a + i, COLS * b + j
                ti, tj = lax.div(row, WIN), lax.div(col, WIN)
                slot = lax.rem(row, WIN) * WIN + lax.rem(col, WIN)
            mine = jnp.logical_and(ti == i, tj == j)

            @pl.when(mine)
            def _():
                pltpu.make_async_copy(send.at[c], recv.at[slot], sems.at[1]).start()

            @pl.when(jnp.logical_not(mine))
            def _():
                pltpu.make_async_remote_copy(
                    src_ref=send.at[c], dst_ref=recv.at[slot], send_sem=sems.at[0],
                    recv_sem=sems.at[1], device_id=(ti, tj), device_id_type=MESH,
                ).start()

            return carry

        lax.fori_loop(0, LEN, body, 0)

    def wait_chunks(recv, sems):
        pltpu.make_async_copy(recv, recv, sems.at[1]).wait()

    def wait_sent(send, sems):
        some = lax.rem(10 * i, ROWS) < WIN

        @pl.when(some)
        def _():
            part = send.at[pl.ds(0, LEN - 1)]
            pltpu.make_async_copy(part, part, sems.at[0]).wait()

        @pl.when(jnp.logical_not(some))
        def _():
            pltpu.make_async_copy(send, send, sems.at[0]).wait()

    greet(reach.at[0], around(1))
    l_places.wait()
    l_cgain.wait()
    l_dw.wait()
    l_cot.wait()
    mixbuf[...] = jnp.zeros_like(mixbuf)
    for r in range(TR):
        for k in range(4):
            mixbuf[pl.ds(112 * r + k, TC, stride=4), :] = cot_ref[
                r, :, 128 * k : 128 * (k + 1)
            ].astype(F32)
    cot_send[...] = mixbuf[0:784, :].reshape(LEN, 16, 128).astype(BF16)

    xhat, scale = standardize(stage[...])
    xhat0[...] = xhat
    scale0[...] = scale
    normed0[...] = (xhat * cgain_ref[...]).astype(BF16)
    l_we.wait()

    w = [dw_ref[n : n + 1, :] for n in range(9)]

    def wide(ref, rows=slice(None)):
        return jnp.concatenate([ref[n, rows, :] for n in range(ref.shape[0])], axis=1)

    def put_wide(ref, rows, value):
        for n in range(ref.shape[0]):
            ref[n, rows, :] = value[:, 128 * n : 128 * (n + 1)]

    def column(first, count):
        return pl.ds(first, count, stride=SW)

    def beside(strip, ends):
        at = lax.broadcasted_iota(jnp.int32, (8, 1), 0)
        first, last = strip[0:8], strip[24:32]
        for slot, row in ends:
            if slot < 8:
                first += jnp.where(at == slot, 1.0, 0.0) * row
            else:
                last += jnp.where(at == slot - 24, 1.0, 0.0) * row
        return jnp.concatenate([first, strip[8:24], last], axis=0)

    def lines(x, first, last):
        return x[SW * first : SW * last]

    def side_by_side(y):
        count = y[0].shape[0]
        return pltpu.roll(y[0], 1, 0) + y[1] + pltpu.roll(y[2], count - 1, 0)

    def expand_own():
        e, slope = gelu_of(dot(normed0[...], we[...]))
        put_wide(slope_u, slice(0, 224), slope)
        e = e.astype(BF16).astype(F32)
        y = []
        for b in range(3):
            t = [e * w[3 * a + b] for a in range(3)]
            y.append(
                jnp.concatenate(
                    [
                        lines(t[2], 0, 1),
                        lines(t[1], 0, 1) + lines(t[2], 1, 2),
                        lines(t[0], 0, 5) + lines(t[1], 1, 6) + lines(t[2], 2, 7),
                        lines(t[0], 5, 6) + lines(t[1], 6, 7),
                        lines(t[0], 6, 7),
                    ],
                    axis=0,
                )
            )
        put_wide(pre_act, slice(None), side_by_side(y))

    expand_own()
    pl.semaphore_wait(reach.at[0], 8)
    greet(reach.at[1], around(2))

    def flip(bias, h):
        square = jnp.concatenate(
            [bias[pl.ds(h, LEN, stride=16), :], jnp.zeros((LEN, 128 - LEN), F32)], axis=1
        )
        square = jnp.concatenate([square, jnp.zeros((WPAD - LEN, 128), F32)], axis=0)
        turned = square.T[0:WPAD]
        key = lax.broadcasted_iota(jnp.int32, (WPAD, WPAD), 0)
        return jnp.where(key < LEN, turned, -1e30)

    def flip_all(bias, bias_t):
        for g in range(4):
            for h in range(2):
                pair = [flip(bias, 4 * g + 2 * h + n) for n in range(2)]
                bias_t[g, :, 128 * h : 128 * (h + 1)] = jnp.concatenate(pair, axis=1)

    l_bb.wait()
    flip_all(bbias, bias_b)
    l_gb.wait()
    flip_all(gbias, bias_g)

    branch, slope = gelu_of(wide(pre_act, slice(32, 256)))
    put_wide(slope_p, slice(32, 256), slope)
    l_wp.wait()
    put_wide(update, slice(None), dot(branch.astype(BF16), wp[...]))

    pl.semaphore_wait(reach.at[1], 8)
    greet(reach.at[2], around(4, cols=(0,)))

    cols_pre[...] = jnp.zeros_like(cols_pre)
    for n, slot in enumerate((1, 2, 29, 30)):
        cols_pre[n, 0:9, :] = wide(pre_act, column(slot, 9))

    for one in halo:
        one.wait_recv()
    has_n, has_s, has_w, has_e = (
        jnp.where(there, 1.0, 0.0) for there in (i > 0, i < ROWS - 1, j > 0, j < COLS - 1)
    )

    def inside(count, strip, column):
        at = lax.broadcasted_iota(jnp.int32, (count, 1), 0)
        slot = lax.bitwise_and(at, SW - 1)
        keep = jnp.where(slot < 2, has_w, 1.0) * jnp.where(slot < 30, 1.0, has_e)
        strips = jnp.where(at < strip, has_n, has_s) * keep
        columns = jnp.where(at < 2 * strip + column, has_w, has_e)
        return jnp.where(at < 2 * strip, strips, columns)

    xh = place("halo", cat[...]) * inside(160, 64, 16)
    normed1[...] = (standardize(xh)[0] * cgain_ref[...]).astype(BF16)
    e, _ = gelu_of(dot(normed1[...], we[...]))
    e = e.astype(BF16).astype(F32)
    halo_e[...] = e

    def side(n):
        x = halo_e[128 + 8 * n : 136 + 8 * n, :]
        return pltpu.roll(jnp.concatenate([x, jnp.zeros((8, FF), F32)], axis=0), 2, 0)

    def downwards(terms):
        return terms[0] + pltpu.roll(terms[1], 15, 0) + pltpu.roll(terms[2], 14, 0)

    def strip(line, y, ends):
        ends = [(slot, x[line : line + 1]) for slot, x in ends]
        rows = slice(SW * line, SW * (line + 1))
        return wide(pre_act, rows) + beside(side_by_side(y), ends)

    left = downwards([side(1) * w[3 * a] for a in range(3)])
    right = downwards([side(2) * w[3 * a + 2] for a in range(3)])
    ends = [(2, left), (29, right)]
    rim = [
        strip(1, [lines(e, 1, 2) * w[b] for b in range(3)], ends),
        strip(7, [lines(e, 2, 3) * w[6 + b] for b in range(3)], ends),
        cols_pre[1] + left,
        cols_pre[2] + right,
    ]
    rim = jnp.concatenate([gelu_of(x)[0] for x in rim], axis=0).astype(BF16)

    def halo_slopes():
        n0, n1, s0, s1 = (halo_e[SW * n : SW * (n + 1), :] for n in range(4))
        w0, w1, e0, e1 = (side(n) for n in range(4))
        sides = [
            downwards([w0 * w[3 * a] + w1 * w[3 * a + 1] for a in range(3)]),
            downwards([w1 * w[3 * a] for a in range(3)]),
            downwards([e0 * w[3 * a + 2] for a in range(3)]),
            downwards([e0 * w[3 * a + 1] + e1 * w[3 * a + 2] for a in range(3)]),
        ]
        ends = list(zip((1, 2, 29, 30), sides))
        for line, y in (
            (0, [n0 * w[b] + n1 * w[3 + b] for b in range(3)]),
            (1, [n1 * w[b] for b in range(3)]),
            (7, [s0 * w[6 + b] for b in range(3)]),
            (8, [s0 * w[3 + b] + s1 * w[6 + b] for b in range(3)]),
        ):
            slope = gelu_of(strip(line, y, ends))[1]
            put_wide(slope_p, slice(SW * line, SW * (line + 1)), slope)
        for n, x in enumerate(sides):
            cols_slope[n] = gelu_of(cols_pre[n] + x)[1]
        for n, slot in enumerate((1, 2, 29, 30)):
            put_wide(slope_p, column(2 * SW + slot, 5), cols_slope[n, 2:7, :])
        for n, slot in ((0, 1), (3, 30)):
            cols_slope[n, 1:8, :] = wide(slope_p, column(SW + slot, TR))

    def put_rim(ref, value, first):
        put_wide(ref, column(2, TR), value[64 + first : 64 + first + TR])
        put_wide(ref, column(29, TR), value[80 + first : 80 + first + TR])
        put_wide(ref, slice(0, 32), value[0:32])
        put_wide(ref, slice(192, 224), value[32:64])

    put_rim(update, dot(rim, wp[...]), 1)
    mixed = (stage[...] + wide(update)).astype(BF16)
    zwin[...] = place("to_win", mixed)

    root = HEAD_DIM**-0.5

    def project_in(z, gain_ref, qkv, packed, xhat_ref, scale_ref):
        xhat, scale = standardize(z)
        xhat_ref[...] = xhat
        scale_ref[...] = scale
        normed = (xhat * gain_ref[...]).astype(BF16)
        for n in range(3):
            at = n * 512
            packed[:, at : at + 512] = dot(normed, qkv[:, at : at + 512]).astype(BF16)

    def parts_of(packed, rows, g):
        return [packed[rows, 512 * n + 128 * g : 512 * n + 128 * (g + 1)] for n in range(3)]

    def attend(packed, bias_t, prob):
        def window(w, carry):
            rows = pl.ds(pl.multiple_of(w * WPAD, WPAD), WPAD)
            for g in range(4):
                q, k, v = parts_of(packed, rows, g)
                s = dot_nt(k, by_head(q)) * root + bias_t[g]
                e = jnp.exp(s - jnp.max(s, axis=0, keepdims=True))
                prob[w, g] = e * (1.0 / jnp.sum(e, axis=0, keepdims=True))
            return carry

        lax.fori_loop(0, NWIN, window, 0, unroll=True)

        def gather(w, carry):
            rows = pl.ds(pl.multiple_of(w * WPAD, WPAD), WPAD)
            for g in range(4):
                v = parts_of(packed, rows, g)[2]
                one = own_head(dot_tn(prob[w, g].astype(BF16), v))
                att[rows, 128 * g : 128 * (g + 1)] = one.astype(BF16)
            return carry

        lax.fori_loop(0, NWIN, gather, 0, unroll=True)

    def attend_back(packed, prob):
        def window(w, carry):
            rows = pl.ds(pl.multiple_of(w * WPAD, WPAD), WPAD)
            for g in range(4):
                q, k, v = parts_of(packed, rows, g)
                p = prob[w, g]
                dam = by_head(da[rows, 128 * g : 128 * (g + 1)])
                dp = dot_nt(v, dam).astype(BF16).astype(F32)
                ds = p * (dp - jnp.sum(p * dp, axis=0, keepdims=True))
                ds = ds.astype(BF16)
                dscore[w, g] = ds
                dk = dot(ds, by_head(q)) * root
                dv = dot(p.astype(BF16), dam)
                for n, one in ((1, dk), (2, dv)):
                    dpk[rows, 512 * n + 128 * g : 512 * n + 128 * (g + 1)] = one.astype(BF16)
            return carry

        lax.fori_loop(0, NWIN, window, 0, unroll=True)

        def queries(w, carry):
            rows = pl.ds(pl.multiple_of(w * WPAD, WPAD), WPAD)
            for g in range(4):
                k = parts_of(packed, rows, g)[1]
                dq = own_head(dot_tn(dscore[w, g], k)) * root
                dpk[rows, 128 * g : 128 * (g + 1)] = dq.astype(BF16)
            return carry

        lax.fori_loop(0, NWIN, queries, 0, unroll=True)

    def project_back(qkv, gain_ref, xhat_ref, scale_ref):
        dn = dot_nt(dpk[...], qkv[...]).astype(BF16).astype(F32)
        dx = standardize_back(dn * gain_ref[...], xhat_ref[...], scale_ref[...])
        return (dout[...].astype(F32) + dx.astype(BF16).astype(F32)).astype(BF16)

    l_bqkv.wait()
    l_bgain.wait()
    l_ggain.wait()
    project_in(zwin[...], bgain_ref, bqkv, packed_b, xhat_b, scale_b)
    attend(packed_b, bias_b, prob_b)
    l_bout.wait()
    blocked = (zwin[...] + dot(att[...], bout[...])).astype(BF16)

    spatial = place("from_win", blocked)
    for k in range(4):
        mixbuf[pl.ds(k, 208, stride=4), :] = spatial[:, 128 * k : 128 * (k + 1)]
    fwd_send[...] = mixbuf[0:784, :].reshape(LEN, 16, 128).astype(BF16)
    pl.semaphore_wait(reach.at[2], 2)
    send_chunks(fwd_send, fwd_recv, grid_sem.at[1], True)
    send_chunks(cot_send, cot_recv, grid_sem.at[0], True)

    halo_slopes()
    cols_u[...] = jnp.zeros_like(cols_u)
    cols_e[...] = jnp.zeros_like(cols_e)
    for n, slot in enumerate((2, 29)):
        cols_u[n, 0:TR, :] = wide(slope_u, column(slot, TR))

    def to_windows(recv, target):
        mixbuf[0:784, :] = recv[...].astype(F32).reshape(784, 128)
        for w in range(NWIN):
            for k in range(4):
                target[WPAD * w : WPAD * w + LEN, 128 * k : 128 * (k + 1)] = mixbuf[
                    pl.ds(4 * w + k, LEN, stride=16), :
                ]

    def from_windows(source, send):
        for w in range(NWIN):
            for k in range(4):
                mixbuf[pl.ds(4 * w + k, LEN, stride=16), :] = source[
                    WPAD * w : WPAD * w + LEN, 128 * k : 128 * (k + 1)
                ]
        send[...] = mixbuf[0:784, :].reshape(LEN, 16, 128).astype(BF16)

    dgrid[...] = jnp.zeros_like(dgrid)
    zgrid[...] = jnp.zeros_like(zgrid)
    l_gqkv.wait()

    wait_chunks(fwd_recv, grid_sem.at[1])
    to_windows(fwd_recv, zgrid)
    project_in(zgrid[...], ggain_ref, gqkv, packed_g, xhat_g, scale_g)
    attend(packed_g, bias_g, prob_g)
    wait_chunks(cot_recv, grid_sem.at[0])
    to_windows(cot_recv, dgrid)
    dout[...] = dgrid[...].astype(BF16)
    l_gout.wait()
    da[...] = dot_nt(dout[...], gout[...]).astype(BF16)
    attend_back(packed_g, prob_g)
    dgrid[...] = project_back(gqkv, ggain_ref, xhat_g, scale_g).astype(F32)
    from_windows(dgrid, gra_send)
    send_chunks(gra_send, gra_recv, grid_sem.at[3], False)
    zgrid[...] = (zgrid[...] + dot(att[...], gout[...])).astype(BF16).astype(F32)
    from_windows(zgrid, res_send)
    send_chunks(res_send, res_recv, grid_sem.at[2], False)

    wait_chunks(gra_recv, grid_sem.at[3])
    mixbuf[0:784, :] = gra_recv[...].astype(F32).reshape(784, 128)
    mixbuf[784:832, :] = jnp.zeros((48, 128), F32)
    spatial = jnp.concatenate([mixbuf[pl.ds(k, 208, stride=4), :] for k in range(4)], axis=1)
    dout[...] = place("back_win", spatial.astype(BF16)).astype(BF16)
    da[...] = dot_nt(dout[...], bout[...]).astype(BF16)
    attend_back(packed_b, prob_b)
    slotted = place("slots", project_back(bqkv, bgain_ref, xhat_b, scale_b))
    stage[...] = slotted[0:224]
    own2[...] = slotted.astype(BF16)
    w_col2, e_col2 = own2.at[pl.ds(224, 16)], own2.at[pl.ds(240, 16)]
    halo2 = swap(
        halo2_sem,
        [
            (own2.at[pl.ds(0, 32)], cat2.at[pl.ds(32, 32)], (north, j)),
            (own2.at[pl.ds(192, 32)], cat2.at[pl.ds(0, 32)], (south, j)),
            (e_col2, cat2.at[pl.ds(64, 16)], (i, east)),
            (w_col2, cat2.at[pl.ds(80, 16)], (i, west)),
            (e_col2, cat2.at[pl.ds(96, 16)], (south, east)),
            (w_col2, cat2.at[pl.ds(112, 16)], (south, west)),
            (e_col2, cat2.at[pl.ds(128, 16)], (north, east)),
            (w_col2, cat2.at[pl.ds(144, 16)], (north, west)),
        ],
    )

    def back_own():
        gp = dot_nt(own2[0:224, :], wp[...]).astype(BF16).astype(F32)
        gp = gp * wide(slope_p, slice(32, 256))
        y = []
        for b in range(3):
            t = [gp * w[3 * a + 2 - b] for a in range(3)]
            y.append(
                jnp.concatenate(
                    [
                        lines(t[0], 1, 2) + lines(t[1], 0, 1),
                        lines(t[0], 2, 7) + lines(t[1], 1, 6) + lines(t[2], 0, 5),
                        lines(t[1], 6, 7) + lines(t[2], 5, 6),
                    ],
                    axis=0,
                )
            )
        put_wide(grad_e, slice(0, 224), side_by_side(y))

    def back_hidden(rows):
        return wide(grad_e, rows).astype(BF16).astype(F32) * wide(slope_u, rows)

    back_own()
    for n, slot in enumerate((2, 29)):
        cols_e[n, 0:TR, :] = wide(grad_e, column(slot, TR))
    put_wide(update, slice(None), dot_nt(back_hidden(slice(0, 224)).astype(BF16), we[...]))
    wait_chunks(res_recv, grid_sem.at[2])
    out_ref[...] = res_recv[...]

    for one in halo2:
        one.wait_recv()
    gm = place("halo2", cat2[...]) * inside(96, 32, 16)
    halo_grad[...] = gm.astype(BF16)

    gp = dot_nt(halo_grad[...], wp[...]).astype(BF16).astype(F32)
    north_gp = gp[0:32] * wide(slope_p, slice(0, 32))
    south_gp = gp[32:64] * wide(slope_p, slice(256, 288))
    sides = []
    for x, b in ((gp[64:80] * cols_slope[0], 2), (gp[80:96] * cols_slope[3], 0)):
        sides.append(
            pltpu.roll(x * w[b], 14, 0) + pltpu.roll(x * w[3 + b], 15, 0) + x * w[6 + b]
        )

    def hidden(grad, slope):
        return grad.astype(BF16).astype(F32) * slope

    rim = []
    for line, y in (
        (0, [north_gp * w[8 - b] for b in range(3)]),
        (6, [south_gp * w[2 - b] for b in range(3)]),
    ):
        rows = slice(SW * line, SW * (line + 1))
        ends = [(slot, x[line : line + 1]) for slot, x in zip((2, 29), sides)]
        rim.append(
            hidden(wide(grad_e, rows) + beside(side_by_side(y), ends), wide(slope_u, rows))
        )
    for n, x in enumerate(sides):
        rim.append(hidden(cols_e[n] + x, cols_u[n]))
    rim = jnp.concatenate(rim, axis=0).astype(BF16)
    put_rim(update, dot_nt(rim, we[...]), 0)
    dn = wide(update).astype(BF16).astype(F32)
    dx = standardize_back(dn * cgain_ref[...], xhat0[...], scale0[...])
    stage[...] = stage[...] + dx.astype(BF16).astype(F32)
    for r in range(TR):
        grad_ref[r] = stage[SW * r + 2 : SW * r + 2 + TC, :].astype(BF16)

    for one in halo + halo2:
        one.wait_send()
    for n, send in enumerate((cot_send, fwd_send, res_send, gra_send)):
        wait_sent(send, grid_sem.at[n])


def finish(chunks_ref, kept_ref, out_ref, grad_ref, mixbuf):
    mixbuf[...] = chunks_ref[...].astype(F32).reshape(784, 128)
    for r in range(TR):
        for k in range(4):
            out_ref[r, :, 128 * k : 128 * (k + 1)] = mixbuf[
                pl.ds(112 * r + k, TC, stride=4), :
            ].astype(BF16)
    grad_ref[...] = kept_ref[...]


def local(
    inputs, cotangent, conv_gain, expand_weight, depth_weight, project_weight,
    block_gain, block_qkv, block_out, block_bias, grid_gain, grid_qkv, grid_out, grid_bias,
):
    def by_query(bias):
        return bias.transpose(1, 0, 2).reshape(16 * LEN, LEN)

    vmem, hbm = pl.BlockSpec(memory_space=pltpu.VMEM), pl.BlockSpec(memory_space=pl.ANY)
    places = jnp.asarray(PLACES, BF16)
    chunks = pltpu.VMEM((LEN, 16, 128), BF16)
    tokens = jax.ShapeDtypeStruct((TR, TC, D), BF16)
    bias = pltpu.VMEM((16 * LEN, LEN), F32)
    bias_t = pltpu.VMEM((4, WPAD, 256), F32)
    win_f32, win_bf16 = pltpu.VMEM((256, D), F32), pltpu.VMEM((256, D), BF16)
    packed = pltpu.VMEM((256, 3 * D), BF16)
    scale = pltpu.VMEM((256, 1), F32)
    prob = pltpu.VMEM((NWIN, 4, WPAD, 256), F32)
    scratch = [
        pltpu.VMEM(PLACES.shape, BF16), pltpu.VMEM((D, FF), BF16), pltpu.VMEM((FF, D), BF16),
        pltpu.VMEM((D, 3 * D), BF16), pltpu.VMEM((D, D), BF16), bias,
        pltpu.VMEM((D, 3 * D), BF16), pltpu.VMEM((D, D), BF16), bias,
        pltpu.SemaphoreType.DMA((15,)), pltpu.SemaphoreType.REGULAR((3,)),
        pltpu.VMEM((TR, TC, D), BF16), pltpu.VMEM((TR, TC, D), BF16), pltpu.VMEM((1, D), F32),
        pltpu.VMEM((9, FF), F32), pltpu.VMEM((1, D), F32), pltpu.VMEM((1, D), F32),
        pltpu.VMEM((32, D), F32),
        pltpu.VMEM((224, D), F32), pltpu.VMEM((224, D), BF16), pltpu.VMEM((224, D), BF16),
        pltpu.VMEM((32, D), BF16), pltpu.VMEM((256, D), BF16), pltpu.VMEM((160, D), BF16),
        pltpu.SemaphoreType.DMA((2, 8)), pltpu.SemaphoreType.DMA((2, 8)),
        chunks, chunks, chunks, chunks, chunks, chunks, chunks, chunks,
        pltpu.SemaphoreType.DMA((4, 2)),
        pltpu.VMEM((832, 128), F32), pltpu.VMEM((224, D), F32), pltpu.VMEM((224, 1), F32),
        pltpu.VMEM((224, D), BF16), pltpu.VMEM((160, D), BF16),
        pltpu.VMEM((FF // 128, 256, 128), F32), pltpu.VMEM((FF // 128, 288, 128), F32),
        pltpu.VMEM((FF // 128, 288, 128), F32), pltpu.VMEM((D // 128, 224, 128), F32),
        bias_t, bias_t, win_f32, packed, win_f32, scale, prob, win_bf16,
        win_f32, win_f32, packed, win_f32, scale, prob, win_bf16, win_bf16, packed,
        pltpu.VMEM((NWIN, 4, WPAD, 256), BF16), pltpu.VMEM((96, D), BF16),
        pltpu.VMEM((FF // 128, 256, 128), F32),
        pltpu.VMEM((4, 16, FF), F32), pltpu.VMEM((4, 16, FF), F32),
        pltpu.VMEM((2, 16, FF), F32), pltpu.VMEM((2, 16, FF), F32), pltpu.VMEM((160, FF), F32),
    ]
    result, grad = pl.pallas_call(
        kernel,
        out_shape=(jax.ShapeDtypeStruct((LEN, 16, 128), BF16), tokens),
        in_specs=[hbm] * 15,
        out_specs=(vmem, vmem),
        scratch_shapes=scratch,
        compiler_params=pltpu.CompilerParams(
            collective_id=0, has_side_effects=True, vmem_limit_bytes=56 * 2**20
        ),
        name="mbconv_attention",
    )(
        inputs, cotangent, conv_gain.reshape(1, D), depth_weight, block_gain.reshape(1, D),
        grid_gain.reshape(1, D), places, expand_weight, project_weight, block_qkv, block_out,
        by_query(block_bias), grid_qkv, grid_out, by_query(grid_bias),
    )
    return pl.pallas_call(
        finish,
        out_shape=(tokens, tokens),
        in_specs=[vmem] * 2,
        out_specs=(vmem, vmem),
        scratch_shapes=[pltpu.VMEM((784, 128), F32)],
        name="finish",
    )(result, grad)


def solution(mesh):
    tokens = P("rows", "cols", None)
    in_specs = (tokens, tokens) + (P(),) * 12
    return jax.shard_map(
        local, mesh=mesh, in_specs=in_specs, out_specs=(tokens, tokens), check_vma=False
    )
```

```python
import functools

import jax
import jax.numpy as jnp
import numpy as np
from jax import lax
from jax.experimental import pallas as pl
from jax.experimental.pallas import tpu as pltpu
from jax.sharding import PartitionSpec as P

ROWS, COLS = 16, 8
HEIGHT, BREADTH = 112, 224
WIN = 7
D = 512
FF = 2048
HEAD_DIM = 32
TR, TC = 7, 28
SW = 32
NWIN, WPAD = 4, 64
LEN = 49
KEYS = 56
EPSILON = 1e-05
F32, BF16 = jnp.float32, jnp.bfloat16
MESH = pl.DeviceIdType.MESH


def win_row(row, col):
    return WPAD * (col // WIN) + WIN * row + col % WIN


def placements():
    slots = np.zeros((256, 256))
    to_win = np.zeros((256, 256))
    from_win = np.zeros((208, 256))
    back_win = np.zeros((256, 256))
    for r in range(TR):
        for c in range(TC):
            to_win[win_row(r, c), SW * r + c + 2] = 1
            slots[SW * r + c + 2, win_row(r, c)] = 1
            from_win[TC * r + c, win_row(r, c)] = 1
            back_win[win_row(r, c), TC * r + c] = 1
        slots[224 + r, win_row(r, 0)] = 1
        slots[240 + r, win_row(r, 27)] = 1
    halo = np.zeros((160, 256))
    for line in range(2):
        for c in range(TC):
            for half in range(2):
                at = 64 * half + SW * line + c + 2
                halo[at, at] = 1
        for c in range(2):
            for half in range(2):
                for side in range(2):
                    at = 64 * half + SW * line + (30 * side + c)
                    row = line + (0 if half else 5)
                    halo[at, 128 + 16 * (2 + 2 * half + side) + 2 * row + c] = 1
    for r in range(TR):
        for c in range(2):
            for side in range(2):
                halo[128 + 8 * (2 * side + c) + r, 128 + 16 * side + 2 * r + c] = 1
    halo2 = np.zeros((96, 256))
    for half in range(2):
        for c in range(TC):
            halo2[32 * half + c + 2, 32 * half + c + 2] = 1
        for side in range(2):
            row = 0 if half else 6
            halo2[32 * half + 1 + 29 * side, 64 + 16 * (2 + 2 * half + side) + row] = 1
    for r in range(TR):
        for side in range(2):
            halo2[64 + 16 * side + r + 1, 64 + 16 * side + r] = 1
    parts = dict(
        halo=halo, to_win=to_win, from_win=from_win, back_win=back_win,
        slots=slots, halo2=halo2,
    )
    starts, at = {}, 0
    for name, part in parts.items():
        starts[name] = (at, part.shape[0])
        at += part.shape[0]
    return np.concatenate(list(parts.values())), starts


PLACES, STARTS = placements()


def dot(a, b):
    return jnp.dot(a, b, preferred_element_type=F32)


def dot_nt(a, b):
    return lax.dot_general(a, b, (((1,), (1,)), ((), ())), preferred_element_type=F32)


def dot_tn(a, b):
    return lax.dot_general(a, b, (((0,), (0,)), ((), ())), preferred_element_type=F32)


def gelu_of(u):
    share = 0.5 + 0.5 * lax.erf(u * 0.5**0.5)
    density = jnp.exp2((-0.5 / np.log(2.0)) * (u * u))
    return u * share, share + (u * (0.5 / np.pi) ** 0.5) * density


def standardize(x):
    center = jnp.mean(x, axis=-1, keepdims=True)
    moved = x - center
    spread = jnp.mean(moved * moved, axis=-1, keepdims=True)
    scale = lax.rsqrt(spread + EPSILON)
    return moved * scale, scale


def standardize_back(grad, xhat, scale):
    first = jnp.mean(grad, axis=-1, keepdims=True)
    second = jnp.mean(grad * xhat, axis=-1, keepdims=True)
    return scale * (grad - first - xhat * second)


def by_head(x):
    head = lax.broadcasted_iota(jnp.int32, x.shape, 1) // HEAD_DIM
    zero = jnp.zeros_like(x)
    return jnp.concatenate([jnp.where(head == h, x, zero) for h in range(4)], axis=0)


def own_head(x):
    head = lax.broadcasted_iota(jnp.int32, (WPAD, 128), 1) // HEAD_DIM
    out = x[0:WPAD]
    for h in range(1, 4):
        out = jnp.where(head == h, x[WPAD * h : WPAD * (h + 1)], out)
    return out


def kernel(
    x_hbm, cot_hbm, cgain_hbm, dw_hbm, bgain_hbm, ggain_hbm,
    places_hbm, we_hbm, wp_hbm, bqkv_hbm, bout_hbm, bbias_hbm, gqkv_hbm, gout_hbm, gbias_hbm,
    out_ref, grad_ref,
    places, we, wp, bqkv, bout, bbias, gqkv, gout, gbias, load_sem, reach,
    x_ref, cot_ref, cgain_ref, dw_ref, bgain_ref, ggain_ref, rims,
    stage, own, cat, edges, own2, cat2, halo_sem, halo2_sem,
    cot_send, cot_recv, fwd_send, fwd_recv, res_send, res_recv, gra_send, gra_recv, grid_sem,
    mixbuf, xhat0, scale0, normed0, normed1, slope_u, slope_p, pre_act, update,
    bias_b, bias_g, zwin, packed_b, xhat_b, scale_b, prob_b, att,
    zgrid, dgrid, packed_g, xhat_g, scale_g, prob_g, dout, da, dpk, dscore, halo_grad, grad_e,
    cols_pre, cols_slope, cols_u, cols_e, halo_e,
):
    i, j = lax.axis_index("rows"), lax.axis_index("cols")
    me = i * COLS + j

    def around(step, rows=(-1, 0, 1), cols=(-1, 0, 1)):
        for a in rows:
            for b in cols:
                if a or b:
                    yield lax.rem(i + ROWS + step * a, ROWS), lax.rem(j + COLS + step * b, COLS)

    def greet(sem, devices):
        for device in devices:
            pl.semaphore_signal(sem, inc=1, device_id=device, device_id_type=MESH)

    barrier = pltpu.get_barrier_semaphore()
    greet(barrier, around(1))

    def load(index, src, dst):
        return pltpu.make_async_copy(src, dst, load_sem.at[index])

    loads = [
        load(n, src, dst)
        for n, (src, dst) in enumerate(
            [
                (x_hbm, x_ref), (places_hbm, places), (cgain_hbm, cgain_ref), (dw_hbm, dw_ref),
                (we_hbm, we), (cot_hbm, cot_ref), (wp_hbm, wp), (bgain_hbm, bgain_ref),
                (ggain_hbm, ggain_ref), (bbias_hbm, bbias),
                (gbias_hbm, gbias), (bqkv_hbm, bqkv), (bout_hbm, bout),
                (gout_hbm, gout), (gqkv_hbm, gqkv),
            ]
        )
    ]
    for one in loads:
        one.start()
    l_x, l_places, l_cgain, l_dw, l_we, l_cot, l_wp, l_bgain, l_ggain, l_bb = loads[:10]
    l_gb, l_bqkv, l_bout, l_gout, l_gqkv = loads[10:]

    def place(name, source):
        at, size = STARTS[name]
        return dot(places[at : at + size, 0 : source.shape[0]], source)

    stage[...] = jnp.zeros_like(stage)
    rims[...] = jnp.zeros_like(rims)
    l_x.wait()
    for r in range(TR):
        stage[SW * r + 2 : SW * r + 2 + TC, :] = x_ref[r].astype(F32)
    for r in range(TR):
        rims[2 * r : 2 * r + 2, :] = stage[SW * r + 2 : SW * r + 4, :]
        rims[16 + 2 * r : 18 + 2 * r, :] = stage[SW * r + 28 : SW * r + 30, :]
    own[...] = stage[...].astype(BF16)
    edges[...] = rims[...].astype(BF16)

    pl.semaphore_wait(barrier, 8)

    north, south = lax.rem(i + ROWS - 1, ROWS), lax.rem(i + 1, ROWS)
    west, east = lax.rem(j + COLS - 1, COLS), lax.rem(j + 1, COLS)

    def swap(sems, parts):
        copies = [
            pltpu.make_async_remote_copy(
                src_ref=src, dst_ref=dst, send_sem=sems.at[0, n], recv_sem=sems.at[1, n],
                device_id=to, device_id_type=MESH,
            )
            for n, (src, dst, to) in enumerate(parts)
        ]
        for one in copies:
            one.start()
        return copies

    w_cols, e_cols = edges.at[pl.ds(0, 16)], edges.at[pl.ds(16, 16)]
    halo = swap(
        halo_sem,
        [
            (own.at[pl.ds(0, 64)], cat.at[pl.ds(64, 64)], (north, j)),
            (own.at[pl.ds(160, 64)], cat.at[pl.ds(0, 64)], (south, j)),
            (e_cols, cat.at[pl.ds(128, 16)], (i, east)),
            (w_cols, cat.at[pl.ds(144, 16)], (i, west)),
            (e_cols, cat.at[pl.ds(160, 16)], (south, east)),
            (w_cols, cat.at[pl.ds(176, 16)], (south, west)),
            (e_cols, cat.at[pl.ds(192, 16)], (north, east)),
            (w_cols, cat.at[pl.ds(208, 16)], (north, west)),
        ],
    )

    def send_chunks(send, recv, sems, forward):
        def body(c, carry):
            a, b = lax.div(c, WIN), lax.rem(c, WIN)
            if forward:
                row, col = WIN * i + a, WIN * j + b
                ti, tj = lax.rem(row, ROWS), lax.rem(col, COLS)
                slot = lax.div(row, ROWS) * WIN + lax.div(col, COLS)
            else:
                row, col = ROWS * a + i, COLS * b + j
                ti, tj = lax.div(row, WIN), lax.div(col, WIN)
                slot = lax.rem(row, WIN) * WIN + lax.rem(col, WIN)
            mine = jnp.logical_and(ti == i, tj == j)

            @pl.when(mine)
            def _():
                pltpu.make_async_copy(send.at[c], recv.at[slot], sems.at[1]).start()

            @pl.when(jnp.logical_not(mine))
            def _():
                pltpu.make_async_remote_copy(
                    src_ref=send.at[c], dst_ref=recv.at[slot], send_sem=sems.at[0],
                    recv_sem=sems.at[1], device_id=(ti, tj), device_id_type=MESH,
                ).start()

            return carry

        lax.fori_loop(0, LEN, body, 0)

    def wait_chunks(recv, sems):
        pltpu.make_async_copy(recv, recv, sems.at[1]).wait()

    def wait_sent(send, sems):
        some = lax.rem(10 * i, ROWS) < WIN

        @pl.when(some)
        def _():
            part = send.at[pl.ds(0, LEN - 1)]
            pltpu.make_async_copy(part, part, sems.at[0]).wait()

        @pl.when(jnp.logical_not(some))
        def _():
            pltpu.make_async_copy(send, send, sems.at[0]).wait()

    greet(reach.at[0], around(1))
    l_places.wait()
    l_cgain.wait()
    l_dw.wait()
    l_cot.wait()
    mixbuf[...] = jnp.zeros_like(mixbuf)
    for r in range(TR):
        for k in range(4):
            mixbuf[pl.ds(112 * r + k, TC, stride=4), :] = cot_ref[
                r, :, 128 * k : 128 * (k + 1)
            ].astype(F32)
    cot_send[...] = mixbuf[0:784, :].reshape(LEN, 16, 128).astype(BF16)

    xhat, scale = standardize(stage[...])
    xhat0[...] = xhat
    scale0[...] = scale
    normed0[...] = (xhat * cgain_ref[...]).astype(BF16)
    l_we.wait()

    w = [dw_ref[n : n + 1, :] for n in range(9)]

    def wide(ref, rows=slice(None)):
        return jnp.concatenate([ref[n, rows, :] for n in range(ref.shape[0])], axis=1)

    def put_wide(ref, rows, value):
        for n in range(ref.shape[0]):
            ref[n, rows, :] = value[:, 128 * n : 128 * (n + 1)]

    def column(first, count):
        return pl.ds(first, count, stride=SW)

    def beside(strip, ends):
        at = lax.broadcasted_iota(jnp.int32, (8, 1), 0)
        first, last = strip[0:8], strip[24:32]
        for slot, row in ends:
            if slot < 8:
                first += jnp.where(at == slot, 1.0, 0.0) * row
            else:
                last += jnp.where(at == slot - 24, 1.0, 0.0) * row
        return jnp.concatenate([first, strip[8:24], last], axis=0)

    def lines(x, first, last):
        return x[SW * first : SW * last]

    def side_by_side(y):
        count = y[0].shape[0]
        return pltpu.roll(y[0], 1, 0) + y[1] + pltpu.roll(y[2], count - 1, 0)

    def expand_own():
        e, slope = gelu_of(dot(normed0[...], we[...]))
        put_wide(slope_u, slice(0, 224), slope)
        e = e.astype(BF16).astype(F32)
        y = []
        for b in range(3):
            t = [e * w[3 * a + b] for a in range(3)]
            y.append(
                jnp.concatenate(
                    [
                        lines(t[2], 0, 1),
                        lines(t[1], 0, 1) + lines(t[2], 1, 2),
                        lines(t[0], 0, 5) + lines(t[1], 1, 6) + lines(t[2], 2, 7),
                        lines(t[0], 5, 6) + lines(t[1], 6, 7),
                        lines(t[0], 6, 7),
                    ],
                    axis=0,
                )
            )
        put_wide(pre_act, slice(None), side_by_side(y))

    expand_own()
    pl.semaphore_wait(reach.at[0], 8)
    greet(reach.at[1], around(2))

    def flip(bias, h):
        square = jnp.concatenate(
            [bias[pl.ds(h, LEN, stride=16), :], jnp.zeros((LEN, 128 - LEN), F32)], axis=1
        )
        square = jnp.concatenate([square, jnp.zeros((WPAD - LEN, 128), F32)], axis=0)
        turned = square.T[0:WPAD]
        key = lax.broadcasted_iota(jnp.int32, (WPAD, WPAD), 0)
        return jnp.where(key < LEN, turned, -1e30)

    def flip_all(bias, bias_t):
        for g in range(4):
            for h in range(2):
                pair = [flip(bias, 4 * g + 2 * h + n) for n in range(2)]
                bias_t[g, :, 128 * h : 128 * (h + 1)] = jnp.concatenate(pair, axis=1)

    l_bb.wait()
    flip_all(bbias, bias_b)
    l_gb.wait()
    flip_all(gbias, bias_g)

    branch, slope = gelu_of(wide(pre_act, slice(32, 256)))
    put_wide(slope_p, slice(32, 256), slope)
    l_wp.wait()
    put_wide(update, slice(None), dot(branch.astype(BF16), wp[...]))

    pl.semaphore_wait(reach.at[1], 8)
    greet(reach.at[2], around(4, cols=(0,)))

    cols_pre[...] = jnp.zeros_like(cols_pre)
    for n, slot in enumerate((1, 2, 29, 30)):
        cols_pre[n, 0:9, :] = wide(pre_act, column(slot, 9))

    for one in halo:
        one.wait_recv()
    has_n, has_s, has_w, has_e = (
        jnp.where(there, 1.0, 0.0) for there in (i > 0, i < ROWS - 1, j > 0, j < COLS - 1)
    )

    def inside(count, strip, column):
        at = lax.broadcasted_iota(jnp.int32, (count, 1), 0)
        slot = lax.bitwise_and(at, SW - 1)
        keep = jnp.where(slot < 2, has_w, 1.0) * jnp.where(slot < 30, 1.0, has_e)
        strips = jnp.where(at < strip, has_n, has_s) * keep
        columns = jnp.where(at < 2 * strip + column, has_w, has_e)
        return jnp.where(at < 2 * strip, strips, columns)

    xh = place("halo", cat[...]) * inside(160, 64, 16)
    normed1[...] = (standardize(xh)[0] * cgain_ref[...]).astype(BF16)
    e, _ = gelu_of(dot(normed1[...], we[...]))
    e = e.astype(BF16).astype(F32)
    halo_e[...] = e

    def side(n):
        x = halo_e[128 + 8 * n : 136 + 8 * n, :]
        return pltpu.roll(jnp.concatenate([x, jnp.zeros((8, FF), F32)], axis=0), 2, 0)

    def downwards(terms):
        return terms[0] + pltpu.roll(terms[1], 15, 0) + pltpu.roll(terms[2], 14, 0)

    def strip(line, y, ends):
        ends = [(slot, x[line : line + 1]) for slot, x in ends]
        rows = slice(SW * line, SW * (line + 1))
        return wide(pre_act, rows) + beside(side_by_side(y), ends)

    left = downwards([side(1) * w[3 * a] for a in range(3)])
    right = downwards([side(2) * w[3 * a + 2] for a in range(3)])
    ends = [(2, left), (29, right)]
    rim = [
        strip(1, [lines(e, 1, 2) * w[b] for b in range(3)], ends),
        strip(7, [lines(e, 2, 3) * w[6 + b] for b in range(3)], ends),
        cols_pre[1] + left,
        cols_pre[2] + right,
    ]
    rim = jnp.concatenate([gelu_of(x)[0] for x in rim], axis=0).astype(BF16)

    def halo_slopes():
        n0, n1, s0, s1 = (halo_e[SW * n : SW * (n + 1), :] for n in range(4))
        w0, w1, e0, e1 = (side(n) for n in range(4))
        sides = [
            downwards([w0 * w[3 * a] + w1 * w[3 * a + 1] for a in range(3)]),
            downwards([w1 * w[3 * a] for a in range(3)]),
            downwards([e0 * w[3 * a + 2] for a in range(3)]),
            downwards([e0 * w[3 * a + 1] + e1 * w[3 * a + 2] for a in range(3)]),
        ]
        ends = list(zip((1, 2, 29, 30), sides))
        for line, y in (
            (0, [n0 * w[b] + n1 * w[3 + b] for b in range(3)]),
            (1, [n1 * w[b] for b in range(3)]),
            (7, [s0 * w[6 + b] for b in range(3)]),
            (8, [s0 * w[3 + b] + s1 * w[6 + b] for b in range(3)]),
        ):
            slope = gelu_of(strip(line, y, ends))[1]
            put_wide(slope_p, slice(SW * line, SW * (line + 1)), slope)
        for n, x in enumerate(sides):
            cols_slope[n] = gelu_of(cols_pre[n] + x)[1]
        for n, slot in enumerate((1, 2, 29, 30)):
            put_wide(slope_p, column(2 * SW + slot, 5), cols_slope[n, 2:7, :])
        for n, slot in ((0, 1), (3, 30)):
            cols_slope[n, 1:8, :] = wide(slope_p, column(SW + slot, TR))

    def put_rim(ref, value, first):
        put_wide(ref, column(2, TR), value[64 + first : 64 + first + TR])
        put_wide(ref, column(29, TR), value[80 + first : 80 + first + TR])
        put_wide(ref, slice(0, 32), value[0:32])
        put_wide(ref, slice(192, 224), value[32:64])

    put_rim(update, dot(rim, wp[...]), 1)
    mixed = (stage[...] + wide(update)).astype(BF16)
    zwin[...] = place("to_win", mixed)

    root = HEAD_DIM**-0.5

    def project_in(z, gain_ref, qkv, packed, xhat_ref, scale_ref):
        xhat, scale = standardize(z)
        xhat_ref[...] = xhat
        scale_ref[...] = scale
        normed = (xhat * gain_ref[...]).astype(BF16)
        for n in range(3):
            at = n * 512
            packed[:, at : at + 512] = dot(normed, qkv[:, at : at + 512]).astype(BF16)

    def parts_of(packed, rows, g):
        return [packed[rows, 512 * n + 128 * g : 512 * n + 128 * (g + 1)] for n in range(3)]

    def attend(packed, bias_t, prob):
        def window(w, carry):
            rows = pl.ds(pl.multiple_of(w * WPAD, WPAD), WPAD)
            for g in range(4):
                q, k, v = parts_of(packed, rows, g)
                s = dot_nt(k, by_head(q))[0:KEYS] * root + bias_t[g, 0:KEYS, :]
                e = jnp.exp(s - jnp.max(s, axis=0, keepdims=True))
                prob[w, g, 0:KEYS, :] = e * (1.0 / jnp.sum(e, axis=0, keepdims=True))
                prob[w, g, KEYS:WPAD, :] = jnp.zeros((WPAD - KEYS, 256), F32)
            return carry

        lax.fori_loop(0, NWIN, window, 0, unroll=True)

        def gather(w, carry):
            rows = pl.ds(pl.multiple_of(w * WPAD, WPAD), WPAD)
            for g in range(4):
                v = parts_of(packed, rows, g)[2]
                one = own_head(dot_tn(prob[w, g].astype(BF16), v))
                att[rows, 128 * g : 128 * (g + 1)] = one.astype(BF16)
            return carry

        lax.fori_loop(0, NWIN, gather, 0, unroll=True)

    def attend_back(packed, prob):
        def window(w, carry):
            rows = pl.ds(pl.multiple_of(w * WPAD, WPAD), WPAD)
            for g in range(4):
                q, k, v = parts_of(packed, rows, g)
                p = prob[w, g]
                dam = by_head(da[rows, 128 * g : 128 * (g + 1)])
                dp = dot_nt(v, dam)[0:KEYS].astype(BF16).astype(F32)
                inner = p[0:KEYS] * dp
                ds = p[0:KEYS] * (dp - jnp.sum(inner, axis=0, keepdims=True))
                ds = jnp.concatenate([ds, jnp.zeros((WPAD - KEYS, 256), F32)], axis=0)
                ds = ds.astype(BF16)
                dscore[w, g] = ds
                dk = dot(ds, by_head(q)) * root
                dv = dot(p.astype(BF16), dam)
                for n, one in ((1, dk), (2, dv)):
                    dpk[rows, 512 * n + 128 * g : 512 * n + 128 * (g + 1)] = one.astype(BF16)
            return carry

        lax.fori_loop(0, NWIN, window, 0, unroll=True)

        def queries(w, carry):
            rows = pl.ds(pl.multiple_of(w * WPAD, WPAD), WPAD)
            for g in range(4):
                k = parts_of(packed, rows, g)[1]
                dq = own_head(dot_tn(dscore[w, g], k)) * root
                dpk[rows, 128 * g : 128 * (g + 1)] = dq.astype(BF16)
            return carry

        lax.fori_loop(0, NWIN, queries, 0, unroll=True)

    def project_back(qkv, gain_ref, xhat_ref, scale_ref):
        dn = dot_nt(dpk[...], qkv[...]).astype(BF16).astype(F32)
        dx = standardize_back(dn * gain_ref[...], xhat_ref[...], scale_ref[...])
        return (dout[...].astype(F32) + dx.astype(BF16).astype(F32)).astype(BF16)

    l_bqkv.wait()
    l_bgain.wait()
    l_ggain.wait()
    project_in(zwin[...], bgain_ref, bqkv, packed_b, xhat_b, scale_b)
    attend(packed_b, bias_b, prob_b)
    l_bout.wait()
    blocked = (zwin[...] + dot(att[...], bout[...])).astype(BF16)

    spatial = place("from_win", blocked)
    for k in range(4):
        mixbuf[pl.ds(k, 208, stride=4), :] = spatial[:, 128 * k : 128 * (k + 1)]
    fwd_send[...] = mixbuf[0:784, :].reshape(LEN, 16, 128).astype(BF16)
    pl.semaphore_wait(reach.at[2], 2)
    send_chunks(fwd_send, fwd_recv, grid_sem.at[1], True)
    send_chunks(cot_send, cot_recv, grid_sem.at[0], True)

    halo_slopes()
    cols_u[...] = jnp.zeros_like(cols_u)
    cols_e[...] = jnp.zeros_like(cols_e)
    for n, slot in enumerate((2, 29)):
        cols_u[n, 0:TR, :] = wide(slope_u, column(slot, TR))

    def to_windows(recv, target):
        mixbuf[0:784, :] = recv[...].astype(F32).reshape(784, 128)
        for w in range(NWIN):
            for k in range(4):
                target[WPAD * w : WPAD * w + LEN, 128 * k : 128 * (k + 1)] = mixbuf[
                    pl.ds(4 * w + k, LEN, stride=16), :
                ]

    def from_windows(source, send):
        for w in range(NWIN):
            for k in range(4):
                mixbuf[pl.ds(4 * w + k, LEN, stride=16), :] = source[
                    WPAD * w : WPAD * w + LEN, 128 * k : 128 * (k + 1)
                ]
        send[...] = mixbuf[0:784, :].reshape(LEN, 16, 128).astype(BF16)

    dgrid[...] = jnp.zeros_like(dgrid)
    zgrid[...] = jnp.zeros_like(zgrid)
    l_gqkv.wait()

    wait_chunks(fwd_recv, grid_sem.at[1])
    to_windows(fwd_recv, zgrid)
    project_in(zgrid[...], ggain_ref, gqkv, packed_g, xhat_g, scale_g)
    attend(packed_g, bias_g, prob_g)
    wait_chunks(cot_recv, grid_sem.at[0])
    to_windows(cot_recv, dgrid)
    dout[...] = dgrid[...].astype(BF16)
    l_gout.wait()
    da[...] = dot_nt(dout[...], gout[...]).astype(BF16)
    attend_back(packed_g, prob_g)
    dgrid[...] = project_back(gqkv, ggain_ref, xhat_g, scale_g).astype(F32)
    from_windows(dgrid, gra_send)
    send_chunks(gra_send, gra_recv, grid_sem.at[3], False)
    zgrid[...] = (zgrid[...] + dot(att[...], gout[...])).astype(BF16).astype(F32)
    from_windows(zgrid, res_send)
    send_chunks(res_send, res_recv, grid_sem.at[2], False)

    wait_chunks(gra_recv, grid_sem.at[3])
    mixbuf[0:784, :] = gra_recv[...].astype(F32).reshape(784, 128)
    mixbuf[784:832, :] = jnp.zeros((48, 128), F32)
    spatial = jnp.concatenate([mixbuf[pl.ds(k, 208, stride=4), :] for k in range(4)], axis=1)
    dout[...] = place("back_win", spatial.astype(BF16)).astype(BF16)
    da[...] = dot_nt(dout[...], bout[...]).astype(BF16)
    attend_back(packed_b, prob_b)
    slotted = place("slots", project_back(bqkv, bgain_ref, xhat_b, scale_b))
    stage[...] = slotted[0:224]
    own2[...] = slotted.astype(BF16)
    w_col2, e_col2 = own2.at[pl.ds(224, 16)], own2.at[pl.ds(240, 16)]
    halo2 = swap(
        halo2_sem,
        [
            (own2.at[pl.ds(0, 32)], cat2.at[pl.ds(32, 32)], (north, j)),
            (own2.at[pl.ds(192, 32)], cat2.at[pl.ds(0, 32)], (south, j)),
            (e_col2, cat2.at[pl.ds(64, 16)], (i, east)),
            (w_col2, cat2.at[pl.ds(80, 16)], (i, west)),
            (e_col2, cat2.at[pl.ds(96, 16)], (south, east)),
            (w_col2, cat2.at[pl.ds(112, 16)], (south, west)),
            (e_col2, cat2.at[pl.ds(128, 16)], (north, east)),
            (w_col2, cat2.at[pl.ds(144, 16)], (north, west)),
        ],
    )

    def back_own():
        gp = dot_nt(own2[0:224, :], wp[...]).astype(BF16).astype(F32)
        gp = gp * wide(slope_p, slice(32, 256))
        y = []
        for b in range(3):
            t = [gp * w[3 * a + 2 - b] for a in range(3)]
            y.append(
                jnp.concatenate(
                    [
                        lines(t[0], 1, 2) + lines(t[1], 0, 1),
                        lines(t[0], 2, 7) + lines(t[1], 1, 6) + lines(t[2], 0, 5),
                        lines(t[1], 6, 7) + lines(t[2], 5, 6),
                    ],
                    axis=0,
                )
            )
        put_wide(grad_e, slice(0, 224), side_by_side(y))

    def back_hidden(rows):
        return wide(grad_e, rows).astype(BF16).astype(F32) * wide(slope_u, rows)

    back_own()
    for n, slot in enumerate((2, 29)):
        cols_e[n, 0:TR, :] = wide(grad_e, column(slot, TR))
    put_wide(update, slice(None), dot_nt(back_hidden(slice(0, 224)).astype(BF16), we[...]))
    wait_chunks(res_recv, grid_sem.at[2])
    out_ref[...] = res_recv[...]

    for one in halo2:
        one.wait_recv()
    gm = place("halo2", cat2[...]) * inside(96, 32, 16)
    halo_grad[...] = gm.astype(BF16)

    gp = dot_nt(halo_grad[...], wp[...]).astype(BF16).astype(F32)
    north_gp = gp[0:32] * wide(slope_p, slice(0, 32))
    south_gp = gp[32:64] * wide(slope_p, slice(256, 288))
    sides = []
    for x, b in ((gp[64:80] * cols_slope[0], 2), (gp[80:96] * cols_slope[3], 0)):
        sides.append(
            pltpu.roll(x * w[b], 14, 0) + pltpu.roll(x * w[3 + b], 15, 0) + x * w[6 + b]
        )

    def hidden(grad, slope):
        return grad.astype(BF16).astype(F32) * slope

    rim = []
    for line, y in (
        (0, [north_gp * w[8 - b] for b in range(3)]),
        (6, [south_gp * w[2 - b] for b in range(3)]),
    ):
        rows = slice(SW * line, SW * (line + 1))
        ends = [(slot, x[line : line + 1]) for slot, x in zip((2, 29), sides)]
        rim.append(
            hidden(wide(grad_e, rows) + beside(side_by_side(y), ends), wide(slope_u, rows))
        )
    for n, x in enumerate(sides):
        rim.append(hidden(cols_e[n] + x, cols_u[n]))
    rim = jnp.concatenate(rim, axis=0).astype(BF16)
    put_rim(update, dot_nt(rim, we[...]), 0)
    dn = wide(update).astype(BF16).astype(F32)
    dx = standardize_back(dn * cgain_ref[...], xhat0[...], scale0[...])
    stage[...] = stage[...] + dx.astype(BF16).astype(F32)
    for r in range(TR):
        grad_ref[r] = stage[SW * r + 2 : SW * r + 2 + TC, :].astype(BF16)

    for one in halo + halo2:
        one.wait_send()
    for n, send in enumerate((cot_send, fwd_send, res_send, gra_send)):
        wait_sent(send, grid_sem.at[n])


def finish(chunks_ref, kept_ref, out_ref, grad_ref, mixbuf):
    mixbuf[...] = chunks_ref[...].astype(F32).reshape(784, 128)
    for r in range(TR):
        for k in range(4):
            out_ref[r, :, 128 * k : 128 * (k + 1)] = mixbuf[
                pl.ds(112 * r + k, TC, stride=4), :
            ].astype(BF16)
    grad_ref[...] = kept_ref[...]


def local(
    inputs, cotangent, conv_gain, expand_weight, depth_weight, project_weight,
    block_gain, block_qkv, block_out, block_bias, grid_gain, grid_qkv, grid_out, grid_bias,
):
    def by_query(bias):
        return bias.transpose(1, 0, 2).reshape(16 * LEN, LEN)

    vmem, hbm = pl.BlockSpec(memory_space=pltpu.VMEM), pl.BlockSpec(memory_space=pl.ANY)
    places = jnp.asarray(PLACES, BF16)
    chunks = pltpu.VMEM((LEN, 16, 128), BF16)
    tokens = jax.ShapeDtypeStruct((TR, TC, D), BF16)
    bias = pltpu.VMEM((16 * LEN, LEN), F32)
    bias_t = pltpu.VMEM((4, WPAD, 256), F32)
    win_f32, win_bf16 = pltpu.VMEM((256, D), F32), pltpu.VMEM((256, D), BF16)
    packed = pltpu.VMEM((256, 3 * D), BF16)
    scale = pltpu.VMEM((256, 1), F32)
    prob = pltpu.VMEM((NWIN, 4, WPAD, 256), F32)
    scratch = [
        pltpu.VMEM(PLACES.shape, BF16), pltpu.VMEM((D, FF), BF16), pltpu.VMEM((FF, D), BF16),
        pltpu.VMEM((D, 3 * D), BF16), pltpu.VMEM((D, D), BF16), bias,
        pltpu.VMEM((D, 3 * D), BF16), pltpu.VMEM((D, D), BF16), bias,
        pltpu.SemaphoreType.DMA((15,)), pltpu.SemaphoreType.REGULAR((3,)),
        pltpu.VMEM((TR, TC, D), BF16), pltpu.VMEM((TR, TC, D), BF16), pltpu.VMEM((1, D), F32),
        pltpu.VMEM((9, FF), F32), pltpu.VMEM((1, D), F32), pltpu.VMEM((1, D), F32),
        pltpu.VMEM((32, D), F32),
        pltpu.VMEM((224, D), F32), pltpu.VMEM((224, D), BF16), pltpu.VMEM((224, D), BF16),
        pltpu.VMEM((32, D), BF16), pltpu.VMEM((256, D), BF16), pltpu.VMEM((160, D), BF16),
        pltpu.SemaphoreType.DMA((2, 8)), pltpu.SemaphoreType.DMA((2, 8)),
        chunks, chunks, chunks, chunks, chunks, chunks, chunks, chunks,
        pltpu.SemaphoreType.DMA((4, 2)),
        pltpu.VMEM((832, 128), F32), pltpu.VMEM((224, D), F32), pltpu.VMEM((224, 1), F32),
        pltpu.VMEM((224, D), BF16), pltpu.VMEM((160, D), BF16),
        pltpu.VMEM((FF // 128, 256, 128), F32), pltpu.VMEM((FF // 128, 288, 128), F32),
        pltpu.VMEM((FF // 128, 288, 128), F32), pltpu.VMEM((D // 128, 224, 128), F32),
        bias_t, bias_t, win_f32, packed, win_f32, scale, prob, win_bf16,
        win_f32, win_f32, packed, win_f32, scale, prob, win_bf16, win_bf16, packed,
        pltpu.VMEM((NWIN, 4, WPAD, 256), BF16), pltpu.VMEM((96, D), BF16),
        pltpu.VMEM((FF // 128, 256, 128), F32),
        pltpu.VMEM((4, 16, FF), F32), pltpu.VMEM((4, 16, FF), F32),
        pltpu.VMEM((2, 16, FF), F32), pltpu.VMEM((2, 16, FF), F32), pltpu.VMEM((160, FF), F32),
    ]
    result, grad = pl.pallas_call(
        kernel,
        out_shape=(jax.ShapeDtypeStruct((LEN, 16, 128), BF16), tokens),
        in_specs=[hbm] * 15,
        out_specs=(vmem, vmem),
        scratch_shapes=scratch,
        compiler_params=pltpu.CompilerParams(
            collective_id=0, has_side_effects=True, vmem_limit_bytes=56 * 2**20
        ),
        name="mbconv_attention",
    )(
        inputs, cotangent, conv_gain.reshape(1, D), depth_weight, block_gain.reshape(1, D),
        grid_gain.reshape(1, D), places, expand_weight, project_weight, block_qkv, block_out,
        by_query(block_bias), grid_qkv, grid_out, by_query(grid_bias),
    )
    return pl.pallas_call(
        finish,
        out_shape=(tokens, tokens),
        in_specs=[vmem] * 2,
        out_specs=(vmem, vmem),
        scratch_shapes=[pltpu.VMEM((784, 128), F32)],
        name="finish",
    )(result, grad)


def solution(mesh):
    tokens = P("rows", "cols", None)
    in_specs = (tokens, tokens) + (P(),) * 12
    return jax.shard_map(
        local, mesh=mesh, in_specs=in_specs, out_specs=(tokens, tokens), check_vma=False
    )
```
